128 devices in a mesh: grp: 8 (over x, core), soil: 16 (over z, y).
Axes of the slice: x: 4, y: 4, z: 4, core: 2. Of those that a mesh axis runs over, the one named last changes fastest.
Arguments:
- warm_start: float32 [3, 131072], P(None, ('grp', 'soil')), may hold values from -5 to 5
- right_side: float32 [3, 131072], P(None, ('grp', 'soil')), may hold values from -16 to 16
- friction: float32 [131072], P(('grp', 'soil')), may hold values from 0.3 to 1
- inverse_mass: float32 [6, 131072], P(None, ('grp', 'soil')), may hold values from 0.5 to 2
- jacobian: bfloat16 [8192, 192, 384], P(('grp', 'soil')), may hold values from -0.15625 to 0.15625
- compliance: bfloat16 [6144, 6144], P(None, 'soil'), may hold values from -0.5 to 2.5, as said below
- entry_block: int32 [8192], P(('grp', 'soil')), may hold values from 0 to 15
- entry_owner: int32 [8192], P(('grp', 'soil')), may hold values from 0 to 15, as said below
- entry_body: int32 [8192], P(('grp', 'soil')), may hold values from 0 to 15
- block_count: int32 [128], P(('grp', 'soil')), may hold values from 16 to 64, as said below
Outputs:
- impulses: float32 [3, 131072], P(None, ('grp', 'soil'))
- velocity_change: float32 [6, 131072], P(None, ('grp', 'soil'))
- change_norm: float32 [], replicated
The draws below stay inside these ranges and needn't reach their ends.
Inputs may be any that keep to these rules, and one draw needn't show every extreme that they name: `entry_owner`: among the first block_count entries of a device at most 4 name one owner, and one owner of every group receives 4 entries from each of the 16 devices of that group; later entries are padding. `block_count`: one device of every group holds 64 live entries; the others hold 16 to 32. `compliance`: Symmetric.
All inputs are finite; a program needn't handle non-finite values.
Results may differ from the reference program's by a relative error of at most 0.0032.
Values may be sent and summed in bfloat16 or wider, within the bound.
No kernel may reach another device: no remote copies, remote signals or barrier semaphores. Data moves between devices by JAX's collectives and lax.ppermute only.
A program may use at most 64 MiB of HBM per device.

```python
import math
import jax
import jax.numpy as jnp
from jax import lax

BLK = 64
CB = 16
NB = 16
TC = 128
CAP = 4
ITERS = 3
NCONT = 131072
NBODY = 131072
ENTRIES = 8192
N_GRP = 8
N_SOIL = 16


def region_loads(key):
    patch_key = jax.random.fold_in(key, 101)
    count_key = jax.random.fold_in(key, 102)
    entry_total = CAP * N_SOIL
    devices = N_GRP * N_SOIL
    patches = jax.random.randint(patch_key, (N_GRP,), 0, N_SOIL)
    device_ids = jnp.arange(devices, dtype=jnp.int32)
    patch_of = patches[device_ids // N_SOIL]
    is_patch = device_ids % N_SOIL == patch_of
    quiet_counts = jax.random.randint(count_key, (devices,), entry_total // 4, entry_total // 2 + 1)
    counts = jnp.where(is_patch, entry_total, quiet_counts).astype(jnp.int32)
    return (patch_of, counts)


def draw_block_count(key, part):
    patch_of, counts = region_loads(key)
    return counts


def draw_entry_owner(key, part):
    patch_of, counts = region_loads(key)
    key = jax.random.fold_in(key, 7)
    entry_total = CAP * N_SOIL
    devices = N_GRP * N_SOIL
    device_keys = jax.random.split(key, devices)

    def one_device(device_key, patch_index, live_count):
        order_key, score_key = jax.random.split(device_key)
        others = jnp.arange((N_SOIL - 1) * CAP, dtype=jnp.int32) // CAP
        others = others + (others >= patch_index).astype(jnp.int32)
        others = jax.random.permutation(order_key, others)
        listing = jnp.concatenate([jnp.full((CAP,), patch_index, jnp.int32), others])
        position = jnp.arange(entry_total, dtype=jnp.int32)
        scores = jax.random.randint(score_key, (entry_total,), 0, 1 << 20) * entry_total + position
        scores = jnp.where(position < live_count, scores, (1 << 30) + position)
        ordering = jnp.argsort(scores, stable=True)
        return listing[ordering]
    owners = jax.vmap(one_device)(device_keys, patch_of, counts)
    return owners.reshape(-1).astype(jnp.int32)


def draw_right_side(key, part):
    key = jax.random.fold_in(key, 11)
    devices = N_GRP * N_SOIL
    total_columns = CB * BLK * devices
    column = jnp.arange(total_columns, dtype=jnp.int32)
    rising = 1.0 + 2.0 * (column // (CB * BLK)).astype(jnp.float32) / (devices - 1)
    values = jnp.clip(jax.random.normal(key, (3, total_columns), jnp.float32), -5.0, 5.0)
    return values * rising[None, :]


def draw_compliance(key, part):
    key = jax.random.fold_in(key, 13)
    matrix_order = 3 * TC * N_SOIL
    noise_key, diagonal_key = jax.random.split(key)
    noise_draw = jnp.clip(jax.random.normal(noise_key, (matrix_order, matrix_order), jnp.float32), -5.0, 5.0)
    symmetric = (noise_draw + noise_draw.T) * (0.3 / math.sqrt(2.0 * matrix_order))
    diagonal = jax.random.uniform(diagonal_key, (matrix_order,), jnp.float32, 1.0, 2.0)
    on_diagonal = jnp.arange(matrix_order)[:, None] == jnp.arange(matrix_order)[None, :]
    return jnp.where(on_diagonal, diagonal[:, None] + symmetric, symmetric).astype(jnp.bfloat16)


def set_ends(values, stream_key, low, largest):
    place = [jax.random.randint(jax.random.fold_in(stream_key, axis), (), 0, length) for axis, length in enumerate(values.shape)]
    main_axis = values.shape.index(max(values.shape))
    beside = place[:main_axis] + [(place[main_axis] + 1) % values.shape[main_axis]] + place[main_axis + 1:]
    return values.at[tuple(place)].set(low).at[tuple(beside)].set(largest)


def block_levels(rng, extent, cuts, least, top_value):
    loudness = 1.0
    for dim, blocks in cuts:
        steps = jax.random.uniform(jax.random.fold_in(jax.random.fold_in(rng, 6), dim), (blocks,), jnp.float32, least / len(cuts), top_value / len(cuts))
        loudness = loudness * jnp.repeat(jnp.exp(steps), extent[dim] // blocks).reshape((-1,) + (1,) * (len(extent) - 1 - dim))
    return loudness


def centred(stream_key, shape, width, bound, cuts=(), kind=jnp.bfloat16):
    array = width * jax.random.normal(stream_key, shape, jnp.float32)
    if cuts:
        array = array * block_levels(stream_key, shape, cuts, -0.22, 0.18)
    return jnp.clip(array, -bound, bound).astype(kind)


def setup_inputs(seed: int = 0) -> dict:
    seeds = jax.random.split(jax.random.key(seed), 11)
    return {
        "warm_start": centred(seeds[0], (3, NCONT), 1.0, 5.0, ((1, 128),), jnp.float32),
        "right_side": draw_right_side(jax.random.fold_in(seeds[10], 71), 0),
        "friction": jnp.clip(jnp.exp(math.log(1.0) - 1.2039728 * jax.random.uniform(seeds[2], (NCONT,), jnp.float32) ** block_levels(seeds[2], (NCONT,), ((0, 128),), -0.2, 0.2)), 0.3, 1.0),
        "inverse_mass": jnp.clip(jnp.exp(math.log(2.0) - 1.3862944 * jax.random.uniform(seeds[3], (6, NBODY), jnp.float32) ** block_levels(seeds[3], (6, NBODY), ((1, 128),), -0.2, 0.2)), 0.5, 2.0),
        "jacobian": centred(seeds[4], (ENTRIES, 3 * BLK, 6 * BLK), (24 * BLK) ** -0.5, 0.15625, ((0, 128),)),
        "compliance": draw_compliance(jax.random.fold_in(seeds[10], 71), 0),
        "entry_block": set_ends(jax.random.randint(seeds[6], (ENTRIES,), 0, CB), jax.random.fold_in(seeds[6], 1), 0, CB - 1).astype(jnp.int32),
        "entry_owner": draw_entry_owner(jax.random.fold_in(seeds[10], 71), 0),
        "entry_body": set_ends(jax.random.randint(seeds[8], (ENTRIES,), 0, NB), jax.random.fold_in(seeds[8], 1), 0, NB - 1).astype(jnp.int32),
        "block_count": draw_block_count(jax.random.fold_in(seeds[10], 71), 0),
    }


step_size = 0.1
hold_eps = 1e-06

def momentum_weights(number):
    nesterov = 1.0
    weights = []
    for iteration in range(number):
        following = 0.5 * (-nesterov * nesterov + nesterov * math.sqrt(nesterov * nesterov + 4.0))
        weights.append(nesterov * (1.0 - nesterov) / (nesterov * nesterov + following))
        nesterov = following
    return weights

def to_blocks(layout, blocks, pieces):
    block_width = layout.shape[1] // blocks
    return layout.reshape(pieces, blocks, block_width).transpose(1, 0, 2).reshape(blocks, pieces * block_width)

def from_blocks(tile_rows, pieces):
    blocks = tile_rows.shape[0]
    block_width = tile_rows.shape[1] // pieces
    return tile_rows.reshape(blocks, pieces, block_width).transpose(1, 0, 2).reshape(pieces, blocks * block_width)

def project_cone(values, friction):
    normal = values[0]
    tangent_one = values[1]
    tangent_two = values[2]
    tangent_size = jnp.sqrt(tangent_one * tangent_one + tangent_two * tangent_two)
    inside = tangent_size <= friction * normal
    polar_side = friction * tangent_size <= -normal
    middle = jnp.logical_not(jnp.logical_or(inside, polar_side))
    safe_size = jnp.where(middle, tangent_size, 1.0)
    new_normal = (friction * tangent_size + normal) / (1.0 + friction * friction)
    shrink = friction * new_normal / safe_size
    out_normal = jnp.where(inside, normal, jnp.where(polar_side, 0.0, new_normal))
    factor = jnp.where(inside, 1.0, jnp.where(polar_side, 0.0, shrink))
    return jnp.stack([out_normal, tangent_one * factor, tangent_two * factor])

def reference(warm_start, right_side, friction, inverse_mass, jacobian, compliance, entry_block, entry_owner, entry_body, block_count):
    devices = N_GRP * N_SOIL
    entry_total = CAP * N_SOIL
    contact_dev = CB * BLK
    jacobian_sets = jacobian.reshape(devices, entry_total, 3 * BLK, 6 * BLK)
    block_ids = entry_block.reshape(devices, entry_total)
    device_ids = jnp.arange(devices, dtype=jnp.int32)
    living = (jnp.arange(entry_total, dtype=jnp.int32)[None, :] < block_count[:, None]).astype(jnp.float32)
    owners = entry_owner.reshape(devices, entry_total)
    global_body = (((device_ids // N_SOIL)[:, None] * N_SOIL + owners) * NB + entry_body.reshape(devices, entry_total)).astype(jnp.int32)
    mass_tiles = to_blocks(inverse_mass, NB * devices, 6)

    def push(impulse_bf):
        tile_sets = to_blocks(impulse_bf, CB * devices, 3).reshape(devices, CB, 3 * BLK)

        def one_device(inputs):
            tile_set, picks, live_mask, jacobian_dev = inputs
            picked = tile_set[picks].astype(jnp.float32) * live_mask[:, None]
            return jnp.einsum('er,erk->ek', picked, jacobian_dev.astype(jnp.float32))
        forces = lax.map(one_device, (tile_sets, block_ids, living, jacobian_sets))
        totals = jax.ops.segment_sum(forces.reshape(-1, 6 * BLK), global_body.reshape(-1), num_segments=NB * devices)
        return totals * mass_tiles

    def pull(velocity_bf):

        def one_device(inputs):
            body_ids, live_mask, jacobian_dev, picks = inputs
            wanted = velocity_bf[body_ids].astype(jnp.float32) * live_mask[:, None]
            contact_terms = jnp.einsum('ek,erk->er', wanted, jacobian_dev.astype(jnp.float32))
            return jax.ops.segment_sum(contact_terms, picks, num_segments=CB)
        gathered = lax.map(one_device, (global_body, living, jacobian_sets, block_ids))
        return from_blocks(gathered.reshape(devices * CB, 3 * BLK), 3)

    def tire_part(impulse_bf):
        tire_values = impulse_bf.reshape(3, devices, contact_dev)[:, :, :TC]
        stacked = tire_values.transpose(1, 0, 2).reshape(N_GRP, N_SOIL * 3 * TC)
        result = jnp.dot(compliance, stacked.T, preferred_element_type=jnp.float32)
        return result.T.reshape(devices, 3, TC).transpose(1, 0, 2)
    weights = momentum_weights(ITERS)
    current = warm_start
    advance = warm_start
    previous = warm_start
    for iteration in range(ITERS):
        advance_bf = advance.astype(jnp.bfloat16)
        velocity_bf = push(advance_bf).astype(jnp.bfloat16)
        operator_part = pull(velocity_bf).reshape(3, devices, contact_dev)
        operator_part = operator_part.at[:, :, :TC].add(tire_part(advance_bf))
        gradient = operator_part.reshape(3, devices * contact_dev) + right_side
        updated = project_cone(advance - step_size * gradient, friction)
        previous = current
        advance = updated + weights[iteration] * (updated - current)
        current = updated
    change = current - previous
    change_norm = jnp.sqrt(jnp.mean(change * change) + hold_eps) / step_size
    velocity_change = from_blocks(push(current.astype(jnp.bfloat16)), 6)
    return (current, velocity_change, change_norm)
```

```python
import math

import jax
import jax.numpy as jnp
from jax import lax
from jax.sharding import PartitionSpec as P

BLK = 64
CB = 16
NB = 16
TC = 128
CAP = 4
ITERS = 3
SHARED = 32


step_size = 0.1
hold_eps = 1e-06


def momentum_weights(number):
    nesterov = 1.0
    weights = []
    for iteration in range(number):
        following = 0.5 * (-nesterov * nesterov + nesterov * math.sqrt(nesterov * nesterov + 4.0))
        weights.append(nesterov * (1.0 - nesterov) / (nesterov * nesterov + following))
        nesterov = following
    return weights


def to_blocks(layout, blocks, pieces):
    block_width = layout.shape[1] // blocks
    return (
        layout.reshape(pieces, blocks, block_width)
        .transpose(1, 0, 2)
        .reshape(blocks, pieces * block_width)
    )


def from_blocks(tile_rows, pieces):
    blocks = tile_rows.shape[0]
    block_width = tile_rows.shape[1] // pieces
    return (
        tile_rows.reshape(blocks, pieces, block_width)
        .transpose(1, 0, 2)
        .reshape(pieces, blocks * block_width)
    )


def project_cone(values, friction):
    normal = values[0]
    tangent_one = values[1]
    tangent_two = values[2]
    tangent_size = jnp.sqrt(tangent_one * tangent_one + tangent_two * tangent_two)
    inside = tangent_size <= friction * normal
    polar_side = friction * tangent_size <= -normal
    middle = jnp.logical_not(jnp.logical_or(inside, polar_side))
    safe_size = jnp.where(middle, tangent_size, 1.0)
    new_normal = (friction * tangent_size + normal) / (1.0 + friction * friction)
    shrink = friction * new_normal / safe_size
    out_normal = jnp.where(inside, normal, jnp.where(polar_side, 0.0, new_normal))
    factor = jnp.where(inside, 1.0, jnp.where(polar_side, 0.0, shrink))
    return jnp.stack([out_normal, tangent_one * factor, tangent_two * factor])


def split_terms(values, terms):
    parts = []
    for _ in range(terms):
        part = values.astype(jnp.bfloat16)
        parts.append(part)
        values = values - part.astype(jnp.float32)
    return parts


def pick_rows(pick_bf, values, terms):
    return jnp.dot(
        jnp.concatenate([pick_bf] * terms, axis=1),
        jnp.concatenate(split_terms(values, terms), axis=0),
        preferred_element_type=jnp.float32,
    )


def on_device(
    warm_start,
    right_side,
    friction,
    inverse_mass,
    jacobian,
    compliance,
    entry_block,
    entry_owner,
    entry_body,
    block_count,
):
    bf16, f32 = jnp.bfloat16, jnp.float32
    groups = lax.axis_size("soil")
    me = lax.axis_index("soil")
    entries = jacobian.shape[0]
    bodies = groups * NB
    width = 6 * BLK
    mass_tiles = to_blocks(inverse_mass, NB, 6)
    live = jnp.arange(entries, dtype=jnp.int32) < block_count[0]
    pick_bf = (
        (entry_block[:, None] == jnp.arange(CB, dtype=jnp.int32)[None, :]) & live[:, None]
    ).astype(bf16)
    ids = jnp.where(live, entry_owner * NB + entry_body, -1)
    hits = ids[:, None] == jnp.arange(bodies, dtype=jnp.int32)[None, :]
    hits_bf = hits.astype(bf16)
    named = jnp.any(hits, axis=0).astype(bf16)
    everyone = lax.all_to_all(
        jnp.broadcast_to(named[None, None, :], (groups, 1, bodies)), "soil", 0, 0, tiled=True
    ).reshape(groups, bodies)

    def ranks(marks):
        size = marks.shape[1]
        before = jnp.triu(jnp.ones((size, size), bf16), 1)
        rank = jnp.dot(marks, before, preferred_element_type=f32)
        return jnp.where(marks > 0, rank + 1.0, 0.0)

    others = (jnp.arange(groups) != me)[:, None]
    common = jnp.where(others, everyone * named[None, :], 0).astype(bf16)
    shared_rank = jnp.dot(
        ranks(common).astype(bf16), hits_bf.T, preferred_element_type=f32
    )
    share_pick = (
        shared_rank[:, None, :] == jnp.arange(1, SHARED + 1, dtype=f32)[None, :, None]
    ).astype(bf16)
    share_pick = share_pick.reshape(groups * SHARED, entries)
    own_pick = (ids[:, None] == ids[None, :]) & live[:, None]
    own_pick = own_pick.astype(bf16)
    owner_rank = ranks(named.reshape(groups, NB)).reshape(1, bodies)
    owner_rank = jnp.dot(owner_rank.astype(bf16), hits_bf.T, preferred_element_type=f32)
    owner_slot = jnp.where(live, entry_owner * CAP, -1).astype(f32) + owner_rank[0]
    owner_pick = (
        owner_slot[None, :] == jnp.arange(1, groups * CAP + 1, dtype=f32)[:, None]
    ).astype(bf16)
    asked = lax.dynamic_slice_in_dim(everyone, me * NB, NB, axis=1)
    asked_pick = (
        ranks(asked)[:, None, :] == jnp.arange(1, CAP + 1, dtype=f32)[None, :, None]
    ).astype(bf16)
    asked_pick = asked_pick.reshape(groups * CAP, NB)

    def forces_of(impulse_bf):
        tile_rows = to_blocks(impulse_bf, CB, 3)
        picked = jnp.dot(pick_bf, tile_rows, preferred_element_type=f32).astype(bf16)
        return jnp.einsum("er,erk->ek", picked, jacobian, preferred_element_type=f32)

    weights = momentum_weights(ITERS)
    current = warm_start
    advance = warm_start
    previous = warm_start
    mass_rows = None
    for iteration in range(ITERS):
        advance_bf = advance.astype(bf16)
        forces = forces_of(advance_bf)
        shares = pick_rows(share_pick, forces, 2).astype(bf16).reshape(groups, SHARED, width)
        tire_row = jnp.broadcast_to(
            advance_bf[:, :TC].reshape(1, 1, 3 * TC), (groups, 1, 3 * TC)
        )
        pieces = [shares, tire_row]
        if iteration == 0:
            mass_hi, mass_lo = split_terms(mass_tiles, 2)
            for part in (mass_hi, mass_lo):
                rows = jnp.dot(asked_pick, part, preferred_element_type=f32).astype(bf16)
                pieces.append(rows.reshape(groups, CAP, width))
        arrived = lax.all_to_all(jnp.concatenate(pieces, axis=1), "soil", 0, 0, tiled=True)
        if iteration == 0:
            mass_parts = jnp.concatenate(
                [arrived[:, SHARED + 1 : SHARED + 1 + CAP], arrived[:, SHARED + 1 + CAP :]],
                axis=0,
            ).reshape(2 * groups * CAP, width)
            mass_rows = jnp.dot(
                jnp.concatenate([owner_pick, owner_pick], axis=0).T,
                mass_parts,
                preferred_element_type=f32,
            )
        sums = jnp.dot(
            share_pick.T,
            arrived[:, :SHARED].reshape(groups * SHARED, width),
            preferred_element_type=f32,
        )
        sums = sums + pick_rows(own_pick, forces, 2)
        wanted = (sums * mass_rows).astype(bf16)
        contact_terms = jnp.einsum("ek,erk->er", wanted, jacobian, preferred_element_type=f32)
        gathered = pick_rows(pick_bf.T, contact_terms, 3)
        operator_part = from_blocks(gathered, 3)
        all_tire = arrived[:, SHARED].reshape(-1)
        tire_term = jnp.dot(all_tire, compliance, preferred_element_type=f32)
        gradient = operator_part.at[:, :TC].add(tire_term.reshape(3, TC)) + right_side
        updated = project_cone(advance - step_size * gradient, friction)
        previous = current
        advance = updated + weights[iteration] * (updated - current)
        current = updated
    change = current - previous
    regions = lax.axis_size("grp")
    squares = jnp.sum(change * change)
    across = lax.all_to_all(
        jnp.broadcast_to(squares, (regions, 1, 128)), "grp", 0, 0, tiled=True
    )
    squares = jnp.sum(across[:, 0, 0])
    forces = forces_of(current.astype(bf16))
    outgoing = pick_rows(owner_pick, forces, 3).reshape(groups, CAP, width)
    square_row = jnp.broadcast_to(squares, (groups, 1, width))
    arrived = lax.all_to_all(
        jnp.concatenate([outgoing, square_row], axis=1), "soil", 0, 0, tiled=True
    )
    totals = pick_rows(asked_pick.T, arrived[:, :CAP].reshape(groups * CAP, width), 3)
    velocity_change = from_blocks(totals * mass_tiles, 6)
    squared_total = jnp.sum(arrived[:, CAP, 0])
    element_total = 3 * current.shape[1] * lax.axis_size(("grp", "soil"))
    change_norm = jnp.sqrt(squared_total / element_total + hold_eps) / step_size
    return (current, velocity_change, change_norm)


def solution(mesh):
    placed = (
        P(None, ("grp", "soil")),
        P(None, ("grp", "soil")),
        P(("grp", "soil")),
        P(None, ("grp", "soil")),
        P(("grp", "soil"), None, None),
        P(None, "soil"),
        P(("grp", "soil")),
        P(("grp", "soil")),
        P(("grp", "soil")),
        P(("grp", "soil")),
    )
    return jax.shard_map(
        on_device,
        mesh=mesh,
        in_specs=placed,
        out_specs=(P(None, ("grp", "soil")), P(None, ("grp", "soil")), P()),
        check_vma=False,
    )
```

```python
import functools
import math

import jax
import jax.numpy as jnp
from jax import lax
from jax.experimental import pallas as pl
from jax.experimental.pallas import tpu as pltpu
from jax.sharding import PartitionSpec as P

BLK = 64
CB = 16
NB = 16
TC = 128
CAP = 4
ITERS = 3
ENT = 64
SOIL = 16
BODIES = SOIL * NB
WIDE = 6 * BLK
TALL = 3 * BLK
SEND_FIRST = 104
SEND = 72

step_size = 0.1
hold_eps = 1e-06

bf16, f32, i32 = jnp.bfloat16, jnp.float32, jnp.int32

IN_HBM = pl.BlockSpec(memory_space=pltpu.HBM)
VECTOR = pl.BlockSpec(memory_space=pltpu.VMEM)
SCALAR = pl.BlockSpec(memory_space=pltpu.SMEM)


def momentum_weights(number):
    nesterov = 1.0
    weights = []
    for iteration in range(number):
        following = 0.5 * (-nesterov * nesterov + nesterov * math.sqrt(nesterov * nesterov + 4.0))
        weights.append(nesterov * (1.0 - nesterov) / (nesterov * nesterov + following))
        nesterov = following
    return weights


def resident(shape, dtype):
    return pltpu.VMEM(shape, dtype)


def keep(array):
    return pltpu.with_memory_space_constraint(array, pltpu.VMEM)


def far(array):
    return pltpu.with_memory_space_constraint(array, pltpu.HBM)


def shape_of(shape, dtype):
    return jax.ShapeDtypeStruct(shape, dtype)


def params(megabytes):
    return pltpu.CompilerParams(vmem_limit_bytes=megabytes << 20)


def iota(shape, dim):
    return lax.broadcasted_iota(i32, shape, dim)


def ones_where(mask):
    return jnp.where(mask, 1.0, 0.0).astype(bf16)


def dot(left, right):
    return jnp.dot(left, right, preferred_element_type=f32)


def dot_rows(left, right):
    return lax.dot_general(left, right, (((1,), (1,)), ((), ())), preferred_element_type=f32)


def split_terms(values, terms):
    parts = []
    for _ in range(terms):
        part = values.astype(bf16)
        parts.append(part)
        values = values - part.astype(f32)
    return jnp.concatenate(parts, axis=0)


def order(block):
    return ((block & 1) << 3) + (block >> 1)


def lanes_low(shape):
    return iota(shape, len(shape) - 1) < BLK


def both(values, upper):
    low = lanes_low(values.shape)
    turned = pltpu.roll(values, BLK, 1)
    return jnp.where(low, turned, values) if upper else jnp.where(low, values, turned)


def lane_tiles(ref, row):
    return jnp.concatenate([ref[row : row + 1, 128 * t : 128 * t + 128] for t in range(8)], axis=0)


def doubled(ref, row):
    tiles = lane_tiles(ref, row)
    return jnp.concatenate([both(tiles, False), both(tiles, True)], axis=0)


def twice(normal, first, second):
    low = lanes_low((CB, 2 * BLK))
    return jnp.concatenate(
        [
            jnp.where(low, normal, first),
            jnp.where(low, second, normal),
            jnp.where(low, first, second),
        ],
        axis=1,
    ).astype(bf16)


def push(picked, tiles, wait=None):
    column = iota((16, 16 * TALL), 1)
    first = iota((16, 16 * TALL), 0) * TALL
    mask = ones_where((column >= first) & (column < first + TALL))
    parts = []
    for group in range(ENT // 16):
        if wait is not None:
            wait(group)
        rows = picked[16 * group : 16 * group + 16]
        spread = jnp.concatenate([rows] * 8, axis=1) * mask
        weights = tiles[16 * group : 16 * group + 16].reshape(16 * TALL, WIDE)
        parts.append(dot(spread, weights))
    return jnp.concatenate(parts, axis=0)


def pull(wanted, block, tiles):
    sublane = iota((CB, WIDE), 0)
    total = jnp.zeros((TALL, CB), f32)
    for pair in range(ENT // 2):
        sides = []
        for entry in (2 * pair, 2 * pair + 1):
            sides.append(
                jnp.where(
                    sublane == order(block[entry]), wanted[entry : entry + 1], 0.0
                ).astype(bf16)
            )
        total += dot_rows(
            jnp.concatenate([tiles[2 * pair], tiles[2 * pair + 1]], axis=1),
            jnp.concatenate(sides, axis=1),
        )
    return total


def tire_row(normal, first, second):
    low = lanes_low((1, 128))
    return jnp.concatenate(
        [jnp.where(low, part[0:1], part[8:9]) for part in (normal, first, second)], axis=1
    )


def eye(size):
    return ones_where(iota((size, size), 0) == iota((size, size), 1))


def first_kernel(
    count,
    owner_far,
    body_far,
    block_far,
    warm_far,
    right_far,
    rough_far,
    mass_far,
    tiles_far,
    payload,
    tiles,
    pick_out,
    id_out,
    owner_pick,
    labels,
    warm_out,
    right_out,
    rough_out,
    mass_out,
    owner,
    body,
    block,
    warm,
    right,
    rough,
    mass,
    sems,
    tile_sems,
):
    small = [
        pltpu.make_async_copy(source, target, sems.at[n])
        for n, (source, target) in enumerate(
            [
                (block_far, block),
                (warm_far, warm),
                (owner_far, owner),
                (body_far, body),
                (mass_far, mass),
                (right_far, right),
                (rough_far, rough),
            ]
        )
    ]
    copies = [
        pltpu.make_async_copy(
            tiles_far.at[pl.ds(16 * g, 16)], tiles.at[pl.ds(16 * g, 16)], tile_sems.at[g]
        )
        for g in range(ENT // 16)
    ]
    for copy in small + copies:
        copy.start()
    for copy in small:
        copy.wait()
    live = iota((1, ENT), 1) < count[0]
    pick_t = ones_where((iota((CB, ENT), 0) == order(block[...])) & live)
    pick = dot_rows(eye(ENT), pick_t).astype(bf16)
    pick_out[...] = pick
    advance = [doubled(warm, piece) for piece in range(3)]
    for piece in range(3):
        warm_out[piece] = advance[piece]
        right_out[piece] = doubled(right, piece)
    rough_out[...] = doubled(rough, 0)
    low = lanes_low((8, 128))
    lanes = []
    for piece in range(3):
        even, odd = lane_tiles(mass, 2 * piece), lane_tiles(mass, 2 * piece + 1)
        lanes.append(
            jnp.concatenate(
                [
                    jnp.where(low, even, pltpu.roll(odd, BLK, 1)),
                    jnp.where(low, pltpu.roll(even, BLK, 1), odd),
                ],
                axis=0,
            )
        )
    mass_tiles = jnp.concatenate(lanes, axis=1)
    mass_out[...] = mass_tiles
    mass_high = mass_tiles.astype(bf16)
    mass_low = (mass_tiles - mass_high.astype(f32)).astype(bf16)

    ids = jnp.where(live, owner[...] * NB + order(body[...]) + 1, 0).astype(f32)
    id_rows = jnp.broadcast_to(ids, (8, ENT))
    id_column = dot_rows(eye(ENT), id_rows.astype(bf16))[:, 0:1]
    id_out[...] = jnp.broadcast_to(id_column, (ENT, 128))
    id_lanes = jnp.concatenate([ids, ids, jnp.zeros((1, WIDE - 2 * ENT), f32)], axis=1)

    owner_row = jnp.where(live, owner[...], -1)
    owner_hit = ones_where(iota((SOIL, ENT), 0) == owner_row)
    earlier = ones_where(iota((ENT, ENT), 0) < iota((ENT, ENT), 1))
    rank = jnp.sum(dot(owner_hit, earlier) * owner_hit.astype(f32), axis=0, keepdims=True)
    slot = jnp.where(live, (owner_row * 8).astype(f32) + rank, -1.0)
    chosen = ones_where(iota((128, ENT), 0).astype(f32) == slot)
    owner_pick[...] = jnp.concatenate([chosen, chosen, chosen], axis=1)
    label = jnp.where(live, order(body[...]) + 1, 0).astype(bf16)
    labels[...] = dot_rows(chosen, jnp.broadcast_to(label, (128, ENT)))

    tail_row = iota((8, WIDE), 0)
    tail = jnp.where(
        tail_row == 0, tire_row(*advance), jnp.where(tail_row == 1, id_lanes, 0.0)
    ).astype(bf16)
    for peer in range(SOIL):
        payload[peer, 64:80] = mass_high
        payload[peer, 80:96] = mass_low
        payload[peer, 96:104] = tail
    picked = dot(pick, twice(*advance)).astype(bf16)
    forces = push(picked, tiles, lambda g: copies[g].wait()).astype(bf16)
    for peer in range(SOIL):
        payload[peer, 0:64] = forces


def project_cone(normal, tangent_one, tangent_two, friction):
    tangent_size = jnp.sqrt(tangent_one * tangent_one + tangent_two * tangent_two)
    inside = tangent_size <= friction * normal
    polar_side = friction * tangent_size <= -normal
    middle = jnp.logical_not(jnp.logical_or(inside, polar_side))
    safe_size = jnp.where(middle, tangent_size, 1.0)
    new_normal = (friction * tangent_size + normal) / (1.0 + friction * friction)
    shrink = friction * new_normal / safe_size
    out_normal = jnp.where(inside, normal, jnp.where(polar_side, 0.0, new_normal))
    factor = jnp.where(inside, 1.0, jnp.where(polar_side, 0.0, shrink))
    return out_normal, tangent_one * factor, tangent_two * factor


def step_kernel(
    weight,
    is_first,
    is_last,
    block,
    arrived,
    pick,
    tiles,
    current,
    advance,
    right_side,
    friction,
    *rest,
):
    if is_first:
        id_column, matrix_far = rest[0:2]
        payload, new_current, new_advance, match_out, mass_out, matrix = rest[2:8]
        spread, sem = rest[8:]
        copy = pltpu.make_async_copy(matrix_far, matrix, sem)
        copy.start()
        tail = arrived[:, 96:104, :].astype(f32).reshape(8 * SOIL, WIDE).astype(bf16)
        tail_lane = iota((2 * SOIL, 8 * SOIL), 1)
        tail_row = iota((2 * SOIL, 8 * SOIL), 0)
        tails = dot(
            ones_where(tail_lane == (tail_row & (SOIL - 1)) * 8 + (tail_row >> 4)), tail
        )
        tire_all = tails[0:SOIL]
        names = tails[SOIL:, 0:128]
        mine = id_column[:, 0:1]
        mine = jnp.where(mine > 0, mine, -1.0)
        low = lanes_low((1, 128))
        match = jnp.concatenate(
            [
                ones_where(
                    mine == jnp.where(low, names[2 * t : 2 * t + 1], names[2 * t + 1 : 2 * t + 2])
                )
                for t in range(SOIL // 2)
            ],
            axis=1,
        )
        match_out[...] = match
        lane = iota((ENT, 32 * SOIL), 1)
        named = (((lane >> 5) << 4) + (lane & 15) + 1).astype(f32)
        mass_rows = dot(
            ones_where(mine == named), arrived[:, 64:96, :].reshape(32 * SOIL, WIDE)
        )
        mass_out[...] = mass_rows
    else:
        match_in, mass_in, matrix = rest[0:3]
        outputs, spread = rest[3:-1], rest[-1]
        tail = arrived[:, 64:72, :].astype(f32).reshape(8 * SOIL, WIDE).astype(bf16)
        tail_lane = iota((SOIL, 8 * SOIL), 1)
        tail_row = iota((SOIL, 8 * SOIL), 0)
        tire_all = dot(ones_where(tail_lane == tail_row * 8), tail)
        match = match_in[...]
        mass_rows = mass_in[...]
        copy = None
    sums = dot(match, arrived[:, 0:64, :].reshape(ENT * SOIL, WIDE))
    wanted = (sums * mass_rows).astype(bf16).astype(f32)
    pulled = pull(wanted, block, tiles).T

    device = iota((SOIL, WIDE), 0)
    for peer in range(SOIL):
        spread[:, WIDE * peer : WIDE * peer + WIDE] = jnp.where(
            device == peer, tire_all, 0.0
        ).astype(bf16)
    if copy is not None:
        copy.wait()
    tire = jnp.sum(dot(spread[...], matrix[...]), axis=0, keepdims=True)

    row = iota((CB, 128), 0)
    last = jnp.concatenate([pulled[:, 128:192], pulled[:, 128:192]], axis=1)
    pieces = (both(pulled[:, 0:128], False), both(pulled[:, 0:128], True), last)
    moved = []
    for piece in range(3):
        line = jnp.broadcast_to(tire[:, 128 * piece : 128 * piece + 128], (CB, 128))
        added = jnp.where(
            row == 0, both(line, False), jnp.where(row == 8, both(line, True), 0.0)
        )
        gradient = pieces[piece] + added + right_side[piece]
        moved.append(advance[piece] - step_size * gradient)
    updated = project_cone(*moved, friction[...])
    change = [updated[piece] - current[piece] for piece in range(3)]
    if is_last:
        impulses, doubles, squares = outputs
        low = lanes_low((8, 128))
        for piece in range(3):
            merged = jnp.where(low, updated[piece][0:8], updated[piece][8:16])
            for t in range(8):
                impulses[piece : piece + 1, 128 * t : 128 * t + 128] = merged[t : t + 1]
        doubles[...] = twice(*updated)
        total = change[0] * change[0] + change[1] * change[1] + change[2] * change[2]
        total = jnp.where(lanes_low((CB, 128)), total, 0.0)
        total = jnp.sum(jnp.sum(total, axis=1, keepdims=True), axis=0, keepdims=True)
        squares[...] = jnp.broadcast_to(total.reshape(1, 1, 1), squares.shape)
        return
    if not is_first:
        payload, new_current, new_advance = outputs
    ahead = [updated[piece] + weight * change[piece] for piece in range(3)]
    for piece in range(3):
        new_current[piece] = updated[piece]
        new_advance[piece] = ahead[piece]
    picked = dot(pick[...], twice(*ahead)).astype(bf16)
    forces = push(picked, tiles).astype(bf16)
    tail_out = jnp.where(iota((8, WIDE), 0) == 0, tire_row(*ahead), 0.0).astype(bf16)
    for peer in range(SOIL):
        payload[peer, 0:64] = forces
        payload[peer, 64:72] = tail_out


def last_kernel(doubles, pick, tiles, owner_pick, labels, across, payload):
    picked = dot(pick[...], doubles[...]).astype(bf16)
    forces = push(picked, tiles)
    rows = dot(owner_pick[...], split_terms(forces, 3))
    payload[:, :, 0:WIDE] = rows.reshape(SOIL, 8, WIDE)
    squares = jnp.sum(across[:, 0, :], axis=0, keepdims=True)
    is_square = (iota((128, 128), 0) & 7) == CAP
    payload[:, :, WIDE:] = jnp.where(is_square, squares, labels[...]).reshape(SOIL, 8, 128)


def totals_kernel(scale, arrived, mass, velocity, norm):
    rows = arrived[:, :, 0:WIDE].reshape(128, WIDE)
    extra = arrived[:, :, WIDE:].reshape(128, 128)
    is_square = (iota((128, 128), 0) & 7) == CAP
    squares = jnp.sum(jnp.where(is_square, extra, 0.0), axis=0, keepdims=True)[:, 0:1]
    norm[...] = jnp.sqrt(squares * scale + hold_eps) / step_size
    lane = (iota((128, 128), 1) + 1).astype(f32)
    is_force = (iota((128, 128), 0) & 7) < CAP
    chosen = jnp.where((extra == lane) & is_force, 1.0, 0.0)
    chosen = chosen.T[0:NB].astype(bf16)
    totals = dot(jnp.concatenate([chosen] * 3, axis=1), split_terms(rows, 3)) * mass[...]
    low = lanes_low((8, 128))
    for piece in range(3):
        tile = totals[:, 128 * piece : 128 * piece + 128]
        even, odd = tile[0:8], tile[8:16]
        for half, merged in enumerate(
            (
                jnp.where(low, even, pltpu.roll(odd, BLK, 1)),
                jnp.where(low, pltpu.roll(even, BLK, 1), odd),
            )
        ):
            component = 2 * piece + half
            for t in range(8):
                velocity[component : component + 1, 128 * t : 128 * t + 128] = merged[t : t + 1]


def on_device(
    warm_start,
    right_side,
    friction,
    inverse_mass,
    jacobian,
    compliance,
    entry_block,
    entry_owner,
    entry_body,
    block_count,
):
    regions = lax.axis_size("grp")
    contacts = warm_start.shape[1]
    elements = 3 * contacts * SOIL * regions
    state = shape_of((3, CB, 128), f32)

    def line(array):
        return far(array.reshape(1, -1))

    (
        payload,
        tiles,
        pick,
        id_column,
        owner_pick,
        labels,
        warm,
        right,
        rough,
        mass_tiles,
    ) = pl.pallas_call(
        first_kernel,
        out_shape=(
            shape_of((SOIL, SEND_FIRST, WIDE), bf16),
            resident((ENT, TALL, WIDE), bf16),
            shape_of((ENT, CB), bf16),
            shape_of((ENT, 128), f32),
            shape_of((128, 3 * ENT), bf16),
            shape_of((128, 128), f32),
            state,
            state,
            shape_of((CB, 128), f32),
            shape_of((NB, WIDE), f32),
        ),
        in_specs=[SCALAR] + [IN_HBM] * 8,
        out_specs=(VECTOR,) * 10,
        scratch_shapes=[
            pltpu.VMEM((1, ENT), i32),
            pltpu.VMEM((1, ENT), i32),
            pltpu.VMEM((1, ENT), i32),
            pltpu.VMEM((3, contacts), f32),
            pltpu.VMEM((3, contacts), f32),
            pltpu.VMEM((1, contacts), f32),
            pltpu.VMEM((6, contacts), f32),
            pltpu.SemaphoreType.DMA((7,)),
            pltpu.SemaphoreType.DMA((ENT // 16,)),
        ],
        compiler_params=params(8),
        name="first",
    )(
        block_count,
        line(entry_owner),
        line(entry_body),
        line(entry_block),
        far(warm_start),
        far(right_side),
        line(friction),
        far(inverse_mass),
        far(jacobian),
    )
    weights = momentum_weights(ITERS)
    current = warm
    advance = warm
    for iteration in range(ITERS):
        arrived = lax.all_to_all(payload, "soil", 0, 0, tiled=True)
        is_first, is_last = iteration == 0, iteration == ITERS - 1
        scratch = [pltpu.VMEM((SOIL, SOIL * 3 * TC), bf16)]
        if is_last:
            outs = [
                shape_of((3, contacts), f32),
                shape_of((CB, WIDE), bf16),
                shape_of((regions, 1, 128), f32),
            ]
        else:
            outs = [shape_of((SOIL, SEND, WIDE), bf16), state, state]
        if is_first:
            outs += [
                shape_of((ENT, ENT * SOIL), bf16),
                shape_of((ENT, WIDE), f32),
                resident(compliance.shape, bf16),
            ]
            scratch.append(pltpu.SemaphoreType.DMA)
            more, more_specs = [id_column, far(compliance)], [VECTOR, IN_HBM]
        else:
            more, more_specs = [match, mass_rows, keep(matrix)], [VECTOR] * 3
        results = pl.pallas_call(
            functools.partial(step_kernel, weights[iteration], is_first, is_last),
            out_shape=tuple(outs),
            in_specs=[SCALAR] + [VECTOR] * 7 + more_specs,
            out_specs=(VECTOR,) * len(outs),
            scratch_shapes=scratch,
            compiler_params=params(10),
            name=f"step{iteration}",
        )(entry_block, arrived, pick, keep(tiles), current, advance, right, rough, *more)
        if is_last:
            impulses, doubles, squares = results
            break
        payload, current, advance = results[:3]
        if is_first:
            match, mass_rows, matrix = results[3:]

    across = lax.all_to_all(squares, "grp", 0, 0, tiled=True)
    outgoing = pl.pallas_call(
        last_kernel,
        out_shape=shape_of((SOIL, 8, WIDE + 128), f32),
        in_specs=[VECTOR] * 6,
        out_specs=VECTOR,
        compiler_params=params(6),
        name="last",
    )(doubles, pick, keep(tiles), owner_pick, labels, across)
    arrived = lax.all_to_all(outgoing, "soil", 0, 0, tiled=True)
    velocity, norm = pl.pallas_call(
        functools.partial(totals_kernel, 1.0 / elements),
        out_shape=(shape_of((6, contacts), f32), shape_of((1, 1), f32)),
        in_specs=[VECTOR] * 2,
        out_specs=(VECTOR, VECTOR),
        compiler_params=params(4),
        name="totals",
    )(arrived, mass_tiles)
    return (impulses, velocity, norm[0, 0])


def solution(mesh):
    placed = (
        P(None, ("grp", "soil")),
        P(None, ("grp", "soil")),
        P(("grp", "soil")),
        P(None, ("grp", "soil")),
        P(("grp", "soil"), None, None),
        P(None, "soil"),
        P(("grp", "soil")),
        P(("grp", "soil")),
        P(("grp", "soil")),
        P(("grp", "soil")),
    )
    return jax.shard_map(
        on_device,
        mesh=mesh,
        in_specs=placed,
        out_specs=(P(None, ("grp", "soil")), P(None, ("grp", "soil")), P()),
        check_vma=False,
    )
```

```python
import functools
import math

import jax
import jax.numpy as jnp
from jax import lax
from jax.experimental import pallas as pl
from jax.experimental.pallas import tpu as pltpu
from jax.sharding import PartitionSpec as P

BLK = 64
CB = 16
NB = 16
TC = 128
CAP = 4
ITERS = 3
ENT = 64
SOIL = 16
BODIES = SOIL * NB
WIDE = 6 * BLK
TALL = 3 * BLK
SHARED = 32
ROWS = SOIL * SHARED
SEND = SHARED + 8

step_size = 0.1
hold_eps = 1e-06

bf16, f32, i32 = jnp.bfloat16, jnp.float32, jnp.int32

IN_HBM = pl.BlockSpec(memory_space=pltpu.HBM)
VECTOR = pl.BlockSpec(memory_space=pltpu.VMEM)
SCALAR = pl.BlockSpec(memory_space=pltpu.SMEM)


def momentum_weights(number):
    nesterov = 1.0
    weights = []
    for iteration in range(number):
        following = 0.5 * (-nesterov * nesterov + nesterov * math.sqrt(nesterov * nesterov + 4.0))
        weights.append(nesterov * (1.0 - nesterov) / (nesterov * nesterov + following))
        nesterov = following
    return weights


def resident(shape, dtype):
    return pltpu.VMEM(shape, dtype)


def keep(array):
    return pltpu.with_memory_space_constraint(array, pltpu.VMEM)


def far(array):
    return pltpu.with_memory_space_constraint(array, pltpu.HBM)


def shape_of(shape, dtype):
    return jax.ShapeDtypeStruct(shape, dtype)


def params(megabytes):
    return pltpu.CompilerParams(vmem_limit_bytes=megabytes << 20)


def iota(shape, dim):
    return lax.broadcasted_iota(i32, shape, dim)


def ones_where(mask):
    return jnp.where(mask, 1.0, 0.0).astype(bf16)


def dot(left, right):
    return jnp.dot(left, right, preferred_element_type=f32)


def dot_rows(left, right):
    return lax.dot_general(left, right, (((1,), (1,)), ((), ())), preferred_element_type=f32)


def split_terms(values, terms):
    parts = []
    for _ in range(terms):
        part = values.astype(bf16)
        parts.append(part)
        values = values - part.astype(f32)
    return jnp.concatenate(parts, axis=0)


def order(block):
    return ((block & 1) << 3) + (block >> 1)


def lanes_low(shape):
    return iota(shape, len(shape) - 1) < BLK


def both(values, upper):
    low = lanes_low(values.shape)
    turned = pltpu.roll(values, BLK, 1)
    return jnp.where(low, turned, values) if upper else jnp.where(low, values, turned)


def lane_tiles(ref, row):
    return jnp.concatenate([ref[row : row + 1, 128 * t : 128 * t + 128] for t in range(8)], axis=0)


def doubled(ref, row):
    tiles = lane_tiles(ref, row)
    return jnp.concatenate([both(tiles, False), both(tiles, True)], axis=0)


def twice(normal, first, second):
    low = lanes_low((CB, 2 * BLK))
    return jnp.concatenate(
        [
            jnp.where(low, normal, first),
            jnp.where(low, second, normal),
            jnp.where(low, first, second),
        ],
        axis=1,
    ).astype(bf16)


PUSH_LOOP = True
PULL_LOOP = False
PULL_PARTS = 4


def push(picked, tiles, forces, wait=None):
    column = iota((16, 16 * TALL), 1)
    first = iota((16, 16 * TALL), 0) * TALL
    mask = ones_where((column >= first) & (column < first + TALL))

    def group(half, part):
        if wait is not None:
            wait(half, part)
        start = 32 * half + 16 * part
        rows = picked[pl.ds(start, 16)]
        spread = jnp.concatenate([rows] * 8, axis=1) * mask
        weights = tiles[pl.ds(16 * part, 16), :, WIDE * half : WIDE * half + WIDE]
        forces[pl.ds(start, 16)] = dot(spread, weights.reshape(16 * TALL, WIDE))

    if PUSH_LOOP and wait is None:

        def step(part, carry):
            group(0, part)
            group(1, part)
            return carry

        lax.fori_loop(0, 2, step, 0)
    else:
        for part in range(2):
            for half in range(2):
                group(half, part)


def pull(wanted, pick_t, tiles):
    empty = jnp.zeros((ENT // 2, WIDE), bf16)
    sides = jnp.concatenate(
        [
            jnp.concatenate([wanted[0:32], empty], axis=1),
            jnp.concatenate([empty, wanted[32:64]], axis=1),
        ],
        axis=0,
    )
    size = 32 // PULL_PARTS
    lane = iota((TALL, ENT), 1) & 31

    def step(part, total):
        rows = tiles[pl.ds(size * part, size)].reshape(size * TALL, 2 * WIDE)
        products = dot_rows(rows, sides)
        for pair in range(size):
            total += jnp.where(
                lane == size * part + pair, products[TALL * pair : TALL * pair + TALL], 0.0
            )
        return total

    total = jnp.zeros((TALL, ENT), f32)
    if PULL_LOOP:
        total = lax.fori_loop(0, PULL_PARTS, step, total)
    else:
        for part in range(PULL_PARTS):
            total = step(part, total)
    return dot(pick_t, split_terms(total.T, 3))


def tire_row(normal, first, second):
    low = lanes_low((1, 128))
    return jnp.concatenate(
        [jnp.where(low, part[0:1], part[8:9]) for part in (normal, first, second)], axis=1
    )


def eye(size):
    return ones_where(iota((size, size), 0) == iota((size, size), 1))


def first_kernel(
    count,
    owner_far,
    body_far,
    block_far,
    warm_far,
    right_far,
    rough_far,
    mass_far,
    tiles_far,
    payload,
    tiles,
    pick_out,
    pick_t_out,
    id_out,
    slot_out,
    owner_pick,
    labels,
    warm_out,
    right_out,
    rough_out,
    mass_out,
    owner,
    body,
    block,
    warm,
    right,
    rough,
    mass,
    picked,
    forces,
    sems,
    tile_sems,
):
    small = [
        pltpu.make_async_copy(source, target, sems.at[n])
        for n, (source, target) in enumerate(
            [
                (block_far, block),
                (warm_far, warm),
                (owner_far, owner),
                (body_far, body),
                (mass_far, mass),
                (right_far, right),
                (rough_far, rough),
            ]
        )
    ]
    copies = {}
    for part in range(2):
        for half in range(2):
            copies[half, part] = pltpu.make_async_copy(
                tiles_far.at[pl.ds(32 * half + 16 * part, 16)],
                tiles.at[pl.ds(16 * part, 16), :, pl.ds(WIDE * half, WIDE)],
                tile_sems.at[2 * part + half],
            )
    for copy in small + list(copies.values()):
        copy.start()
    for copy in small:
        copy.wait()
    live = iota((1, ENT), 1) < count[0]
    pick_t = ones_where((iota((CB, ENT), 0) == order(block[...])) & live)
    pick = dot_rows(eye(ENT), pick_t).astype(bf16)
    pick_out[...] = pick
    pick_t_out[...] = jnp.concatenate([pick_t] * 3, axis=1)
    advance = [doubled(warm, piece) for piece in range(3)]
    for piece in range(3):
        warm_out[piece] = advance[piece]
        right_out[piece] = doubled(right, piece)
    rough_out[...] = doubled(rough, 0)
    low = lanes_low((8, 128))
    lanes = []
    for piece in range(3):
        even, odd = lane_tiles(mass, 2 * piece), lane_tiles(mass, 2 * piece + 1)
        lanes.append(
            jnp.concatenate(
                [
                    jnp.where(low, even, pltpu.roll(odd, BLK, 1)),
                    jnp.where(low, pltpu.roll(even, BLK, 1), odd),
                ],
                axis=0,
            )
        )
    mass_tiles = jnp.concatenate(lanes, axis=1)
    mass_out[...] = mass_tiles
    ids = jnp.where(live, owner[...] * NB + order(body[...]), -1)
    hits_t = ones_where(iota((BODIES, ENT), 0) == ids)
    counts = dot_rows(jnp.ones((8, ENT), bf16), hits_t)
    named = jnp.where(counts > 0, 1.0, 0.0)
    named = jnp.concatenate([named, jnp.zeros((8, WIDE - BODIES), f32)], axis=1)

    owner_row = jnp.where(live, owner[...], -1)
    owner_hit = ones_where(iota((SOIL, ENT), 0) == owner_row)
    earlier = ones_where(iota((ENT, ENT), 0) < iota((ENT, ENT), 1))
    rank = jnp.sum(dot(owner_hit, earlier) * owner_hit.astype(f32), axis=0, keepdims=True)
    slot = jnp.where(live, (owner_row * 8).astype(f32) + rank, -100.0)
    line = iota((128, ENT), 0)
    chosen = ones_where(line.astype(f32) == slot)
    owner_pick[...] = jnp.concatenate([chosen, chosen, chosen], axis=1)
    again = ones_where((line.astype(f32) == slot) | ((line - CAP).astype(f32) == slot))
    label = jnp.where(live, order(body[...]) + 1, 0).astype(bf16)
    label_rows = dot_rows(again, jnp.broadcast_to(label, (128, ENT)))
    labels[...] = label_rows
    for_columns = jnp.concatenate(
        [
            jnp.broadcast_to(slot, (8, ENT)),
            jnp.broadcast_to(ids.astype(f32), (8, ENT)),
        ],
        axis=0,
    )
    columns = dot_rows(eye(ENT), for_columns.astype(bf16))
    slot_out[...] = jnp.broadcast_to(columns[:, 0:1], (ENT, 128))
    id_out[...] = jnp.broadcast_to(columns[:, 8:9], (ENT, 128))

    place = iota((128, WIDE), 0) & 7
    tire = tire_row(*advance).astype(bf16).astype(f32)
    picked[...] = dot(pick, twice(*advance)).astype(bf16)
    push(picked, tiles, forces, lambda half, part: copies[half, part].wait())
    rows = dot(owner_pick[...], split_terms(forces[...], 3))
    rows = jnp.where(place == CAP, tire, jnp.where(place == CAP + 1, named[0:1], rows))
    payload[:, :, 0:WIDE] = rows.reshape(SOIL, 8, WIDE)
    payload[:, :, WIDE:] = label_rows.reshape(SOIL, 8, 128)


def owner_kernel(
    arrived,
    mass,
    id_column,
    matrix_far,
    payload,
    tire_out,
    share,
    share_t,
    own,
    matrix,
    sem,
):
    copy = pltpu.make_async_copy(matrix_far, matrix, sem)
    copy.start()
    me = lax.axis_index("soil")
    rows = arrived[:, :, 0:WIDE].reshape(128, WIDE)
    extra = arrived[:, :, WIDE:].reshape(128, 128)
    lane = iota((128, 128), 1)
    place = iota((128, 128), 0) & 7
    chosen = jnp.where(extra == ((lane & 15) + 1).astype(f32), 1.0, 0.0)
    gather = jnp.where(place < CAP, chosen, 0.0).T[0:NB].astype(bf16)
    totals = dot(jnp.concatenate([gather] * 3, axis=1), split_terms(rows, 3)) * mass[...]
    back = jnp.concatenate([totals.astype(bf16), split_terms(mass[...], 3)], axis=0)
    scatter = jnp.where((lane < NB) == (place < CAP), chosen, 0.0)[:, 0 : 4 * NB]
    payload[...] = dot(scatter.astype(bf16), back).reshape(SOIL, 8, WIDE)

    tail_lane = iota((2 * SOIL, 128), 1)
    tail_row = iota((2 * SOIL, 128), 0)
    tail_pick = ones_where(tail_lane == (tail_row & (SOIL - 1)) * 8 + CAP + (tail_row >> 4))
    tails = dot(tail_pick, rows.astype(bf16))
    tire_out[...] = tails[0:SOIL]
    all_named = tails[SOIL:, 0:BODIES]

    mine = iota((SOIL, BODIES), 0) == me
    named = jnp.sum(jnp.where(mine, all_named, 0.0), axis=0, keepdims=True)
    hits = ones_where(id_column[:, 0:1] == iota((ENT, BODIES), 1).astype(f32))
    hits_two = jnp.concatenate([hits, hits], axis=0)
    common = jnp.where(mine, 0.0, all_named * named)
    earlier = ones_where(iota((BODIES, BODIES), 0) < iota((BODIES, BODIES), 1))
    slots = jnp.where(common > 0, dot(common.astype(bf16), earlier) + 1.0, 0.0).astype(bf16)
    rank_t = dot_rows(hits, slots).astype(bf16)
    lane_start = iota((SOIL, ROWS), 0) * SHARED
    lanes = iota((SOIL, ROWS), 1)
    spread_lanes = ones_where((lanes >= lane_start) & (lanes < lane_start + SHARED))
    lane_rank = ((iota((ENT, ROWS), 1) & (SHARED - 1)) + 1).astype(f32)
    share_t[...] = ones_where(dot(rank_t, spread_lanes) == lane_rank)
    rank_two = dot_rows(slots, hits_two).astype(bf16)
    row_start = iota((ROWS, SOIL), 1) * SHARED
    row = iota((ROWS, SOIL), 0)
    spread_rows = ones_where((row >= row_start) & (row < row_start + SHARED))
    row_rank = ((iota((ROWS, 128), 0) & (SHARED - 1)) + 1).astype(f32)
    share[...] = ones_where(dot(spread_rows, rank_two) == row_rank)
    own[...] = dot_rows(hits, hits_two).astype(bf16)
    copy.wait()


def project_cone(normal, tangent_one, tangent_two, friction):
    tangent_size = jnp.sqrt(tangent_one * tangent_one + tangent_two * tangent_two)
    inside = tangent_size <= friction * normal
    polar_side = friction * tangent_size <= -normal
    middle = jnp.logical_not(jnp.logical_or(inside, polar_side))
    safe_size = jnp.where(middle, tangent_size, 1.0)
    new_normal = (friction * tangent_size + normal) / (1.0 + friction * friction)
    shrink = friction * new_normal / safe_size
    out_normal = jnp.where(inside, normal, jnp.where(polar_side, 0.0, new_normal))
    factor = jnp.where(inside, 1.0, jnp.where(polar_side, 0.0, shrink))
    return out_normal, tangent_one * factor, tangent_two * factor


def step_kernel(
    weight,
    is_first,
    is_last,
    arrived,
    pick,
    pick_t,
    share,
    tiles,
    matrix,
    current,
    advance,
    right_side,
    friction,
    *rest,
):
    if is_first:
        tire_in, slot_column = rest[0:2]
        payload, new_current, new_advance, new_forces, mass_rows = rest[2:7]
        tire_all = tire_in[...]
        rows = arrived[...].reshape(128, WIDE)
        lane = iota((ENT, 128), 1).astype(f32)
        slot = slot_column[:, 0:1]
        wanted = dot(ones_where(lane == slot), rows.astype(bf16))
        for_mass = ones_where(lane == slot + CAP)
        mass_rows[...] = dot(
            jnp.concatenate([for_mass] * 3, axis=1), split_terms(rows, 3)
        )
    else:
        forces_in, share_t, own, mass_rows = rest[0:4]
        outputs = rest[4:-2]
        tail = arrived[:, SHARED:SEND, :].astype(f32).reshape(8 * SOIL, WIDE).astype(bf16)
        tail_lane = iota((SOIL, 8 * SOIL), 1)
        tail_row = iota((SOIL, 8 * SOIL), 0)
        tire_all = dot(ones_where(tail_lane == tail_row * 8), tail)
        received = arrived[:, 0:SHARED, :].reshape(ROWS, WIDE)
        sums = dot(share_t[...], received) + dot(own[...], split_terms(forces_in[...], 2))
        wanted = sums * mass_rows[...]
    spread, picked = rest[-2:]
    pulled = pull(wanted.astype(bf16), pick_t[...], tiles)

    device = iota((SOIL, WIDE), 0)
    for peer in range(SOIL):
        spread[:, WIDE * peer : WIDE * peer + WIDE] = jnp.where(
            device == peer, tire_all, 0.0
        ).astype(bf16)
    tire = jnp.sum(dot(spread[...], matrix[...]), axis=0, keepdims=True)

    row = iota((CB, 128), 0)
    last = jnp.concatenate([pulled[:, 128:192], pulled[:, 128:192]], axis=1)
    pieces = (both(pulled[:, 0:128], False), both(pulled[:, 0:128], True), last)
    moved = []
    for piece in range(3):
        line = jnp.broadcast_to(tire[:, 128 * piece : 128 * piece + 128], (CB, 128))
        added = jnp.where(
            row == 0, both(line, False), jnp.where(row == 8, both(line, True), 0.0)
        )
        gradient = pieces[piece] + added + right_side[piece]
        moved.append(advance[piece] - step_size * gradient)
    updated = project_cone(*moved, friction[...])
    change = [updated[piece] - current[piece] for piece in range(3)]
    if is_last:
        impulses, doubles, squares = outputs
        low = lanes_low((8, 128))
        for piece in range(3):
            merged = jnp.where(low, updated[piece][0:8], updated[piece][8:16])
            for t in range(8):
                impulses[piece : piece + 1, 128 * t : 128 * t + 128] = merged[t : t + 1]
        doubles[...] = twice(*updated)
        total = change[0] * change[0] + change[1] * change[1] + change[2] * change[2]
        total = jnp.where(lanes_low((CB, 128)), total, 0.0)
        total = jnp.sum(jnp.sum(total, axis=1, keepdims=True), axis=0, keepdims=True)
        squares[...] = jnp.broadcast_to(total.reshape(1, 1, 1), squares.shape)
        return
    if not is_first:
        payload, new_current, new_advance, new_forces = outputs
    ahead = [updated[piece] + weight * change[piece] for piece in range(3)]
    for piece in range(3):
        new_current[piece] = updated[piece]
        new_advance[piece] = ahead[piece]
    picked[...] = dot(pick[...], twice(*ahead)).astype(bf16)
    push(picked, tiles, new_forces)
    shares = dot(share[...], split_terms(new_forces[...], 2)).astype(bf16)
    payload[:, 0:SHARED, :] = shares.reshape(SOIL, SHARED, WIDE)
    tail_out = jnp.where(iota((8, WIDE), 0) == 0, tire_row(*ahead), 0.0).astype(bf16)
    for peer in range(SOIL):
        payload[peer, SHARED:SEND] = tail_out


def last_kernel(doubles, pick, tiles, owner_pick, labels, across, payload, picked, forces):
    picked[...] = dot(pick[...], doubles[...]).astype(bf16)
    push(picked, tiles, forces)
    rows = dot(owner_pick[...], split_terms(forces[...], 3))
    payload[:, :, 0:WIDE] = rows.reshape(SOIL, 8, WIDE)
    squares = jnp.sum(across[:, 0, :], axis=0, keepdims=True)
    extra = jnp.where(lanes_low((128, 128)), labels[...], squares)
    payload[:, :, WIDE:] = extra.reshape(SOIL, 8, 128)


def totals_kernel(scale, arrived, mass, velocity, norm):
    rows = arrived[:, :, 0:WIDE].reshape(128, WIDE)
    extra = arrived[:, :, WIDE:].reshape(128, 128)
    is_first = (iota((128, 128), 0) & 7) == 0
    squares = jnp.sum(jnp.where(is_first, extra, 0.0), axis=0, keepdims=True)[:, BLK : BLK + 1]
    norm[...] = jnp.sqrt(squares * scale + hold_eps) / step_size
    lane = (iota((128, 128), 1) + 1).astype(f32)
    is_force = (iota((128, 128), 0) & 7) < CAP
    chosen = jnp.where((extra == lane) & is_force, 1.0, 0.0)
    chosen = chosen.T[0:NB].astype(bf16)
    totals = dot(jnp.concatenate([chosen] * 3, axis=1), split_terms(rows, 3)) * mass[...]
    low = lanes_low((8, 128))
    for piece in range(3):
        tile = totals[:, 128 * piece : 128 * piece + 128]
        even, odd = tile[0:8], tile[8:16]
        for half, merged in enumerate(
            (
                jnp.where(low, even, pltpu.roll(odd, BLK, 1)),
                jnp.where(low, pltpu.roll(even, BLK, 1), odd),
            )
        ):
            component = 2 * piece + half
            for t in range(8):
                velocity[component : component + 1, 128 * t : 128 * t + 128] = merged[t : t + 1]


def step_scratch():
    return [pltpu.VMEM((SOIL, SOIL * 3 * TC), bf16), pltpu.VMEM((ENT, WIDE), bf16)]


def on_device(
    warm_start,
    right_side,
    friction,
    inverse_mass,
    jacobian,
    compliance,
    entry_block,
    entry_owner,
    entry_body,
    block_count,
):
    regions = lax.axis_size("grp")
    contacts = warm_start.shape[1]
    elements = 3 * contacts * SOIL * regions
    state = shape_of((3, CB, 128), f32)

    def line(array):
        return far(array.reshape(1, -1))

    (
        payload,
        tiles,
        pick,
        pick_t,
        id_column,
        slot_column,
        owner_pick,
        labels,
        warm,
        right,
        rough,
        mass_tiles,
    ) = pl.pallas_call(
        first_kernel,
        out_shape=(
            shape_of((SOIL, 8, WIDE + 128), f32),
            resident((ENT // 2, TALL, 2 * WIDE), bf16),
            shape_of((ENT, CB), bf16),
            shape_of((CB, 3 * ENT), bf16),
            shape_of((ENT, 128), f32),
            shape_of((ENT, 128), f32),
            shape_of((128, 3 * ENT), bf16),
            shape_of((128, 128), f32),
            state,
            state,
            shape_of((CB, 128), f32),
            shape_of((NB, WIDE), f32),
        ),
        in_specs=[SCALAR] + [IN_HBM] * 8,
        out_specs=(VECTOR,) * 12,
        scratch_shapes=[
            pltpu.VMEM((1, ENT), i32),
            pltpu.VMEM((1, ENT), i32),
            pltpu.VMEM((1, ENT), i32),
            pltpu.VMEM((3, contacts), f32),
            pltpu.VMEM((3, contacts), f32),
            pltpu.VMEM((1, contacts), f32),
            pltpu.VMEM((6, contacts), f32),
            pltpu.VMEM((ENT, WIDE), bf16),
            pltpu.VMEM((ENT, WIDE), f32),
            pltpu.SemaphoreType.DMA((7,)),
            pltpu.SemaphoreType.DMA((ENT // 16,)),
        ],
        compiler_params=params(8),
        name="first",
    )(
        block_count,
        line(entry_owner),
        line(entry_body),
        line(entry_block),
        far(warm_start),
        far(right_side),
        line(friction),
        far(inverse_mass),
        far(jacobian),
    )
    arrived = lax.all_to_all(payload, "soil", 0, 0, tiled=True)
    payload, tire_all, share, share_t, own, matrix = pl.pallas_call(
        owner_kernel,
        out_shape=(
            shape_of((SOIL, 8, WIDE), f32),
            shape_of((SOIL, WIDE), f32),
            shape_of((ROWS, 128), bf16),
            shape_of((ENT, ROWS), bf16),
            shape_of((ENT, 128), bf16),
            resident(compliance.shape, bf16),
        ),
        in_specs=[VECTOR] * 3 + [IN_HBM],
        out_specs=(VECTOR,) * 6,
        scratch_shapes=[pltpu.SemaphoreType.DMA],
        compiler_params=params(6),
        name="owner",
    )(arrived, mass_tiles, id_column, far(compliance))

    weights = momentum_weights(ITERS)
    current = warm
    advance = warm
    for iteration in range(ITERS):
        arrived = lax.all_to_all(payload, "soil", 0, 0, tiled=True)
        is_first, is_last = iteration == 0, iteration == ITERS - 1
        if is_last:
            outs = [
                shape_of((3, contacts), f32),
                shape_of((CB, WIDE), bf16),
                shape_of((regions, 1, 128), f32),
            ]
        else:
            outs = [
                shape_of((SOIL, SEND, WIDE), bf16),
                state,
                state,
                shape_of((ENT, WIDE), f32),
            ]
        if is_first:
            outs.append(shape_of((ENT, WIDE), f32))
            more = [tire_all, slot_column]
        else:
            more = [forces, share_t, own, mass_rows]
        results = pl.pallas_call(
            functools.partial(step_kernel, weights[iteration], is_first, is_last),
            out_shape=tuple(outs),
            in_specs=[VECTOR] * (10 + len(more)),
            out_specs=(VECTOR,) * len(outs),
            scratch_shapes=step_scratch(),
            compiler_params=params(12),
            name=f"step{iteration}",
        )(
            arrived,
            pick,
            pick_t,
            share,
            keep(tiles),
            keep(matrix),
            current,
            advance,
            right,
            rough,
            *more,
        )
        if is_last:
            impulses, doubles, squares = results
            break
        payload, current, advance, forces = results[:4]
        if is_first:
            mass_rows = results[4]

    across = lax.all_to_all(squares, "grp", 0, 0, tiled=True)
    outgoing = pl.pallas_call(
        last_kernel,
        out_shape=shape_of((SOIL, 8, WIDE + 128), f32),
        in_specs=[VECTOR] * 6,
        out_specs=VECTOR,
        scratch_shapes=[pltpu.VMEM((ENT, WIDE), bf16), pltpu.VMEM((ENT, WIDE), f32)],
        compiler_params=params(6),
        name="last",
    )(doubles, pick, keep(tiles), owner_pick, labels, across)
    arrived = lax.all_to_all(outgoing, "soil", 0, 0, tiled=True)
    velocity, norm = pl.pallas_call(
        functools.partial(totals_kernel, 1.0 / elements),
        out_shape=(shape_of((6, contacts), f32), shape_of((1, 1), f32)),
        in_specs=[VECTOR] * 2,
        out_specs=(VECTOR, VECTOR),
        compiler_params=params(4),
        name="totals",
    )(arrived, mass_tiles)
    return (impulses, velocity, norm[0, 0])


def solution(mesh):
    placed = (
        P(None, ("grp", "soil")),
        P(None, ("grp", "soil")),
        P(("grp", "soil")),
        P(None, ("grp", "soil")),
        P(("grp", "soil"), None, None),
        P(None, "soil"),
        P(("grp", "soil")),
        P(("grp", "soil")),
        P(("grp", "soil")),
        P(("grp", "soil")),
    )
    return jax.shard_map(
        on_device,
        mesh=mesh,
        in_specs=placed,
        out_specs=(P(None, ("grp", "soil")), P(None, ("grp", "soil")), P()),
        check_vma=False,
    )
```

```python
import functools
import math

import jax
import jax.numpy as jnp
from jax import lax
from jax.experimental import pallas as pl
from jax.experimental.pallas import tpu as pltpu
from jax.sharding import PartitionSpec as P

BLK = 64
CB = 16
NB = 16
TC = 128
CAP = 4
ITERS = 3
ENT = 64
SOIL = 16
BODIES = SOIL * NB
WIDE = 6 * BLK
TALL = 3 * BLK
SHARED = 32
ROWS = SOIL * SHARED
SEND = SHARED + 8

step_size = 0.1
hold_eps = 1e-06

bf16, f32, i32 = jnp.bfloat16, jnp.float32, jnp.int32

IN_HBM = pl.BlockSpec(memory_space=pltpu.HBM)
VECTOR = pl.BlockSpec(memory_space=pltpu.VMEM)
SCALAR = pl.BlockSpec(memory_space=pltpu.SMEM)


def momentum_weights(number):
    nesterov = 1.0
    weights = []
    for iteration in range(number):
        following = 0.5 * (-nesterov * nesterov + nesterov * math.sqrt(nesterov * nesterov + 4.0))
        weights.append(nesterov * (1.0 - nesterov) / (nesterov * nesterov + following))
        nesterov = following
    return weights


def resident(shape, dtype):
    return pltpu.VMEM(shape, dtype)


def keep(array):
    return pltpu.with_memory_space_constraint(array, pltpu.VMEM)


def far(array):
    return pltpu.with_memory_space_constraint(array, pltpu.HBM)


def shape_of(shape, dtype):
    return jax.ShapeDtypeStruct(shape, dtype)


def params(megabytes):
    return pltpu.CompilerParams(vmem_limit_bytes=megabytes << 20)


def iota(shape, dim):
    return lax.broadcasted_iota(i32, shape, dim)


def ones_where(mask):
    return jnp.where(mask, 1.0, 0.0).astype(bf16)


def dot(left, right):
    return jnp.dot(left, right, preferred_element_type=f32)


def dot_rows(left, right):
    return lax.dot_general(left, right, (((1,), (1,)), ((), ())), preferred_element_type=f32)


def split_terms(values, terms):
    parts = []
    for _ in range(terms):
        part = values.astype(bf16)
        parts.append(part)
        values = values - part.astype(f32)
    return jnp.concatenate(parts, axis=0)


def order(block):
    return ((block & 1) << 3) + (block >> 1)


def lanes_low(shape):
    return iota(shape, len(shape) - 1) < BLK


def both(values, upper):
    low = lanes_low(values.shape)
    turned = pltpu.roll(values, BLK, 1)
    return jnp.where(low, turned, values) if upper else jnp.where(low, values, turned)


def lane_tiles(ref, row):
    return jnp.concatenate([ref[row : row + 1, 128 * t : 128 * t + 128] for t in range(8)], axis=0)


def doubled(ref, row):
    tiles = lane_tiles(ref, row)
    return jnp.concatenate([both(tiles, False), both(tiles, True)], axis=0)


def twice(normal, first, second):
    low = lanes_low((CB, 2 * BLK))
    return jnp.concatenate(
        [
            jnp.where(low, normal, first),
            jnp.where(low, second, normal),
            jnp.where(low, first, second),
        ],
        axis=1,
    ).astype(bf16)


def entry_mask():
    column = iota((16, 16 * TALL), 1)
    first = iota((16, 16 * TALL), 0) * TALL
    return ones_where((column >= first) & (column < first + TALL))


def push(picked, tiles, forces):
    mask = entry_mask()

    def group(number):
        rows = picked[pl.ds(16 * number, 16)]
        spread = jnp.concatenate([rows] * 8, axis=1) * mask
        weights = tiles[pl.ds(16 * number, 16)].reshape(16 * TALL, WIDE)
        forces[pl.ds(16 * number, 16)] = dot(spread, weights)

    def step(number, carry):
        group(number)
        group(number + 2)
        return carry

    lax.fori_loop(0, 2, step, 0)


def pull(wanted, pick_t, flipped):
    row = iota((16, WIDE), 0)
    lower, upper = [], []
    for part in range(2):
        sides = []
        for half in range(2):
            start = 32 * half + 16 * part
            rows = wanted[start : start + 16]
            sides.append(
                jnp.concatenate(
                    [rows * ones_where(row == pair) for pair in range(16)], axis=1
                )
            )
        weights = flipped[16 * part : 16 * part + 16].reshape(16 * WIDE, WIDE)
        terms = dot(jnp.concatenate(sides, axis=0), weights)
        lower.append(terms[0:16])
        upper.append(terms[16:32])
    terms = jnp.concatenate(lower + upper, axis=0)
    wrong = (iota((ENT, WIDE), 0) < ENT // 2) == (iota((ENT, WIDE), 1) >= TALL)
    sums = dot(pick_t, split_terms(jnp.where(wrong, 0.0, terms), 3))
    left, middle, right = sums[:, 0:128], sums[:, 128:256], sums[:, 256:384]
    return (
        both(left, False) + both(middle, True),
        both(left, True) + both(right, False),
        both(middle, False) + both(right, True),
    )


def tire_row(normal, first, second):
    low = lanes_low((1, 128))
    return jnp.concatenate(
        [jnp.where(low, part[0:1], part[8:9]) for part in (normal, first, second)], axis=1
    )


def eye(size):
    return ones_where(iota((size, size), 0) == iota((size, size), 1))


def first_kernel(
    count,
    owner_far,
    body_far,
    block_far,
    warm_far,
    right_far,
    rough_far,
    mass_far,
    tiles_far,
    payload,
    tiles,
    flipped,
    pick_out,
    pick_t_out,
    id_out,
    slot_out,
    owner_pick,
    labels,
    warm_out,
    right_out,
    rough_out,
    mass_out,
    owner,
    body,
    block,
    warm,
    right,
    rough,
    mass,
    picked,
    forces,
    sems,
    tile_sems,
):
    small = [
        pltpu.make_async_copy(source, target, sems.at[n])
        for n, (source, target) in enumerate(
            [
                (block_far, block),
                (warm_far, warm),
                (owner_far, owner),
                (body_far, body),
                (mass_far, mass),
                (right_far, right),
                (rough_far, rough),
            ]
        )
    ]
    copies = []
    for start in (0, 32, 8, 40, 16, 48, 24, 56):
        part = pl.ds(start, 8)
        copies.append(
            pltpu.make_async_copy(tiles_far.at[part], tiles.at[part], tile_sems.at[start // 8])
        )
    for copy in small + copies:
        copy.start()
    for copy in small:
        copy.wait()
    live = iota((1, ENT), 1) < count[0]
    pick_t = ones_where((iota((CB, ENT), 0) == order(block[...])) & live)
    pick = dot_rows(eye(ENT), pick_t).astype(bf16)
    pick_out[...] = pick
    pick_t_out[...] = jnp.concatenate([pick_t] * 3, axis=1)
    advance = [doubled(warm, piece) for piece in range(3)]
    picked[...] = dot(pick, twice(*advance))
    def tile_part(part):
        copies[2 * part].wait()
        copies[2 * part + 1].wait()

        def step(number, carry):
            near, away = 8 * part + number, 32 + 8 * part + number
            above, below = tiles[near], tiles[away]
            flipped[near] = jnp.concatenate([above, below], axis=0).T
            for entry, tile in ((near, above), (away, below)):
                line = picked[pl.ds(entry, 1), 0:TALL].astype(bf16)
                forces[pl.ds(entry, 1)] = dot(line, tile)
            return carry

        lax.fori_loop(0, 8, step, 0, unroll=8)

    tile_part(0)
    for piece in range(3):
        warm_out[piece] = advance[piece]
        right_out[piece] = doubled(right, piece)
    rough_out[...] = doubled(rough, 0)
    low = lanes_low((8, 128))
    lanes = []
    for piece in range(3):
        even, odd = lane_tiles(mass, 2 * piece), lane_tiles(mass, 2 * piece + 1)
        lanes.append(
            jnp.concatenate(
                [
                    jnp.where(low, even, pltpu.roll(odd, BLK, 1)),
                    jnp.where(low, pltpu.roll(even, BLK, 1), odd),
                ],
                axis=0,
            )
        )
    mass_tiles = jnp.concatenate(lanes, axis=1)
    mass_out[...] = mass_tiles
    ids = jnp.where(live, owner[...] * NB + order(body[...]), -1)
    hits_t = ones_where(iota((BODIES, ENT), 0) == ids)
    counts = dot_rows(jnp.ones((8, ENT), bf16), hits_t)
    named = jnp.where(counts > 0, 1.0, 0.0)
    named = jnp.concatenate([named, jnp.zeros((8, WIDE - BODIES), f32)], axis=1)

    owner_row = jnp.where(live, owner[...], -1)
    owner_hit = ones_where(iota((SOIL, ENT), 0) == owner_row)
    earlier = ones_where(iota((ENT, ENT), 0) < iota((ENT, ENT), 1))
    rank = jnp.sum(dot(owner_hit, earlier) * owner_hit.astype(f32), axis=0, keepdims=True)
    slot = jnp.where(live, (owner_row * 8).astype(f32) + rank, -100.0)
    line = iota((128, ENT), 0)
    chosen = ones_where(line.astype(f32) == slot)
    owner_pick[...] = jnp.concatenate([chosen, chosen, chosen], axis=1)
    again = ones_where((line.astype(f32) == slot) | ((line - CAP).astype(f32) == slot))
    label = jnp.where(live, order(body[...]) + 1, 0).astype(bf16)
    label_rows = dot_rows(again, jnp.broadcast_to(label, (128, ENT)))
    labels[...] = label_rows
    for_columns = jnp.concatenate(
        [
            jnp.broadcast_to(slot, (8, ENT)),
            jnp.broadcast_to(ids.astype(f32), (8, ENT)),
        ],
        axis=0,
    )
    columns = dot_rows(eye(ENT), for_columns.astype(bf16))
    slot_out[...] = jnp.broadcast_to(columns[:, 0:1], (ENT, 128))
    id_out[...] = jnp.broadcast_to(columns[:, 8:9], (ENT, 128))

    place = iota((128, WIDE), 0) & 7
    tire = tire_row(*advance).astype(bf16).astype(f32)
    for part in range(1, 4):
        tile_part(part)
    rows = dot(owner_pick[...], split_terms(forces[...], 3))
    rows = jnp.where(place == CAP, tire, jnp.where(place == CAP + 1, named[0:1], rows))
    payload[:, :, 0:WIDE] = rows.reshape(SOIL, 8, WIDE)
    payload[:, :, WIDE:] = label_rows.reshape(SOIL, 8, 128)


def owner_kernel(arrived, mass, payload, tails_out):
    rows = arrived[:, :, 0:WIDE].reshape(128, WIDE)
    extra = arrived[:, :, WIDE:].reshape(128, 128)
    lane = iota((128, 128), 1)
    place = iota((128, 128), 0) & 7
    chosen = jnp.where(extra == ((lane & 15) + 1).astype(f32), 1.0, 0.0)
    gather = jnp.where(place < CAP, chosen, 0.0).T[0:NB].astype(bf16)
    totals = dot(jnp.concatenate([gather] * 3, axis=1), split_terms(rows, 3)) * mass[...]
    back = jnp.concatenate([totals.astype(bf16), split_terms(mass[...], 3)], axis=0)
    scatter = jnp.where((lane < NB) == (place < CAP), chosen, 0.0)[:, 0 : 4 * NB]
    payload[...] = dot(scatter.astype(bf16), back).reshape(SOIL, 8, WIDE)
    tail_lane = iota((2 * SOIL, 128), 1)
    tail_row = iota((2 * SOIL, 128), 0)
    tail_pick = ones_where(tail_lane == (tail_row & (SOIL - 1)) * 8 + CAP + (tail_row >> 4))
    tails_out[...] = dot(tail_pick, rows.astype(bf16))


def match_shares(all_named, id_column, share, share_t, own):
    me = lax.axis_index("soil")
    mine = iota((SOIL, BODIES), 0) == me
    named = jnp.sum(jnp.where(mine, all_named, 0.0), axis=0, keepdims=True)
    hits = ones_where(id_column == iota((ENT, BODIES), 1).astype(f32))
    hits_two = jnp.concatenate([hits, hits], axis=0)
    common = jnp.where(mine, 0.0, all_named * named)
    earlier = ones_where(iota((BODIES, BODIES), 0) < iota((BODIES, BODIES), 1))
    slots = jnp.where(common > 0, dot(common.astype(bf16), earlier) + 1.0, 0.0).astype(bf16)
    rank_t = dot_rows(hits, slots).astype(bf16)
    lane_start = iota((SOIL, ROWS), 0) * SHARED
    lanes = iota((SOIL, ROWS), 1)
    spread_lanes = ones_where((lanes >= lane_start) & (lanes < lane_start + SHARED))
    lane_rank = ((iota((ENT, ROWS), 1) & (SHARED - 1)) + 1).astype(f32)
    share_t[...] = ones_where(dot(rank_t, spread_lanes) == lane_rank)
    rank_two = dot_rows(slots, hits_two).astype(bf16)
    row_start = iota((ROWS, SOIL), 1) * SHARED
    row = iota((ROWS, SOIL), 0)
    spread_rows = ones_where((row >= row_start) & (row < row_start + SHARED))
    row_rank = ((iota((ROWS, 128), 0) & (SHARED - 1)) + 1).astype(f32)
    share[...] = ones_where(dot(spread_rows, rank_two) == row_rank)
    own[...] = dot_rows(hits, hits_two).astype(bf16)


def project_cone(normal, tangent_one, tangent_two, friction):
    tangent_size = jnp.sqrt(tangent_one * tangent_one + tangent_two * tangent_two)
    inside = tangent_size <= friction * normal
    polar_side = friction * tangent_size <= -normal
    middle = jnp.logical_not(jnp.logical_or(inside, polar_side))
    safe_size = jnp.where(middle, tangent_size, 1.0)
    new_normal = (friction * tangent_size + normal) / (1.0 + friction * friction)
    shrink = friction * new_normal / safe_size
    out_normal = jnp.where(inside, normal, jnp.where(polar_side, 0.0, new_normal))
    factor = jnp.where(inside, 1.0, jnp.where(polar_side, 0.0, shrink))
    return out_normal, tangent_one * factor, tangent_two * factor


def step_kernel(
    weight,
    is_first,
    is_last,
    arrived,
    pick,
    pick_t,
    tiles,
    flipped,
    current,
    advance,
    right_side,
    friction,
    *rest,
):
    copy = None
    if is_first:
        tails, slot_column, id_column, matrix_far = rest[0:4]
        payload, new_current, new_advance, new_forces, mass_rows = rest[4:9]
        share, share_t, own, matrix = rest[9:13]
        spread, picked, sem = rest[13:]
        copy = pltpu.make_async_copy(matrix_far, matrix, sem)
        copy.start()
        tire_all = tails[0:SOIL]
        match_shares(tails[SOIL:, 0:BODIES], id_column[:, 0:1], share, share_t, own)
        rows = arrived[...].reshape(128, WIDE)
        lane = iota((ENT, 128), 1).astype(f32)
        slot = slot_column[:, 0:1]
        wanted = dot(ones_where(lane == slot), rows.astype(bf16))
        for_mass = ones_where(lane == slot + CAP)
        mass_rows[...] = dot(
            jnp.concatenate([for_mass] * 3, axis=1), split_terms(rows, 3)
        )
    else:
        forces_in, mass_rows, share, share_t, own, matrix = rest[0:6]
        outputs, (spread, picked) = rest[6:-2], rest[-2:]
        tail = arrived[:, SHARED:SEND, :].astype(f32).reshape(8 * SOIL, WIDE).astype(bf16)
        tail_lane = iota((SOIL, 8 * SOIL), 1)
        tail_row = iota((SOIL, 8 * SOIL), 0)
        tire_all = dot(ones_where(tail_lane == tail_row * 8), tail)
        received = arrived[:, 0:SHARED, :].reshape(ROWS, WIDE)
        sums = dot(share_t[...], received) + dot(own[...], split_terms(forces_in[...], 2))
        wanted = sums * mass_rows[...]
    pieces = pull(wanted.astype(bf16), pick_t[...], flipped)

    device = iota((SOIL, WIDE), 0)
    for peer in range(SOIL):
        spread[:, WIDE * peer : WIDE * peer + WIDE] = jnp.where(
            device == peer, tire_all, 0.0
        ).astype(bf16)
    if copy is not None:
        copy.wait()
    tire = jnp.sum(dot(spread[...], matrix[...]), axis=0, keepdims=True)

    row = iota((CB, 128), 0)
    moved = []
    for piece in range(3):
        line = jnp.broadcast_to(tire[:, 128 * piece : 128 * piece + 128], (CB, 128))
        added = jnp.where(
            row == 0, both(line, False), jnp.where(row == 8, both(line, True), 0.0)
        )
        gradient = pieces[piece] + added + right_side[piece]
        moved.append(advance[piece] - step_size * gradient)
    updated = project_cone(*moved, friction[...])
    change = [updated[piece] - current[piece] for piece in range(3)]
    if is_last:
        impulses, doubles, squares = outputs
        low = lanes_low((8, 128))
        for piece in range(3):
            merged = jnp.where(low, updated[piece][0:8], updated[piece][8:16])
            for t in range(8):
                impulses[piece : piece + 1, 128 * t : 128 * t + 128] = merged[t : t + 1]
        doubles[...] = twice(*updated)
        total = change[0] * change[0] + change[1] * change[1] + change[2] * change[2]
        total = jnp.where(lanes_low((CB, 128)), total, 0.0)
        total = jnp.sum(jnp.sum(total, axis=1, keepdims=True), axis=0, keepdims=True)
        squares[...] = jnp.broadcast_to(total.reshape(1, 1, 1), squares.shape)
        return
    if not is_first:
        payload, new_current, new_advance, new_forces = outputs
    ahead = [updated[piece] + weight * change[piece] for piece in range(3)]
    for piece in range(3):
        new_current[piece] = updated[piece]
        new_advance[piece] = ahead[piece]
    picked[...] = dot(pick[...], twice(*ahead)).astype(bf16)
    push(picked, tiles, new_forces)
    shares = dot(share[...], split_terms(new_forces[...], 2)).astype(bf16)
    payload[:, 0:SHARED, :] = shares.reshape(SOIL, SHARED, WIDE)
    tail_out = jnp.where(iota((8, WIDE), 0) == 0, tire_row(*ahead), 0.0).astype(bf16)
    for peer in range(SOIL):
        payload[peer, SHARED:SEND] = tail_out


def last_push_kernel(doubles, pick, tiles_far, forces, tiles, sems):
    copies = [
        pltpu.make_async_copy(
            tiles_far.at[pl.ds(16 * g, 16)], tiles.at[pl.ds(16 * g, 16)], sems.at[g]
        )
        for g in range(4)
    ]
    for copy in copies:
        copy.start()
    picked = dot(pick[...], doubles[...]).astype(bf16)
    mask = entry_mask()
    for group in range(4):
        copies[group].wait()
        part = slice(16 * group, 16 * group + 16)
        spread = jnp.concatenate([picked[part]] * 8, axis=1) * mask
        forces[part] = dot(spread, tiles[part].reshape(16 * TALL, WIDE))


def outgoing_kernel(forces, owner_pick, labels, across, payload):
    rows = dot(owner_pick[...], split_terms(forces[...], 3))
    payload[:, :, 0:WIDE] = rows.reshape(SOIL, 8, WIDE)
    squares = jnp.sum(across[:, 0, :], axis=0, keepdims=True)
    extra = jnp.where(lanes_low((128, 128)), labels[...], squares)
    payload[:, :, WIDE:] = extra.reshape(SOIL, 8, 128)


def totals_kernel(scale, arrived, mass, velocity, norm):
    rows = arrived[:, :, 0:WIDE].reshape(128, WIDE)
    extra = arrived[:, :, WIDE:].reshape(128, 128)
    is_first = (iota((128, 128), 0) & 7) == 0
    squares = jnp.sum(jnp.where(is_first, extra, 0.0), axis=0, keepdims=True)[:, BLK : BLK + 1]
    norm[...] = jnp.sqrt(squares * scale + hold_eps) / step_size
    lane = (iota((128, 128), 1) + 1).astype(f32)
    is_force = (iota((128, 128), 0) & 7) < CAP
    chosen = jnp.where((extra == lane) & is_force, 1.0, 0.0)
    chosen = chosen.T[0:NB].astype(bf16)
    totals = dot(jnp.concatenate([chosen] * 3, axis=1), split_terms(rows, 3)) * mass[...]
    low = lanes_low((8, 128))
    for piece in range(3):
        tile = totals[:, 128 * piece : 128 * piece + 128]
        even, odd = tile[0:8], tile[8:16]
        for half, merged in enumerate(
            (
                jnp.where(low, even, pltpu.roll(odd, BLK, 1)),
                jnp.where(low, pltpu.roll(even, BLK, 1), odd),
            )
        ):
            component = 2 * piece + half
            for t in range(8):
                velocity[component : component + 1, 128 * t : 128 * t + 128] = merged[t : t + 1]


def step_scratch():
    return [pltpu.VMEM((SOIL, SOIL * 3 * TC), bf16), pltpu.VMEM((ENT, WIDE), bf16)]


def on_device(
    warm_start,
    right_side,
    friction,
    inverse_mass,
    jacobian,
    compliance,
    entry_block,
    entry_owner,
    entry_body,
    block_count,
):
    regions = lax.axis_size("grp")
    contacts = warm_start.shape[1]
    elements = 3 * contacts * SOIL * regions
    state = shape_of((3, CB, 128), f32)

    def line(array):
        return far(array.reshape(1, -1))

    (
        payload,
        tiles,
        flipped,
        pick,
        pick_t,
        id_column,
        slot_column,
        owner_pick,
        labels,
        warm,
        right,
        rough,
        mass_tiles,
    ) = pl.pallas_call(
        first_kernel,
        out_shape=(
            shape_of((SOIL, 8, WIDE + 128), f32),
            resident((ENT, TALL, WIDE), bf16),
            resident((ENT // 2, WIDE, 2 * TALL), bf16),
            shape_of((ENT, CB), bf16),
            shape_of((CB, 3 * ENT), bf16),
            shape_of((ENT, 128), f32),
            shape_of((ENT, 128), f32),
            shape_of((128, 3 * ENT), bf16),
            shape_of((128, 128), f32),
            state,
            state,
            shape_of((CB, 128), f32),
            shape_of((NB, WIDE), f32),
        ),
        in_specs=[SCALAR] + [IN_HBM] * 8,
        out_specs=(VECTOR,) * 13,
        scratch_shapes=[
            pltpu.VMEM((1, ENT), i32),
            pltpu.VMEM((1, ENT), i32),
            pltpu.VMEM((1, ENT), i32),
            pltpu.VMEM((3, contacts), f32),
            pltpu.VMEM((3, contacts), f32),
            pltpu.VMEM((1, contacts), f32),
            pltpu.VMEM((6, contacts), f32),
            pltpu.VMEM((ENT, WIDE), f32),
            pltpu.VMEM((ENT, WIDE), f32),
            pltpu.SemaphoreType.DMA((7,)),
            pltpu.SemaphoreType.DMA((ENT // 8,)),
        ],
        compiler_params=params(8),
        name="first",
    )(
        block_count,
        line(entry_owner),
        line(entry_body),
        line(entry_block),
        far(warm_start),
        far(right_side),
        line(friction),
        far(inverse_mass),
        far(jacobian),
    )
    arrived = lax.all_to_all(payload, "soil", 0, 0, tiled=True)
    payload, tails = pl.pallas_call(
        owner_kernel,
        out_shape=(shape_of((SOIL, 8, WIDE), f32), shape_of((2 * SOIL, WIDE), f32)),
        in_specs=[VECTOR] * 2,
        out_specs=(VECTOR,) * 2,
        compiler_params=params(6),
        name="owner",
    )(arrived, mass_tiles)

    weights = momentum_weights(ITERS)
    current = warm
    advance = warm
    for iteration in range(ITERS):
        arrived = lax.all_to_all(payload, "soil", 0, 0, tiled=True)
        is_first, is_last = iteration == 0, iteration == ITERS - 1
        if is_last:
            outs = [
                shape_of((3, contacts), f32),
                shape_of((CB, WIDE), bf16),
                shape_of((regions, 1, 128), f32),
            ]
        else:
            outs = [
                shape_of((SOIL, SEND, WIDE), bf16),
                state,
                state,
                shape_of((ENT, WIDE), f32),
            ]
        scratch = step_scratch()
        if is_first:
            outs += [
                shape_of((ENT, WIDE), f32),
                shape_of((ROWS, 128), bf16),
                shape_of((ENT, ROWS), bf16),
                shape_of((ENT, 128), bf16),
                resident(compliance.shape, bf16),
            ]
            more = [tails, slot_column, id_column, far(compliance)]
            more_specs = [VECTOR] * 3 + [IN_HBM]
            scratch.append(pltpu.SemaphoreType.DMA)
        else:
            more = [forces, *kept, keep(matrix)]
            more_specs = [VECTOR] * 6
        results = pl.pallas_call(
            functools.partial(step_kernel, weights[iteration], is_first, is_last),
            out_shape=tuple(outs),
            in_specs=[VECTOR] * 9 + more_specs,
            out_specs=(VECTOR,) * len(outs),
            scratch_shapes=scratch,
            compiler_params=params(12),
            name=f"step{iteration}",
        )(
            arrived,
            pick,
            pick_t,
            keep(tiles),
            keep(flipped),
            current,
            advance,
            right,
            rough,
            *more,
        )
        if is_last:
            impulses, doubles, squares = results
            break
        payload, current, advance, forces = results[:4]
        if is_first:
            kept, matrix = results[4:8], results[8]

    across = lax.all_to_all(squares, "grp", 0, 0, tiled=True)
    forces = pl.pallas_call(
        last_push_kernel,
        out_shape=shape_of((ENT, WIDE), f32),
        in_specs=[VECTOR, VECTOR, IN_HBM],
        out_specs=VECTOR,
        scratch_shapes=[
            pltpu.VMEM((ENT, TALL, WIDE), bf16),
            pltpu.SemaphoreType.DMA((4,)),
        ],
        compiler_params=params(14),
        cost_estimate=pl.CostEstimate(
            flops=10000000, bytes_accessed=10000000, transcendentals=0
        ),
        name="last_push",
    )(doubles, pick, far(jacobian))
    outgoing = pl.pallas_call(
        outgoing_kernel,
        out_shape=shape_of((SOIL, 8, WIDE + 128), f32),
        in_specs=[VECTOR] * 4,
        out_specs=VECTOR,
        compiler_params=params(6),
        name="outgoing",
    )(forces, owner_pick, labels, across)
    arrived = lax.all_to_all(outgoing, "soil", 0, 0, tiled=True)
    velocity, norm = pl.pallas_call(
        functools.partial(totals_kernel, 1.0 / elements),
        out_shape=(shape_of((6, contacts), f32), shape_of((1, 1), f32)),
        in_specs=[VECTOR] * 2,
        out_specs=(VECTOR, VECTOR),
        compiler_params=params(4),
        name="totals",
    )(arrived, mass_tiles)
    return (impulses, velocity, norm[0, 0])


def solution(mesh):
    placed = (
        P(None, ("grp", "soil")),
        P(None, ("grp", "soil")),
        P(("grp", "soil")),
        P(None, ("grp", "soil")),
        P(("grp", "soil"), None, None),
        P(None, "soil"),
        P(("grp", "soil")),
        P(("grp", "soil")),
        P(("grp", "soil")),
        P(("grp", "soil")),
    )
    return jax.shard_map(
        on_device,
        mesh=mesh,
        in_specs=placed,
        out_specs=(P(None, ("grp", "soil")), P(None, ("grp", "soil")), P()),
        check_vma=False,
    )
```

```python
import functools
import math

import jax
import jax.numpy as jnp
from jax import lax
from jax.experimental import pallas as pl
from jax.experimental.pallas import tpu as pltpu
from jax.sharding import PartitionSpec as P

BLK = 64
CB = 16
NB = 16
TC = 128
CAP = 4
ITERS = 3
ENT = 64
SOIL = 16
BODIES = SOIL * NB
WIDE = 6 * BLK
TALL = 3 * BLK
SHARED = 32
ROWS = SOIL * SHARED
FORCE_ROWS = 3 * ENT
SEND_FIRST = FORCE_ROWS + 3 * NB + 8
SHARE_ROWS = 3 * SHARED
SEND_SECOND = SHARE_ROWS + 16
SEND_THIRD = SHARE_ROWS + 8

step_size = 0.1
hold_eps = 1e-06

bf16, f32, i32 = jnp.bfloat16, jnp.float32, jnp.int32

IN_HBM = pl.BlockSpec(memory_space=pltpu.HBM)
VECTOR = pl.BlockSpec(memory_space=pltpu.VMEM)
SCALAR = pl.BlockSpec(memory_space=pltpu.SMEM)


def momentum_weights(number):
    nesterov = 1.0
    weights = []
    for iteration in range(number):
        following = 0.5 * (-nesterov * nesterov + nesterov * math.sqrt(nesterov * nesterov + 4.0))
        weights.append(nesterov * (1.0 - nesterov) / (nesterov * nesterov + following))
        nesterov = following
    return weights


def resident(shape, dtype):
    return pltpu.VMEM(shape, dtype)


def keep(array):
    return pltpu.with_memory_space_constraint(array, pltpu.VMEM)


def far(array):
    return pltpu.with_memory_space_constraint(array, pltpu.HBM)


def shape_of(shape, dtype):
    return jax.ShapeDtypeStruct(shape, dtype)


def params(megabytes):
    return pltpu.CompilerParams(vmem_limit_bytes=megabytes << 20)


def iota(shape, dim):
    return lax.broadcasted_iota(i32, shape, dim)


def ones_where(mask):
    return jnp.where(mask, 1.0, 0.0).astype(bf16)


def dot(left, right):
    return jnp.dot(left, right, preferred_element_type=f32)


def dot_rows(left, right):
    return lax.dot_general(left, right, (((1,), (1,)), ((), ())), preferred_element_type=f32)


def planes(values):
    return [values[:, 128 * c : 128 * c + 128] for c in range(3)]


def side_by_side(rows, size):
    return jnp.concatenate([rows[size * c : size * c + size] for c in range(3)], axis=1)


def split_terms(values, terms):
    parts = []
    for _ in range(terms):
        part = values.astype(bf16)
        parts.append(part)
        values = values - part.astype(f32)
    return jnp.concatenate(parts, axis=0)


def order(block):
    return ((block & 1) << 3) + (block >> 1)


def lanes_low(shape):
    return iota(shape, len(shape) - 1) < BLK


def both(values, upper):
    low = lanes_low(values.shape)
    turned = pltpu.roll(values, BLK, 1)
    return jnp.where(low, turned, values) if upper else jnp.where(low, values, turned)


def lane_tiles(ref, row):
    return jnp.concatenate([ref[row : row + 1, 128 * t : 128 * t + 128] for t in range(8)], axis=0)


def doubled(ref, row):
    tiles = lane_tiles(ref, row)
    return jnp.concatenate([both(tiles, False), both(tiles, True)], axis=0)


def twice(normal, first, second):
    low = lanes_low((CB, 2 * BLK))
    return jnp.concatenate(
        [
            jnp.where(low, normal, first),
            jnp.where(low, second, normal),
            jnp.where(low, first, second),
        ],
        axis=1,
    ).astype(bf16)


def entry_mask():
    column = iota((16, 16 * TALL), 1)
    first = iota((16, 16 * TALL), 0) * TALL
    return ones_where((column >= first) & (column < first + TALL))


def push(picked, tiles, forces):
    mask = entry_mask()

    def group(number):
        rows = picked[pl.ds(16 * number, 16)]
        spread = jnp.concatenate([rows] * 8, axis=1) * mask
        weights = tiles[pl.ds(16 * number, 16)].reshape(16 * TALL, WIDE)
        forces[pl.ds(16 * number, 16)] = dot(spread, weights)

    def step(number, carry):
        group(number)
        group(number + 2)
        return carry

    lax.fori_loop(0, 2, step, 0)


def pull(wanted, pick_t, flipped):
    row = iota((16, WIDE), 0)
    lower, upper = [], []
    for part in range(2):
        sides = []
        for half in range(2):
            start = 32 * half + 16 * part
            rows = wanted[start : start + 16]
            sides.append(
                jnp.concatenate(
                    [rows * ones_where(row == pair) for pair in range(16)], axis=1
                )
            )
        weights = flipped[16 * part : 16 * part + 16].reshape(16 * WIDE, WIDE)
        terms = dot(jnp.concatenate(sides, axis=0), weights)
        lower.append(terms[0:16])
        upper.append(terms[16:32])
    terms = jnp.concatenate(lower + upper, axis=0)
    wrong = (iota((ENT, WIDE), 0) < ENT // 2) == (iota((ENT, WIDE), 1) >= TALL)
    sums = dot(pick_t, split_terms(jnp.where(wrong, 0.0, terms), 3))
    left, middle, right = sums[:, 0:128], sums[:, 128:256], sums[:, 256:384]
    return (
        both(left, False) + both(middle, True),
        both(left, True) + both(right, False),
        both(middle, False) + both(right, True),
    )


def tire_row(normal, first, second):
    low = lanes_low((1, 128))
    return jnp.concatenate(
        [jnp.where(low, part[0:1], part[8:9]) for part in (normal, first, second)], axis=1
    )


def eye(size):
    return ones_where(iota((size, size), 0) == iota((size, size), 1))


def first_kernel(
    count,
    owner_far,
    body_far,
    block_far,
    warm_far,
    right_far,
    rough_far,
    mass_far,
    tiles_far,
    payload,
    tiles,
    flipped,
    pick_out,
    pick_t_out,
    id_out,
    slot_out,
    slot_row,
    warm_out,
    right_out,
    rough_out,
    mass_out,
    owner,
    body,
    block,
    warm,
    right,
    rough,
    mass,
    picked,
    forces,
    sems,
    tile_sems,
):
    small = [
        pltpu.make_async_copy(source, target, sems.at[n])
        for n, (source, target) in enumerate(
            [
                (block_far, block),
                (warm_far, warm),
                (owner_far, owner),
                (body_far, body),
                (mass_far, mass),
                (right_far, right),
                (rough_far, rough),
            ]
        )
    ]
    copies = []
    for start in (0, 32, 8, 40, 16, 48, 24, 56):
        part = pl.ds(start, 8)
        copies.append(
            pltpu.make_async_copy(tiles_far.at[part], tiles.at[part], tile_sems.at[start // 8])
        )
    for copy in small + copies:
        copy.start()
    for copy in small:
        copy.wait()
    live = iota((1, ENT), 1) < count[0]
    pick_t = ones_where((iota((CB, ENT), 0) == order(block[...])) & live)
    pick = dot_rows(eye(ENT), pick_t).astype(bf16)
    pick_out[...] = pick
    pick_t_out[...] = jnp.concatenate([pick_t] * 3, axis=1)
    advance = [doubled(warm, piece) for piece in range(3)]
    picked[...] = dot(pick, twice(*advance))
    def tile_part(part):
        copies[2 * part].wait()
        copies[2 * part + 1].wait()

        for number in range(8):
            near, away = 8 * part + number, 32 + 8 * part + number
            above, below = tiles[near], tiles[away]
            flipped[near] = jnp.concatenate([above, below], axis=0).T
            for entry, tile in ((near, above), (away, below)):
                line = picked[entry : entry + 1, 0:TALL].astype(bf16)
                forces[entry : entry + 1] = dot(line, tile)

    tile_part(0)
    for piece in range(3):
        warm_out[piece] = advance[piece]
        right_out[piece] = doubled(right, piece)
    rough_out[...] = doubled(rough, 0)
    low = lanes_low((8, 128))
    lanes = []
    for piece in range(3):
        even, odd = lane_tiles(mass, 2 * piece), lane_tiles(mass, 2 * piece + 1)
        lanes.append(
            jnp.concatenate(
                [
                    jnp.where(low, even, pltpu.roll(odd, BLK, 1)),
                    jnp.where(low, pltpu.roll(even, BLK, 1), odd),
                ],
                axis=0,
            )
        )
    mass_tiles = jnp.concatenate(lanes, axis=1)
    mass_out[...] = mass_tiles
    ids = jnp.where(live, owner[...] * NB + order(body[...]), -1)
    hits_t = ones_where(iota((BODIES, ENT), 0) == ids)
    counts = dot_rows(jnp.ones((8, ENT), bf16), hits_t)
    named = jnp.where(counts > 0, 1.0, 0.0)

    owner_row = jnp.where(live, owner[...], -1)
    owner_hit = ones_where(iota((SOIL, ENT), 0) == owner_row)
    earlier = ones_where(iota((ENT, ENT), 0) < iota((ENT, ENT), 1))
    rank = jnp.sum(dot(owner_hit, earlier) * owner_hit.astype(f32), axis=0, keepdims=True)
    slot = jnp.where(live, (owner_row * 16).astype(f32) + rank, -100.0)
    slot_row[...] = jnp.broadcast_to(slot, (8, ENT))
    slot_four = jnp.where(live, (owner_row * CAP).astype(f32) + rank, -100.0)
    chosen_four = ones_where(iota((ENT, ENT), 0).astype(f32) == slot_four)
    label = jnp.where(live, order(body[...]) + 1, 0).astype(bf16)
    label_row = dot_rows(jnp.broadcast_to(label, (8, ENT)), chosen_four)
    id_row = jnp.broadcast_to((ids + 1).astype(f32), (8, ENT))
    label_row = jnp.concatenate([label_row, label_row], axis=1)
    id_row = jnp.concatenate([id_row, id_row], axis=1)
    place = iota((8, 128), 0)
    tail = jnp.zeros((8, 128), f32)
    for number, line in enumerate(
        planes(tire_row(*advance)) + [id_row, named[:, 0:128], named[:, 128:256], label_row]
    ):
        tail = jnp.where(place == number, line, tail)
    tail = tail.astype(bf16)
    mass_high = mass_tiles.astype(bf16)
    for peer in range(SOIL):
        for c, plane in enumerate(planes(mass_high)):
            payload[peer, FORCE_ROWS + NB * c : FORCE_ROWS + NB * c + NB] = plane
        payload[peer, FORCE_ROWS + 3 * NB :] = tail
    for_columns = jnp.concatenate(
        [
            jnp.broadcast_to(slot, (8, ENT)),
            jnp.broadcast_to(ids.astype(f32), (8, ENT)),
        ],
        axis=0,
    )
    columns = dot_rows(eye(ENT), for_columns.astype(bf16))
    slot_out[...] = jnp.broadcast_to(columns[:, 0:1], (ENT, 128))
    id_out[...] = jnp.broadcast_to(columns[:, 8:9], (ENT, 128))

    for part in range(1, 4):
        tile_part(part)
    sent = planes(forces[...].astype(bf16))
    for peer in range(SOIL):
        for c in range(3):
            payload[peer, ENT * c : ENT * c + ENT] = sent[c]


def slot_hits(me, slot_labels):
    column = iota((128, 128), 1)
    row = iota((128, 128), 0)
    mine = ones_where((row == me * CAP + (column >> 4)) & (column < CAP * NB))
    labels = dot(slot_labels.astype(bf16), mine)
    hits = ones_where(labels == ((iota((SOIL, 128), 1) & 15) + 1).astype(f32))
    peer = ones_where((iota((16 * SOIL, SOIL), 0) >> 4) == iota((16 * SOIL, SOIL), 1))
    return dot(peer, hits)


def mass_slots(rows):
    place = iota((16 * SOIL, 128), 0) & 15
    slot = iota((16 * SOIL, 128), 1) >> 4
    low = lanes_low((16 * SOIL, 128))
    shifted = slot - jnp.where(low, 0, CAP)
    first = jnp.where(shifted + jnp.where(low, 3, 3 + CAP) == place, both(rows, False), 0.0)
    second = jnp.where((slot + 3 + 2 * CAP == place) & low, rows, 0.0)
    return jnp.concatenate([first, second], axis=1).astype(bf16)


def owner_slots(rows, gather):
    place = iota((16 * SOIL, 128), 0) & 15
    slot = iota((16 * SOIL, 128), 1) >> 4
    fold = ones_where((iota((NB, 128), 1) & 15) == iota((NB, 128), 0))
    for c in range(3):
        chosen = jnp.where((slot + CAP * c == place) & (slot < CAP), rows, 0.0).astype(bf16)
        gather[NB * c : NB * c + NB] = dot_rows(fold, chosen).astype(bf16)


def match_shares(me, all_named, id_column, share, share_t, own):
    mine = iota((SOIL, BODIES), 0) == me
    named = jnp.sum(jnp.where(mine, all_named, 0.0), axis=0, keepdims=True)
    hits = ones_where(id_column == iota((ENT, BODIES), 1).astype(f32))
    hits_two = jnp.concatenate([hits, hits], axis=0)
    common = jnp.where(mine, 0.0, all_named * named)
    earlier = ones_where(iota((BODIES, BODIES), 0) < iota((BODIES, BODIES), 1))
    slots = jnp.where(common > 0, dot(common.astype(bf16), earlier) + 1.0, 0.0).astype(bf16)
    rank_t = dot_rows(hits, slots).astype(bf16)
    lane_start = iota((SOIL, ROWS), 0) * SHARED
    lanes = iota((SOIL, ROWS), 1)
    spread_lanes = ones_where((lanes >= lane_start) & (lanes < lane_start + SHARED))
    lane_rank = ((iota((ENT, ROWS), 1) & (SHARED - 1)) + 1).astype(f32)
    share_t[...] = ones_where(dot(rank_t, spread_lanes) == lane_rank)
    rank_two = dot_rows(slots, hits_two).astype(bf16)
    row_start = iota((ROWS, SOIL), 1) * SHARED
    row = iota((ROWS, SOIL), 0)
    spread_rows = ones_where((row >= row_start) & (row < row_start + SHARED))
    row_rank = ((iota((ROWS, 128), 0) & (SHARED - 1)) + 1).astype(f32)
    share[...] = ones_where(dot(spread_rows, rank_two) == row_rank)
    own[...] = dot_rows(hits, hits_two).astype(bf16)


def project_cone(normal, tangent_one, tangent_two, friction):
    tangent_size = jnp.sqrt(tangent_one * tangent_one + tangent_two * tangent_two)
    inside = tangent_size <= friction * normal
    polar_side = friction * tangent_size <= -normal
    middle = jnp.logical_not(jnp.logical_or(inside, polar_side))
    safe_size = jnp.where(middle, tangent_size, 1.0)
    new_normal = (friction * tangent_size + normal) / (1.0 + friction * friction)
    shrink = friction * new_normal / safe_size
    out_normal = jnp.where(inside, normal, jnp.where(polar_side, 0.0, new_normal))
    factor = jnp.where(inside, 1.0, jnp.where(polar_side, 0.0, shrink))
    return out_normal, tangent_one * factor, tangent_two * factor


def step_kernel(
    weight,
    is_first,
    is_last,
    arrived,
    pick,
    pick_t,
    tiles,
    flipped,
    current,
    advance,
    right_side,
    friction,
    *rest,
):
    copy = None
    if is_first:
        id_column, mass_in, matrix_far = rest[0:3]
        payload, new_current, new_advance, new_forces, mass_rows = rest[3:8]
        share, share_t, own, matrix, slot_labels = rest[8:13]
        spread, picked, sem = rest[13:]
        copy = pltpu.make_async_copy(matrix_far, matrix, sem)
        copy.start()
        me = lax.axis_index("soil")
        mine = id_column[:, 0:1]
        tail = arrived[:, FORCE_ROWS + 3 * NB :, :].astype(f32)
        tail = tail.reshape(8 * SOIL, 128).astype(bf16)
        tail_lane = iota((7 * SOIL, 8 * SOIL), 1)
        tail_row = iota((7 * SOIL, 8 * SOIL), 0)
        tails = dot(
            ones_where(tail_lane == (tail_row & (SOIL - 1)) * 8 + (tail_row >> 4)), tail
        )
        tire_all = side_by_side(tails, SOIL)
        names = tails[3 * SOIL : 4 * SOIL]
        all_named = jnp.concatenate(
            [tails[4 * SOIL : 5 * SOIL], tails[5 * SOIL : 6 * SOIL]], axis=1
        )
        low_lanes = lanes_low((1, 128))
        own_name = jnp.where(mine >= 0, mine + 1.0, -1.0)
        match = jnp.concatenate(
            [
                ones_where(
                    own_name
                    == jnp.where(
                        low_lanes, names[2 * t : 2 * t + 1], names[2 * t + 1 : 2 * t + 2]
                    )
                )
                for t in range(SOIL // 2)
            ],
            axis=1,
        )
        name_pick = ones_where(mine == iota((ENT, BODIES), 1).astype(f32))
        found, sums = [], []
        for c in range(3):
            start = FORCE_ROWS + NB * c
            found.append(dot(name_pick, arrived[:, start : start + NB, :].reshape(BODIES, 128)))
            plane = arrived[:, ENT * c : ENT * c + ENT, :].reshape(SOIL * ENT, 128)
            sums.append(dot(match, plane))
        mass_high = jnp.concatenate(found, axis=1)
        mass_rows[...] = mass_high
        wanted = jnp.concatenate(sums, axis=1) * mass_high
        match_shares(me, all_named, mine, share, share_t, own)
        slot_labels[...] = tails[6 * SOIL : 7 * SOIL]
        tail_pick = mass_slots(slot_hits(me, tails[6 * SOIL : 7 * SOIL]))
        mass_low = (mass_in[...] - mass_in[...].astype(bf16).astype(f32)).astype(bf16)
        tail_rows = dot(
            tail_pick,
            jnp.concatenate(
                [plane for plane in planes(mass_low) for _ in range(CAP)]
                + [jnp.zeros((CAP * NB, 128), bf16)],
                axis=0,
            ),
        )
    else:
        forces_in, mass_in, share, share_t, own, matrix = rest[0:6]
        if is_last:
            outputs, (spread, picked) = rest[6:-2], rest[-2:]
        else:
            slot_column, outputs, (spread, picked) = rest[6], rest[7:-2], rest[-2:]
        size = 8 if is_last else 16
        tail = arrived[:, SHARE_ROWS:, :].astype(f32).reshape(size * SOIL, 128).astype(bf16)
        tail_lane = iota((3 * SOIL, size * SOIL), 1)
        tail_row = iota((3 * SOIL, size * SOIL), 0)
        tire_all = side_by_side(
            dot(
                ones_where(tail_lane == (tail_row & (SOIL - 1)) * size + (tail_row >> 4)), tail
            ),
            SOIL,
        )
        received = [
            arrived[:, SHARED * c : SHARED * c + SHARED, :].reshape(ROWS, 128) for c in range(3)
        ]
        sums = jnp.concatenate([dot(share_t[...], plane) for plane in received], axis=1)
        sums += dot(own[...], split_terms(forces_in[...], 2))
        mass_all = mass_in[...]
        if not is_last:
            lane = iota((ENT, 16 * SOIL), 1).astype(f32)
            first = slot_column[:, 0:1] + 3.0
            chosen = [ones_where(lane == first + float(CAP * c)) for c in range(3)]
            mass_all += side_by_side(dot(jnp.concatenate(chosen, axis=0), tail), ENT)
        wanted = sums * mass_all
    pieces = pull(wanted.astype(bf16), pick_t[...], flipped)

    device = iota((SOIL, WIDE), 0)
    for peer in range(SOIL):
        spread[:, WIDE * peer : WIDE * peer + WIDE] = jnp.where(
            device == peer, tire_all, 0.0
        ).astype(bf16)
    if copy is not None:
        copy.wait()
    tire = jnp.sum(dot(spread[...], matrix[...]), axis=0, keepdims=True)

    row = iota((CB, 128), 0)
    moved = []
    for piece in range(3):
        line = jnp.broadcast_to(tire[:, 128 * piece : 128 * piece + 128], (CB, 128))
        added = jnp.where(
            row == 0, both(line, False), jnp.where(row == 8, both(line, True), 0.0)
        )
        gradient = pieces[piece] + added + right_side[piece]
        moved.append(advance[piece] - step_size * gradient)
    updated = project_cone(*moved, friction[...])
    change = [updated[piece] - current[piece] for piece in range(3)]
    if is_last:
        impulses, doubles, squares = outputs
        low = lanes_low((8, 128))
        for piece in range(3):
            merged = jnp.where(low, updated[piece][0:8], updated[piece][8:16])
            for t in range(8):
                impulses[piece : piece + 1, 128 * t : 128 * t + 128] = merged[t : t + 1]
        doubles[...] = twice(*updated)
        total = change[0] * change[0] + change[1] * change[1] + change[2] * change[2]
        total = jnp.where(lanes_low((CB, 128)), total, 0.0)
        total = jnp.sum(jnp.sum(total, axis=1, keepdims=True), axis=0, keepdims=True)
        squares[...] = jnp.broadcast_to(total.reshape(1, 1, 1), squares.shape)
        return
    if not is_first:
        payload, new_current, new_advance, new_forces, mass_rows = outputs
        mass_rows[...] = mass_all
    ahead = [updated[piece] + weight * change[piece] for piece in range(3)]
    for piece in range(3):
        new_current[piece] = updated[piece]
        new_advance[piece] = ahead[piece]
    picked[...] = dot(pick[...], twice(*ahead)).astype(bf16)
    push(picked, tiles, new_forces)
    shares = dot(share[...], split_terms(new_forces[...], 2)).astype(bf16)
    for c, plane in enumerate(planes(shares)):
        payload[:, SHARED * c : SHARED * c + SHARED, :] = plane.reshape(SOIL, SHARED, 128)
    size = 16 if is_first else 8
    place = iota((size * SOIL, 128), 0) & (size - 1)
    tail_out = tail_rows if is_first else jnp.zeros((size * SOIL, 128), f32)
    for c, line in enumerate(planes(tire_row(*ahead))):
        tail_out = jnp.where(place == c, line, tail_out)
    payload[:, SHARE_ROWS:, :] = tail_out.reshape(SOIL, size, 128).astype(bf16)


def last_push_kernel(
    doubles, pick, slot_row, slot_labels, tiles_far, forces, owner_pick, gather, tiles, sems
):
    copies = [
        pltpu.make_async_copy(
            tiles_far.at[pl.ds(16 * g, 16)], tiles.at[pl.ds(16 * g, 16)], sems.at[g]
        )
        for g in range(4)
    ]
    for copy in copies:
        copy.start()
    picked = dot(pick[...], doubles[...]).astype(bf16)
    mask = entry_mask()
    for group in range(4):
        copies[group].wait()
        part = slice(16 * group, 16 * group + 16)
        spread = jnp.concatenate([picked[part]] * 8, axis=1) * mask
        forces[part] = dot(spread, tiles[part].reshape(16 * TALL, WIDE))
        if group == 0:
            line = iota((16 * SOIL, ENT), 0).astype(f32)
            chosen = [ones_where(line == slot_row[0:1] + float(CAP * c)) for c in range(3)]
            owner_pick[...] = jnp.concatenate([part for part in chosen for _ in range(3)], axis=1)
        if group == 1:
            owner_slots(slot_hits(lax.axis_index("soil"), slot_labels[...]), gather)


def outgoing_kernel(forces, owner_pick, across, payload):
    terms = [split_terms(plane, 3) for plane in planes(forces[...])]
    rows = dot(owner_pick[...], jnp.concatenate(terms, axis=0))
    squares = jnp.sum(across[:, 0, :], axis=0, keepdims=True)[:, 0:1]
    place = iota((16 * SOIL, 128), 0) & 15
    payload[...] = jnp.where(place == 3 * CAP, squares, rows).reshape(SOIL, 16, 128)


def totals_kernel(scale, arrived, gather, mass, velocity, norm):
    rows = arrived[...].reshape(16 * SOIL, 128)
    is_square = (iota((16 * SOIL, 128), 0) & 15) == 3 * CAP
    squares = jnp.sum(jnp.where(is_square, rows, 0.0), axis=0, keepdims=True)
    norm[...] = jnp.sqrt(squares[:, 0:1] * scale + hold_eps) / step_size
    totals = dot(jnp.concatenate([gather[...]] * 3, axis=1), split_terms(rows, 3))
    totals = side_by_side(totals, NB) * mass[...]
    low = lanes_low((8, 128))
    for piece in range(3):
        tile = totals[:, 128 * piece : 128 * piece + 128]
        even, odd = tile[0:8], tile[8:16]
        for half, merged in enumerate(
            (
                jnp.where(low, even, pltpu.roll(odd, BLK, 1)),
                jnp.where(low, pltpu.roll(even, BLK, 1), odd),
            )
        ):
            component = 2 * piece + half
            for t in range(8):
                velocity[component : component + 1, 128 * t : 128 * t + 128] = merged[t : t + 1]


def step_scratch():
    return [pltpu.VMEM((SOIL, SOIL * 3 * TC), bf16), pltpu.VMEM((ENT, WIDE), bf16)]


def on_device(
    warm_start,
    right_side,
    friction,
    inverse_mass,
    jacobian,
    compliance,
    entry_block,
    entry_owner,
    entry_body,
    block_count,
):
    regions = lax.axis_size("grp")
    contacts = warm_start.shape[1]
    elements = 3 * contacts * SOIL * regions
    state = shape_of((3, CB, 128), f32)

    def line(array):
        return far(array.reshape(1, -1))

    (
        payload,
        tiles,
        flipped,
        pick,
        pick_t,
        id_column,
        slot_column,
        slot_row,
        warm,
        right,
        rough,
        mass_tiles,
    ) = pl.pallas_call(
        first_kernel,
        out_shape=(
            shape_of((SOIL, SEND_FIRST, 128), bf16),
            resident((ENT, TALL, WIDE), bf16),
            resident((ENT // 2, WIDE, 2 * TALL), bf16),
            shape_of((ENT, CB), bf16),
            shape_of((CB, 3 * ENT), bf16),
            shape_of((ENT, 128), f32),
            shape_of((ENT, 128), f32),
            shape_of((8, ENT), f32),
            state,
            state,
            shape_of((CB, 128), f32),
            shape_of((NB, WIDE), f32),
        ),
        in_specs=[SCALAR] + [IN_HBM] * 8,
        out_specs=(VECTOR,) * 12,
        scratch_shapes=[
            pltpu.VMEM((1, ENT), i32),
            pltpu.VMEM((1, ENT), i32),
            pltpu.VMEM((1, ENT), i32),
            pltpu.VMEM((3, contacts), f32),
            pltpu.VMEM((3, contacts), f32),
            pltpu.VMEM((1, contacts), f32),
            pltpu.VMEM((6, contacts), f32),
            pltpu.VMEM((ENT, WIDE), f32),
            pltpu.VMEM((ENT, WIDE), f32),
            pltpu.SemaphoreType.DMA((7,)),
            pltpu.SemaphoreType.DMA((ENT // 8,)),
        ],
        compiler_params=params(8),
        name="first",
    )(
        block_count,
        line(entry_owner),
        line(entry_body),
        line(entry_block),
        far(warm_start),
        far(right_side),
        line(friction),
        far(inverse_mass),
        far(jacobian),
    )
    weights = momentum_weights(ITERS)
    current = warm
    advance = warm
    for iteration in range(ITERS):
        arrived = lax.all_to_all(payload, "soil", 0, 0, tiled=True)
        is_first, is_last = iteration == 0, iteration == ITERS - 1
        if is_last:
            outs = [
                shape_of((3, contacts), f32),
                shape_of((CB, WIDE), bf16),
                shape_of((regions, 1, 128), f32),
            ]
        else:
            outs = [
                shape_of((SOIL, SEND_SECOND if is_first else SEND_THIRD, 128), bf16),
                state,
                state,
                shape_of((ENT, WIDE), f32),
                shape_of((ENT, WIDE), f32),
            ]
        scratch = step_scratch()
        if is_first:
            outs += [
                shape_of((ROWS, 128), bf16),
                shape_of((ENT, ROWS), bf16),
                shape_of((ENT, 128), bf16),
                resident(compliance.shape, bf16),
                shape_of((SOIL, 128), f32),
            ]
            more = [id_column, mass_tiles, far(compliance)]
            more_specs = [VECTOR] * 2 + [IN_HBM]
            scratch.append(pltpu.SemaphoreType.DMA)
        else:
            more = [forces, mass_rows, *kept, keep(matrix)]
            if not is_last:
                more.append(slot_column)
            more_specs = [VECTOR] * len(more)
        results = pl.pallas_call(
            functools.partial(step_kernel, weights[iteration], is_first, is_last),
            out_shape=tuple(outs),
            in_specs=[VECTOR] * 9 + more_specs,
            out_specs=(VECTOR,) * len(outs),
            scratch_shapes=scratch,
            compiler_params=params(12),
            name=f"step{iteration}",
        )(
            arrived,
            pick,
            pick_t,
            keep(tiles),
            keep(flipped),
            current,
            advance,
            right,
            rough,
            *more,
        )
        if is_last:
            impulses, doubles, squares = results
            break
        payload, current, advance, forces, mass_rows = results[:5]
        if is_first:
            kept, matrix, slot_labels = results[5:8], results[8], results[9]

    across = lax.all_to_all(squares, "grp", 0, 0, tiled=True)
    forces, owner_pick, gather = pl.pallas_call(
        last_push_kernel,
        out_shape=(
            shape_of((ENT, WIDE), f32),
            shape_of((16 * SOIL, 9 * ENT), bf16),
            shape_of((3 * NB, 16 * SOIL), bf16),
        ),
        in_specs=[VECTOR] * 4 + [IN_HBM],
        out_specs=(VECTOR,) * 3,
        scratch_shapes=[
            pltpu.VMEM((ENT, TALL, WIDE), bf16),
            pltpu.SemaphoreType.DMA((4,)),
        ],
        compiler_params=params(14),
        cost_estimate=pl.CostEstimate(
            flops=10000000, bytes_accessed=10000000, transcendentals=0
        ),
        name="last_push",
    )(doubles, pick, slot_row, slot_labels, far(jacobian))
    outgoing = pl.pallas_call(
        outgoing_kernel,
        out_shape=shape_of((SOIL, 16, 128), f32),
        in_specs=[VECTOR] * 3,
        out_specs=VECTOR,
        compiler_params=params(6),
        name="outgoing",
    )(forces, owner_pick, across)
    arrived = lax.all_to_all(outgoing, "soil", 0, 0, tiled=True)
    velocity, norm = pl.pallas_call(
        functools.partial(totals_kernel, 1.0 / elements),
        out_shape=(shape_of((6, contacts), f32), shape_of((1, 1), f32)),
        in_specs=[VECTOR] * 3,
        out_specs=(VECTOR, VECTOR),
        compiler_params=params(4),
        name="totals",
    )(arrived, gather, mass_tiles)
    return (impulses, velocity, norm[0, 0])


def solution(mesh):
    placed = (
        P(None, ("grp", "soil")),
        P(None, ("grp", "soil")),
        P(("grp", "soil")),
        P(None, ("grp", "soil")),
        P(("grp", "soil"), None, None),
        P(None, "soil"),
        P(("grp", "soil")),
        P(("grp", "soil")),
        P(("grp", "soil")),
        P(("grp", "soil")),
    )
    return jax.shard_map(
        on_device,
        mesh=mesh,
        in_specs=placed,
        out_specs=(P(None, ("grp", "soil")), P(None, ("grp", "soil")), P()),
        check_vma=False,
    )
```

```python
import functools
import math

import jax
import jax.numpy as jnp
from jax import lax
from jax.experimental import pallas as pl
from jax.experimental.pallas import tpu as pltpu
from jax.sharding import PartitionSpec as P

BLK = 64
CB = 16
NB = 16
TC = 128
CAP = 4
ITERS = 3
ENT = 64
SOIL = 16
BODIES = SOIL * NB
WIDE = 6 * BLK
TALL = 3 * BLK
SHARED = 32
ROWS = SOIL * SHARED
FORCE_ROWS = 3 * ENT
SEND_FIRST = FORCE_ROWS + 3 * NB + 8
SHARE_ROWS = 3 * SHARED
SEND_SECOND = SHARE_ROWS + 16
SEND_THIRD = SHARE_ROWS + 8

step_size = 0.1
hold_eps = 1e-06

bf16, f32, i32 = jnp.bfloat16, jnp.float32, jnp.int32

IN_HBM = pl.BlockSpec(memory_space=pltpu.HBM)
VECTOR = pl.BlockSpec(memory_space=pltpu.VMEM)
SCALAR = pl.BlockSpec(memory_space=pltpu.SMEM)


def momentum_weights(number):
    nesterov = 1.0
    weights = []
    for iteration in range(number):
        following = 0.5 * (-nesterov * nesterov + nesterov * math.sqrt(nesterov * nesterov + 4.0))
        weights.append(nesterov * (1.0 - nesterov) / (nesterov * nesterov + following))
        nesterov = following
    return weights


def resident(shape, dtype):
    return pltpu.VMEM(shape, dtype)


def keep(array):
    return pltpu.with_memory_space_constraint(array, pltpu.VMEM)


def far(array):
    return pltpu.with_memory_space_constraint(array, pltpu.HBM)


def shape_of(shape, dtype):
    return jax.ShapeDtypeStruct(shape, dtype)


def params(megabytes):
    return pltpu.CompilerParams(vmem_limit_bytes=megabytes << 20)


def iota(shape, dim):
    return lax.broadcasted_iota(i32, shape, dim)


def ones_where(mask):
    return jnp.where(mask, 1.0, 0.0).astype(bf16)


def dot(left, right):
    return jnp.dot(left, right, preferred_element_type=f32)


def dot_rows(left, right):
    return lax.dot_general(left, right, (((1,), (1,)), ((), ())), preferred_element_type=f32)


def planes(values):
    return [values[:, 128 * c : 128 * c + 128] for c in range(3)]


def side_by_side(rows, size):
    return jnp.concatenate([rows[size * c : size * c + size] for c in range(3)], axis=1)


def split_terms(values, terms):
    parts = []
    for _ in range(terms):
        part = values.astype(bf16)
        parts.append(part)
        values = values - part.astype(f32)
    return jnp.concatenate(parts, axis=0)


def order(block):
    return ((block & 1) << 3) + (block >> 1)


def lanes_low(shape):
    return iota(shape, len(shape) - 1) < BLK


def both(values, upper):
    low = lanes_low(values.shape)
    turned = pltpu.roll(values, BLK, 1)
    return jnp.where(low, turned, values) if upper else jnp.where(low, values, turned)


def lane_tiles(ref, row):
    return jnp.concatenate([ref[row : row + 1, 128 * t : 128 * t + 128] for t in range(8)], axis=0)


def doubled(ref, row):
    tiles = lane_tiles(ref, row)
    return jnp.concatenate([both(tiles, False), both(tiles, True)], axis=0)


def twice(normal, first, second):
    low = lanes_low((CB, 2 * BLK))
    return jnp.concatenate(
        [
            jnp.where(low, normal, first),
            jnp.where(low, second, normal),
            jnp.where(low, first, second),
        ],
        axis=1,
    ).astype(bf16)


def entry_mask():
    column = iota((16, 16 * TALL), 1)
    first = iota((16, 16 * TALL), 0) * TALL
    return ones_where((column >= first) & (column < first + TALL))


def push(picked, tiles, forces):
    mask = entry_mask()

    def group(number):
        rows = picked[pl.ds(16 * number, 16)]
        spread = jnp.concatenate([rows] * 8, axis=1) * mask
        weights = tiles[pl.ds(16 * number, 16)].reshape(16 * TALL, WIDE)
        forces[pl.ds(16 * number, 16)] = dot(spread, weights)

    def step(number, carry):
        group(number)
        group(number + 2)
        return carry

    lax.fori_loop(0, 2, step, 0)


def pull(wanted, pick_t, flipped):
    row = iota((16, WIDE), 0)
    lower, upper = [], []
    for part in range(2):
        sides = []
        for half in range(2):
            start = 32 * half + 16 * part
            rows = wanted[start : start + 16]
            sides.append(
                jnp.concatenate(
                    [rows * ones_where(row == pair) for pair in range(16)], axis=1
                )
            )
        weights = flipped[16 * part : 16 * part + 16].reshape(16 * WIDE, WIDE)
        terms = dot(jnp.concatenate(sides, axis=0), weights)
        lower.append(terms[0:16])
        upper.append(terms[16:32])
    terms = jnp.concatenate(lower + upper, axis=0)
    wrong = (iota((ENT, WIDE), 0) < ENT // 2) == (iota((ENT, WIDE), 1) >= TALL)
    sums = dot(pick_t, split_terms(jnp.where(wrong, 0.0, terms), 3))
    left, middle, right = sums[:, 0:128], sums[:, 128:256], sums[:, 256:384]
    return (
        both(left, False) + both(middle, True),
        both(left, True) + both(right, False),
        both(middle, False) + both(right, True),
    )


def tire_row(normal, first, second):
    low = lanes_low((1, 128))
    return jnp.concatenate(
        [jnp.where(low, part[0:1], part[8:9]) for part in (normal, first, second)], axis=1
    )


def eye(size):
    return ones_where(iota((size, size), 0) == iota((size, size), 1))


def first_kernel(
    count,
    owner_far,
    body_far,
    block_far,
    warm_far,
    right_far,
    rough_far,
    mass_far,
    tiles_far,
    payload,
    tiles,
    flipped,
    pick_out,
    pick_t_out,
    id_out,
    slot_out,
    slot_row,
    warm_out,
    right_out,
    rough_out,
    mass_out,
    owner,
    body,
    block,
    warm,
    right,
    rough,
    mass,
    picked,
    forces,
    sems,
    tile_sems,
):
    small = [
        pltpu.make_async_copy(source, target, sems.at[n])
        for n, (source, target) in enumerate(
            [
                (block_far, block),
                (warm_far, warm),
                (owner_far, owner),
                (body_far, body),
                (mass_far, mass),
                (right_far, right),
                (rough_far, rough),
            ]
        )
    ]
    copies = []
    for start in (0, 32, 8, 40, 16, 48, 24, 56):
        part = pl.ds(start, 8)
        copies.append(
            pltpu.make_async_copy(tiles_far.at[part], tiles.at[part], tile_sems.at[start // 8])
        )
    for copy in small + copies[0 : 2 * 2]:
        copy.start()
    for copy in small[0:2]:
        copy.wait()
    live = iota((1, ENT), 1) < count[0]
    pick_t = ones_where((iota((CB, ENT), 0) == order(block[...])) & live)
    pick = dot_rows(eye(ENT), pick_t).astype(bf16)
    pick_out[...] = pick
    pick_t_out[...] = jnp.concatenate([pick_t] * 3, axis=1)
    advance = [doubled(warm, piece) for piece in range(3)]
    picked[...] = dot(pick, twice(*advance))

    def tile_part(part):
        copies[2 * part].wait()
        copies[2 * part + 1].wait()
        for copy in copies[2 * (part + 2) : 2 * (part + 2) + 2]:
            copy.start()
        for number in range(8):
            near, away = 8 * part + number, 32 + 8 * part + number
            above, below = tiles[near], tiles[away]
            flipped[near] = jnp.concatenate([above, below], axis=0).T
            for entry, tile in ((near, above), (away, below)):
                line = picked[entry : entry + 1, 0:TALL].astype(bf16)
                forces[entry : entry + 1] = dot(line, tile)

    for copy in small[2:]:
        copy.wait()
    tile_part(0)
    for piece in range(3):
        warm_out[piece] = advance[piece]
        right_out[piece] = doubled(right, piece)
    rough_out[...] = doubled(rough, 0)
    low = lanes_low((8, 128))
    lanes = []
    for piece in range(3):
        even, odd = lane_tiles(mass, 2 * piece), lane_tiles(mass, 2 * piece + 1)
        lanes.append(
            jnp.concatenate(
                [
                    jnp.where(low, even, pltpu.roll(odd, BLK, 1)),
                    jnp.where(low, pltpu.roll(even, BLK, 1), odd),
                ],
                axis=0,
            )
        )
    mass_tiles = jnp.concatenate(lanes, axis=1)
    mass_out[...] = mass_tiles
    ids = jnp.where(live, owner[...] * NB + order(body[...]), -1)
    hits_t = ones_where(iota((BODIES, ENT), 0) == ids)
    counts = dot_rows(jnp.ones((8, ENT), bf16), hits_t)
    named = jnp.where(counts > 0, 1.0, 0.0)

    owner_row = jnp.where(live, owner[...], -1)
    owner_hit = ones_where(iota((SOIL, ENT), 0) == owner_row)
    earlier = ones_where(iota((ENT, ENT), 0) < iota((ENT, ENT), 1))
    rank = jnp.sum(dot(owner_hit, earlier) * owner_hit.astype(f32), axis=0, keepdims=True)
    tile_part(1)
    slot = jnp.where(live, (owner_row * 16).astype(f32) + rank, -100.0)
    slot_row[...] = jnp.broadcast_to(slot, (8, ENT))
    slot_four = jnp.where(live, (owner_row * CAP).astype(f32) + rank, -100.0)
    chosen_four = ones_where(iota((ENT, ENT), 0).astype(f32) == slot_four)
    label = jnp.where(live, order(body[...]) + 1, 0).astype(bf16)
    label_row = dot_rows(jnp.broadcast_to(label, (8, ENT)), chosen_four)
    id_row = jnp.broadcast_to((ids + 1).astype(f32), (8, ENT))
    label_row = jnp.concatenate([label_row, label_row], axis=1)
    id_row = jnp.concatenate([id_row, id_row], axis=1)
    tile_part(2)
    place = iota((8, 128), 0)
    tail = jnp.zeros((8, 128), f32)
    for number, line in enumerate(
        planes(tire_row(*advance)) + [id_row, named[:, 0:128], named[:, 128:256], label_row]
    ):
        tail = jnp.where(place == number, line, tail)
    tail = tail.astype(bf16)
    mass_high = mass_tiles.astype(bf16)
    for peer in range(SOIL):
        for c, plane in enumerate(planes(mass_high)):
            payload[peer, FORCE_ROWS + NB * c : FORCE_ROWS + NB * c + NB] = plane
        payload[peer, FORCE_ROWS + 3 * NB :] = tail
    for_columns = jnp.concatenate(
        [
            jnp.broadcast_to(slot, (8, ENT)),
            jnp.broadcast_to(ids.astype(f32), (8, ENT)),
        ],
        axis=0,
    )
    columns = dot_rows(eye(ENT), for_columns.astype(bf16))
    slot_out[...] = jnp.broadcast_to(columns[:, 0:1], (ENT, 128))
    id_out[...] = jnp.broadcast_to(columns[:, 8:9], (ENT, 128))

    tile_part(3)
    sent = planes(forces[...].astype(bf16))
    for peer in range(SOIL):
        for c in range(3):
            payload[peer, ENT * c : ENT * c + ENT] = sent[c]


def slot_hits(me, slot_labels):
    column = iota((128, 128), 1)
    row = iota((128, 128), 0)
    mine = ones_where((row == me * CAP + (column >> 4)) & (column < CAP * NB))
    labels = dot(slot_labels.astype(bf16), mine)
    hits = ones_where(labels == ((iota((SOIL, 128), 1) & 15) + 1).astype(f32))
    peer = ones_where((iota((16 * SOIL, SOIL), 0) >> 4) == iota((16 * SOIL, SOIL), 1))
    return dot(peer, hits)


def mass_slots(rows):
    place = iota((16 * SOIL, 128), 0) & 15
    slot = iota((16 * SOIL, 128), 1) >> 4
    low = lanes_low((16 * SOIL, 128))
    shifted = slot - jnp.where(low, 0, CAP)
    first = jnp.where(shifted + jnp.where(low, 3, 3 + CAP) == place, both(rows, False), 0.0)
    second = jnp.where((slot + 3 + 2 * CAP == place) & low, rows, 0.0)
    return jnp.concatenate([first, second], axis=1).astype(bf16)


def owner_slots(rows, gather):
    place = iota((16 * SOIL, 128), 0) & 15
    slot = iota((16 * SOIL, 128), 1) >> 4
    fold = ones_where((iota((NB, 128), 1) & 15) == iota((NB, 128), 0))
    for c in range(3):
        chosen = jnp.where((slot + CAP * c == place) & (slot < CAP), rows, 0.0).astype(bf16)
        gather[NB * c : NB * c + NB] = dot_rows(fold, chosen).astype(bf16)


def match_shares(me, all_named, id_column, share, share_t, own):
    mine = iota((SOIL, BODIES), 0) == me
    named = jnp.sum(jnp.where(mine, all_named, 0.0), axis=0, keepdims=True)
    hits = ones_where(id_column == iota((ENT, BODIES), 1).astype(f32))
    hits_two = jnp.concatenate([hits, hits], axis=0)
    common = jnp.where(mine, 0.0, all_named * named)
    earlier = ones_where(iota((BODIES, BODIES), 0) < iota((BODIES, BODIES), 1))
    slots = jnp.where(common > 0, dot(common.astype(bf16), earlier) + 1.0, 0.0).astype(bf16)
    rank_t = dot_rows(hits, slots).astype(bf16)
    lane_start = iota((SOIL, ROWS), 0) * SHARED
    lanes = iota((SOIL, ROWS), 1)
    spread_lanes = ones_where((lanes >= lane_start) & (lanes < lane_start + SHARED))
    lane_rank = ((iota((ENT, ROWS), 1) & (SHARED - 1)) + 1).astype(f32)
    share_t[...] = ones_where(dot(rank_t, spread_lanes) == lane_rank)
    rank_two = dot_rows(slots, hits_two)
    order_row = (iota((SHARED, 128), 0) + 1).astype(f32)
    for peer in range(SOIL):
        line = jnp.broadcast_to(rank_two[peer : peer + 1], (SHARED, 128))
        share[SHARED * peer : SHARED * peer + SHARED] = ones_where(line == order_row)
    own[...] = dot_rows(hits, hits_two).astype(bf16)


def project_cone(normal, tangent_one, tangent_two, friction):
    tangent_size = jnp.sqrt(tangent_one * tangent_one + tangent_two * tangent_two)
    inside = tangent_size <= friction * normal
    polar_side = friction * tangent_size <= -normal
    middle = jnp.logical_not(jnp.logical_or(inside, polar_side))
    safe_size = jnp.where(middle, tangent_size, 1.0)
    new_normal = (friction * tangent_size + normal) / (1.0 + friction * friction)
    shrink = friction * new_normal / safe_size
    out_normal = jnp.where(inside, normal, jnp.where(polar_side, 0.0, new_normal))
    factor = jnp.where(inside, 1.0, jnp.where(polar_side, 0.0, shrink))
    return out_normal, tangent_one * factor, tangent_two * factor


def step_kernel(
    weight,
    is_first,
    is_last,
    arrived,
    pick,
    pick_t,
    tiles,
    flipped,
    current,
    advance,
    right_side,
    friction,
    *rest,
):
    copy = None
    if is_first:
        id_column, mass_in, matrix_far = rest[0:3]
        payload, new_current, new_advance, new_forces, mass_rows = rest[3:8]
        share, share_t, own, matrix, slot_labels = rest[8:13]
        spread, picked, sem = rest[13:]
        copy = pltpu.make_async_copy(matrix_far, matrix, sem)
        copy.start()
        me = lax.axis_index("soil")
        mine = id_column[:, 0:1]
        tail = arrived[:, FORCE_ROWS + 3 * NB :, :].astype(f32)
        tail = tail.reshape(8 * SOIL, 128).astype(bf16)
        tail_lane = iota((7 * SOIL, 8 * SOIL), 1)
        tail_row = iota((7 * SOIL, 8 * SOIL), 0)
        tails = dot(
            ones_where(tail_lane == (tail_row & (SOIL - 1)) * 8 + (tail_row >> 4)), tail
        )
        tire_all = side_by_side(tails, SOIL)
        names = tails[3 * SOIL : 4 * SOIL]
        all_named = jnp.concatenate(
            [tails[4 * SOIL : 5 * SOIL], tails[5 * SOIL : 6 * SOIL]], axis=1
        )
        low_lanes = lanes_low((1, 128))
        own_name = jnp.where(mine >= 0, mine + 1.0, -1.0)
        match = jnp.concatenate(
            [
                ones_where(
                    own_name
                    == jnp.where(
                        low_lanes, names[2 * t : 2 * t + 1], names[2 * t + 1 : 2 * t + 2]
                    )
                )
                for t in range(SOIL // 2)
            ],
            axis=1,
        )
        name_pick = ones_where(mine == iota((ENT, BODIES), 1).astype(f32))
        found, sums = [], []
        for c in range(3):
            start = FORCE_ROWS + NB * c
            found.append(dot(name_pick, arrived[:, start : start + NB, :].reshape(BODIES, 128)))
            plane = arrived[:, ENT * c : ENT * c + ENT, :].reshape(SOIL * ENT, 128)
            sums.append(dot(match, plane))
        mass_high = jnp.concatenate(found, axis=1)
        mass_rows[...] = mass_high
        wanted = jnp.concatenate(sums, axis=1) * mass_high
        match_shares(me, all_named, mine, share, share_t, own)
        slot_labels[...] = tails[6 * SOIL : 7 * SOIL]
        tail_pick = mass_slots(slot_hits(me, tails[6 * SOIL : 7 * SOIL]))
        mass_low = (mass_in[...] - mass_in[...].astype(bf16).astype(f32)).astype(bf16)
        tail_rows = dot(
            tail_pick,
            jnp.concatenate(
                [plane for plane in planes(mass_low) for _ in range(CAP)]
                + [jnp.zeros((CAP * NB, 128), bf16)],
                axis=0,
            ),
        )
    else:
        forces_in, mass_in, share, share_t, own, matrix = rest[0:6]
        if is_last:
            outputs, (spread, picked) = rest[6:-2], rest[-2:]
        else:
            slot_column, outputs, (spread, picked) = rest[6], rest[7:-2], rest[-2:]
        size = 8 if is_last else 16
        tail = arrived[:, SHARE_ROWS:, :].astype(f32).reshape(size * SOIL, 128).astype(bf16)
        tail_lane = iota((3 * SOIL, size * SOIL), 1)
        tail_row = iota((3 * SOIL, size * SOIL), 0)
        tire_all = side_by_side(
            dot(
                ones_where(tail_lane == (tail_row & (SOIL - 1)) * size + (tail_row >> 4)), tail
            ),
            SOIL,
        )
        received = [
            arrived[:, SHARED * c : SHARED * c + SHARED, :].reshape(ROWS, 128) for c in range(3)
        ]
        sums = jnp.concatenate([dot(share_t[...], plane) for plane in received], axis=1)
        sums += dot(own[...], split_terms(forces_in[...], 2))
        mass_all = mass_in[...]
        if not is_last:
            lane = iota((ENT, 16 * SOIL), 1).astype(f32)
            first = slot_column[:, 0:1] + 3.0
            chosen = [ones_where(lane == first + float(CAP * c)) for c in range(3)]
            mass_all += side_by_side(dot(jnp.concatenate(chosen, axis=0), tail), ENT)
        wanted = sums * mass_all
    pieces = pull(wanted.astype(bf16), pick_t[...], flipped)

    device = iota((SOIL, WIDE), 0)
    for peer in range(SOIL):
        spread[:, WIDE * peer : WIDE * peer + WIDE] = jnp.where(
            device == peer, tire_all, 0.0
        ).astype(bf16)
    if copy is not None:
        copy.wait()
    tire = jnp.sum(dot(spread[...], matrix[...]), axis=0, keepdims=True)

    row = iota((CB, 128), 0)
    moved = []
    for piece in range(3):
        line = jnp.broadcast_to(tire[:, 128 * piece : 128 * piece + 128], (CB, 128))
        added = jnp.where(
            row == 0, both(line, False), jnp.where(row == 8, both(line, True), 0.0)
        )
        gradient = pieces[piece] + added + right_side[piece]
        moved.append(advance[piece] - step_size * gradient)
    updated = project_cone(*moved, friction[...])
    change = [updated[piece] - current[piece] for piece in range(3)]
    if is_last:
        impulses, doubles, squares = outputs
        low = lanes_low((8, 128))
        for piece in range(3):
            merged = jnp.where(low, updated[piece][0:8], updated[piece][8:16])
            for t in range(8):
                impulses[piece : piece + 1, 128 * t : 128 * t + 128] = merged[t : t + 1]
        doubles[...] = twice(*updated)
        total = change[0] * change[0] + change[1] * change[1] + change[2] * change[2]
        total = jnp.where(lanes_low((CB, 128)), total, 0.0)
        total = jnp.sum(jnp.sum(total, axis=1, keepdims=True), axis=0, keepdims=True)
        squares[...] = jnp.broadcast_to(total.reshape(1, 1, 1), squares.shape)
        return
    if not is_first:
        payload, new_current, new_advance, new_forces, mass_rows = outputs
        mass_rows[...] = mass_all
    ahead = [updated[piece] + weight * change[piece] for piece in range(3)]
    for piece in range(3):
        new_current[piece] = updated[piece]
        new_advance[piece] = ahead[piece]
    picked[...] = dot(pick[...], twice(*ahead)).astype(bf16)
    push(picked, tiles, new_forces)
    shares = dot(share[...], split_terms(new_forces[...], 2)).astype(bf16)
    for c, plane in enumerate(planes(shares)):
        payload[:, SHARED * c : SHARED * c + SHARED, :] = plane.reshape(SOIL, SHARED, 128)
    size = 16 if is_first else 8
    place = iota((size * SOIL, 128), 0) & (size - 1)
    tail_out = tail_rows if is_first else jnp.zeros((size * SOIL, 128), f32)
    for c, line in enumerate(planes(tire_row(*ahead))):
        tail_out = jnp.where(place == c, line, tail_out)
    payload[:, SHARE_ROWS:, :] = tail_out.reshape(SOIL, size, 128).astype(bf16)


def last_push_kernel(
    doubles, pick, slot_row, slot_labels, tiles_far, forces, owner_pick, gather, tiles, sems
):
    copies = [
        pltpu.make_async_copy(
            tiles_far.at[pl.ds(16 * g, 16)], tiles.at[pl.ds(16 * g, 16)], sems.at[g]
        )
        for g in range(4)
    ]
    for copy in copies:
        copy.start()
    picked = dot(pick[...], doubles[...]).astype(bf16)
    mask = entry_mask()
    for group in range(4):
        copies[group].wait()
        part = slice(16 * group, 16 * group + 16)
        spread = jnp.concatenate([picked[part]] * 8, axis=1) * mask
        forces[part] = dot(spread, tiles[part].reshape(16 * TALL, WIDE))
        if group == 0:
            line = iota((16 * SOIL, ENT), 0).astype(f32)
            chosen = [ones_where(line == slot_row[0:1] + float(CAP * c)) for c in range(3)]
            owner_pick[...] = jnp.concatenate([part for part in chosen for _ in range(3)], axis=1)
        if group == 1:
            owner_slots(slot_hits(lax.axis_index("soil"), slot_labels[...]), gather)


def outgoing_kernel(forces, owner_pick, across, payload):
    terms = [split_terms(plane, 3) for plane in planes(forces[...])]
    rows = dot(owner_pick[...], jnp.concatenate(terms, axis=0))
    squares = jnp.sum(across[:, 0, :], axis=0, keepdims=True)[:, 0:1]
    place = iota((16 * SOIL, 128), 0) & 15
    payload[...] = jnp.where(place == 3 * CAP, squares, rows).reshape(SOIL, 16, 128)


def totals_kernel(scale, arrived, gather, mass, velocity, norm):
    rows = arrived[...].reshape(16 * SOIL, 128)
    is_square = (iota((16 * SOIL, 128), 0) & 15) == 3 * CAP
    squares = jnp.sum(jnp.where(is_square, rows, 0.0), axis=0, keepdims=True)
    norm[...] = jnp.sqrt(squares[:, 0:1] * scale + hold_eps) / step_size
    totals = dot(jnp.concatenate([gather[...]] * 3, axis=1), split_terms(rows, 3))
    totals = side_by_side(totals, NB) * mass[...]
    low = lanes_low((8, 128))
    for piece in range(3):
        tile = totals[:, 128 * piece : 128 * piece + 128]
        even, odd = tile[0:8], tile[8:16]
        for half, merged in enumerate(
            (
                jnp.where(low, even, pltpu.roll(odd, BLK, 1)),
                jnp.where(low, pltpu.roll(even, BLK, 1), odd),
            )
        ):
            component = 2 * piece + half
            for t in range(8):
                velocity[component : component + 1, 128 * t : 128 * t + 128] = merged[t : t + 1]


def step_scratch():
    return [pltpu.VMEM((SOIL, SOIL * 3 * TC), bf16), pltpu.VMEM((ENT, WIDE), bf16)]


def on_device(
    warm_start,
    right_side,
    friction,
    inverse_mass,
    jacobian,
    compliance,
    entry_block,
    entry_owner,
    entry_body,
    block_count,
):
    regions = lax.axis_size("grp")
    contacts = warm_start.shape[1]
    elements = 3 * contacts * SOIL * regions
    state = shape_of((3, CB, 128), f32)

    def line(array):
        return far(array.reshape(1, -1))

    (
        payload,
        tiles,
        flipped,
        pick,
        pick_t,
        id_column,
        slot_column,
        slot_row,
        warm,
        right,
        rough,
        mass_tiles,
    ) = pl.pallas_call(
        first_kernel,
        out_shape=(
            shape_of((SOIL, SEND_FIRST, 128), bf16),
            resident((ENT, TALL, WIDE), bf16),
            resident((ENT // 2, WIDE, 2 * TALL), bf16),
            shape_of((ENT, CB), bf16),
            shape_of((CB, 3 * ENT), bf16),
            shape_of((ENT, 128), f32),
            shape_of((ENT, 128), f32),
            shape_of((8, ENT), f32),
            state,
            state,
            shape_of((CB, 128), f32),
            shape_of((NB, WIDE), f32),
        ),
        in_specs=[SCALAR] + [IN_HBM] * 8,
        out_specs=(VECTOR,) * 12,
        scratch_shapes=[
            pltpu.VMEM((1, ENT), i32),
            pltpu.VMEM((1, ENT), i32),
            pltpu.VMEM((1, ENT), i32),
            pltpu.VMEM((3, contacts), f32),
            pltpu.VMEM((3, contacts), f32),
            pltpu.VMEM((1, contacts), f32),
            pltpu.VMEM((6, contacts), f32),
            pltpu.VMEM((ENT, WIDE), f32),
            pltpu.VMEM((ENT, WIDE), f32),
            pltpu.SemaphoreType.DMA((7,)),
            pltpu.SemaphoreType.DMA((ENT // 8,)),
        ],
        compiler_params=params(8),
        name="first",
    )(
        block_count,
        line(entry_owner),
        line(entry_body),
        line(entry_block),
        far(warm_start),
        far(right_side),
        line(friction),
        far(inverse_mass),
        far(jacobian),
    )
    weights = momentum_weights(ITERS)
    current = warm
    advance = warm
    for iteration in range(ITERS):
        arrived = lax.all_to_all(payload, "soil", 0, 0, tiled=True)
        is_first, is_last = iteration == 0, iteration == ITERS - 1
        if is_last:
            outs = [
                shape_of((3, contacts), f32),
                shape_of((CB, WIDE), bf16),
                shape_of((regions, 1, 128), f32),
            ]
        else:
            outs = [
                shape_of((SOIL, SEND_SECOND if is_first else SEND_THIRD, 128), bf16),
                state,
                state,
                shape_of((ENT, WIDE), f32),
                shape_of((ENT, WIDE), f32),
            ]
        scratch = step_scratch()
        if is_first:
            outs += [
                shape_of((ROWS, 128), bf16),
                shape_of((ENT, ROWS), bf16),
                shape_of((ENT, 128), bf16),
                resident(compliance.shape, bf16),
                shape_of((SOIL, 128), f32),
            ]
            more = [id_column, mass_tiles, far(compliance)]
            more_specs = [VECTOR] * 2 + [IN_HBM]
            scratch.append(pltpu.SemaphoreType.DMA)
        else:
            more = [forces, mass_rows, *kept, keep(matrix)]
            if not is_last:
                more.append(slot_column)
            more_specs = [VECTOR] * len(more)
        results = pl.pallas_call(
            functools.partial(step_kernel, weights[iteration], is_first, is_last),
            out_shape=tuple(outs),
            in_specs=[VECTOR] * 9 + more_specs,
            out_specs=(VECTOR,) * len(outs),
            scratch_shapes=scratch,
            compiler_params=params(12),
            name=f"step{iteration}",
        )(
            arrived,
            pick,
            pick_t,
            keep(tiles),
            keep(flipped),
            current,
            advance,
            right,
            rough,
            *more,
        )
        if is_last:
            impulses, doubles, squares = results
            break
        payload, current, advance, forces, mass_rows = results[:5]
        if is_first:
            kept, matrix, slot_labels = results[5:8], results[8], results[9]

    across = lax.all_to_all(squares, "grp", 0, 0, tiled=True)
    forces, owner_pick, gather = pl.pallas_call(
        last_push_kernel,
        out_shape=(
            shape_of((ENT, WIDE), f32),
            shape_of((16 * SOIL, 9 * ENT), bf16),
            shape_of((3 * NB, 16 * SOIL), bf16),
        ),
        in_specs=[VECTOR] * 4 + [IN_HBM],
        out_specs=(VECTOR,) * 3,
        scratch_shapes=[
            pltpu.VMEM((ENT, TALL, WIDE), bf16),
            pltpu.SemaphoreType.DMA((4,)),
        ],
        compiler_params=params(14),
        cost_estimate=pl.CostEstimate(
            flops=10000000, bytes_accessed=10000000, transcendentals=0
        ),
        name="last_push",
    )(doubles, pick, slot_row, slot_labels, far(jacobian))
    outgoing = pl.pallas_call(
        outgoing_kernel,
        out_shape=shape_of((SOIL, 16, 128), f32),
        in_specs=[VECTOR] * 3,
        out_specs=VECTOR,
        compiler_params=params(6),
        name="outgoing",
    )(forces, owner_pick, across)
    arrived = lax.all_to_all(outgoing, "soil", 0, 0, tiled=True)
    velocity, norm = pl.pallas_call(
        functools.partial(totals_kernel, 1.0 / elements),
        out_shape=(shape_of((6, contacts), f32), shape_of((1, 1), f32)),
        in_specs=[VECTOR] * 3,
        out_specs=(VECTOR, VECTOR),
        compiler_params=params(4),
        name="totals",
    )(arrived, gather, mass_tiles)
    return (impulses, velocity, norm[0, 0])


def solution(mesh):
    placed = (
        P(None, ("grp", "soil")),
        P(None, ("grp", "soil")),
        P(("grp", "soil")),
        P(None, ("grp", "soil")),
        P(("grp", "soil"), None, None),
        P(None, "soil"),
        P(("grp", "soil")),
        P(("grp", "soil")),
        P(("grp", "soil")),
        P(("grp", "soil")),
    )
    return jax.shard_map(
        on_device,
        mesh=mesh,
        in_specs=placed,
        out_specs=(P(None, ("grp", "soil")), P(None, ("grp", "soil")), P()),
        check_vma=False,
    )
```

```python
import functools
import math

import jax
import jax.numpy as jnp
from jax import lax
from jax.experimental import pallas as pl
from jax.experimental.pallas import tpu as pltpu
from jax.sharding import PartitionSpec as P

BLK = 64
CB = 16
NB = 16
TC = 128
CAP = 4
ITERS = 3
ENT = 64
SOIL = 16
BODIES = SOIL * NB
WIDE = 6 * BLK
TALL = 3 * BLK
SHARED = 32
ROWS = SOIL * SHARED
FORCE_ROWS = 3 * ENT
SEND_FIRST = FORCE_ROWS + 3 * NB + 8
SHARE_ROWS = 3 * SHARED
SEND_SECOND = SHARE_ROWS + 16
SEND_THIRD = SHARE_ROWS + 8

step_size = 0.1
hold_eps = 1e-06

bf16, f32, i32 = jnp.bfloat16, jnp.float32, jnp.int32

IN_HBM = pl.BlockSpec(memory_space=pltpu.HBM)
VECTOR = pl.BlockSpec(memory_space=pltpu.VMEM)
SCALAR = pl.BlockSpec(memory_space=pltpu.SMEM)


def momentum_weights(number):
    nesterov = 1.0
    weights = []
    for iteration in range(number):
        following = 0.5 * (-nesterov * nesterov + nesterov * math.sqrt(nesterov * nesterov + 4.0))
        weights.append(nesterov * (1.0 - nesterov) / (nesterov * nesterov + following))
        nesterov = following
    return weights


def resident(shape, dtype):
    return pltpu.VMEM(shape, dtype)


def keep(array):
    return pltpu.with_memory_space_constraint(array, pltpu.VMEM)


def far(array):
    return pltpu.with_memory_space_constraint(array, pltpu.HBM)


def shape_of(shape, dtype):
    return jax.ShapeDtypeStruct(shape, dtype)


def params(megabytes):
    return pltpu.CompilerParams(vmem_limit_bytes=megabytes << 20)


def iota(shape, dim):
    return lax.broadcasted_iota(i32, shape, dim)


def ones_where(mask):
    return jnp.where(mask, 1.0, 0.0).astype(bf16)


def dot(left, right):
    return jnp.dot(left, right, preferred_element_type=f32)


def dot_rows(left, right):
    return lax.dot_general(left, right, (((1,), (1,)), ((), ())), preferred_element_type=f32)


def planes(values):
    return [values[:, 128 * c : 128 * c + 128] for c in range(3)]


def side_by_side(rows, size):
    return jnp.concatenate([rows[size * c : size * c + size] for c in range(3)], axis=1)


def split_terms(values, terms):
    parts = []
    for _ in range(terms):
        part = values.astype(bf16)
        parts.append(part)
        values = values - part.astype(f32)
    return jnp.concatenate(parts, axis=0)


def order(block):
    return ((block & 1) << 3) + (block >> 1)


def lanes_low(shape):
    return iota(shape, len(shape) - 1) < BLK


def both(values, upper):
    low = lanes_low(values.shape)
    turned = pltpu.roll(values, BLK, 1)
    return jnp.where(low, turned, values) if upper else jnp.where(low, values, turned)


def lane_tiles(ref, row):
    return jnp.concatenate([ref[row : row + 1, 128 * t : 128 * t + 128] for t in range(8)], axis=0)


def doubled(ref, row):
    tiles = lane_tiles(ref, row)
    return jnp.concatenate([both(tiles, False), both(tiles, True)], axis=0)


def twice(normal, first, second):
    low = lanes_low((CB, 2 * BLK))
    return jnp.concatenate(
        [
            jnp.where(low, normal, first),
            jnp.where(low, second, normal),
            jnp.where(low, first, second),
        ],
        axis=1,
    ).astype(bf16)


def entry_mask():
    column = iota((16, 16 * TALL), 1)
    first = iota((16, 16 * TALL), 0) * TALL
    return ones_where((column >= first) & (column < first + TALL))


def push(picked, tiles, forces):
    mask = entry_mask()

    def group(number):
        rows = picked[pl.ds(16 * number, 16)]
        spread = jnp.concatenate([rows] * 8, axis=1) * mask
        weights = tiles[pl.ds(16 * number, 16)].reshape(16 * TALL, WIDE)
        forces[pl.ds(16 * number, 16)] = dot(spread, weights)

    def step(number, carry):
        group(number)
        group(number + 2)
        return carry

    lax.fori_loop(0, 2, step, 0)


def pull(wanted, pick_t, flipped):
    row = iota((8, WIDE), 0)
    lower, upper = [], []
    for part in range(4):
        sides = []
        for half in range(2):
            start = 32 * half + 8 * part
            rows = wanted[start : start + 8]
            sides.append(
                jnp.concatenate(
                    [jnp.where(row == pair, rows, 0.0) for pair in range(8)], axis=1
                )
            )
        weights = flipped[8 * part : 8 * part + 8].reshape(8 * WIDE, WIDE)
        terms = dot(jnp.concatenate(sides, axis=0).astype(bf16), weights)
        lower.append(terms[0:8])
        upper.append(terms[8:16])
    terms = jnp.concatenate(lower + upper, axis=0)
    wrong = (iota((ENT, WIDE), 0) < ENT // 2) == (iota((ENT, WIDE), 1) >= TALL)
    sums = dot(pick_t, split_terms(jnp.where(wrong, 0.0, terms), 3))
    left, middle, right = sums[:, 0:128], sums[:, 128:256], sums[:, 256:384]
    return (
        both(left, False) + both(middle, True),
        both(left, True) + both(right, False),
        both(middle, False) + both(right, True),
    )


def tire_row(normal, first, second):
    low = lanes_low((1, 128))
    return jnp.concatenate(
        [jnp.where(low, part[0:1], part[8:9]) for part in (normal, first, second)], axis=1
    )


def eye(size):
    return ones_where(iota((size, size), 0) == iota((size, size), 1))


def first_kernel(
    count,
    owner_far,
    body_far,
    block_far,
    warm_far,
    right_far,
    rough_far,
    mass_far,
    tiles_far,
    payload,
    tiles,
    flipped,
    pick_out,
    pick_t_out,
    id_out,
    slot_out,
    slot_row,
    warm_out,
    right_out,
    rough_out,
    mass_out,
    owner,
    body,
    block,
    warm,
    right,
    rough,
    mass,
    picked,
    forces,
    sems,
    tile_sems,
):
    small = [
        pltpu.make_async_copy(source, target, sems.at[n])
        for n, (source, target) in enumerate(
            [
                (block_far, block),
                (warm_far, warm),
                (owner_far, owner),
                (body_far, body),
                (mass_far, mass),
                (right_far, right),
                (rough_far, rough),
            ]
        )
    ]
    copies = []
    for start in (0, 32, 8, 40, 16, 48, 24, 56):
        part = pl.ds(start, 8)
        copies.append(
            pltpu.make_async_copy(tiles_far.at[part], tiles.at[part], tile_sems.at[start // 8])
        )
    for copy in small + copies[0 : 2 * 2]:
        copy.start()
    for copy in small[0:2]:
        copy.wait()
    live = iota((1, ENT), 1) < count[0]
    pick_t = ones_where((iota((CB, ENT), 0) == order(block[...])) & live)
    pick = dot_rows(eye(ENT), pick_t).astype(bf16)
    pick_out[...] = pick
    pick_t_out[...] = jnp.concatenate([pick_t] * 3, axis=1)
    advance = [doubled(warm, piece) for piece in range(3)]
    picked[...] = dot(pick, twice(*advance))

    def tile_part(part):
        copies[2 * part].wait()
        copies[2 * part + 1].wait()
        for copy in copies[2 * (part + 2) : 2 * (part + 2) + 2]:
            copy.start()
        for number in range(8):
            near, away = 8 * part + number, 32 + 8 * part + number
            above, below = tiles[near], tiles[away]
            flipped[near] = jnp.concatenate([above, below], axis=0).T
            for entry, tile in ((near, above), (away, below)):
                line = picked[entry : entry + 1, 0:TALL].astype(bf16)
                forces[entry : entry + 1] = dot(line, tile)

    for copy in small[2:]:
        copy.wait()
    tile_part(0)
    for piece in range(3):
        warm_out[piece] = advance[piece]
        right_out[piece] = doubled(right, piece)
    rough_out[...] = doubled(rough, 0)
    low = lanes_low((8, 128))
    lanes = []
    for piece in range(3):
        even, odd = lane_tiles(mass, 2 * piece), lane_tiles(mass, 2 * piece + 1)
        lanes.append(
            jnp.concatenate(
                [
                    jnp.where(low, even, pltpu.roll(odd, BLK, 1)),
                    jnp.where(low, pltpu.roll(even, BLK, 1), odd),
                ],
                axis=0,
            )
        )
    mass_tiles = jnp.concatenate(lanes, axis=1)
    mass_out[...] = mass_tiles
    ids = jnp.where(live, owner[...] * NB + order(body[...]), -1)
    hits_t = ones_where(iota((BODIES, ENT), 0) == ids)
    counts = dot_rows(jnp.ones((8, ENT), bf16), hits_t)
    named = jnp.where(counts > 0, 1.0, 0.0)

    owner_row = jnp.where(live, owner[...], -1)
    owner_hit = ones_where(iota((SOIL, ENT), 0) == owner_row)
    earlier = ones_where(iota((ENT, ENT), 0) < iota((ENT, ENT), 1))
    rank = jnp.sum(dot(owner_hit, earlier) * owner_hit.astype(f32), axis=0, keepdims=True)
    tile_part(1)
    slot = jnp.where(live, (owner_row * 16).astype(f32) + rank, -100.0)
    slot_row[...] = jnp.broadcast_to(slot, (8, ENT))
    slot_four = jnp.where(live, (owner_row * CAP).astype(f32) + rank, -100.0)
    chosen_four = ones_where(iota((ENT, ENT), 0).astype(f32) == slot_four)
    label = jnp.where(live, order(body[...]) + 1, 0).astype(bf16)
    label_row = dot_rows(jnp.broadcast_to(label, (8, ENT)), chosen_four)
    id_row = jnp.broadcast_to((ids + 1).astype(f32), (8, ENT))
    label_row = jnp.concatenate([label_row, label_row], axis=1)
    id_row = jnp.concatenate([id_row, id_row], axis=1)
    tile_part(2)
    place = iota((8, 128), 0)
    tail = jnp.zeros((8, 128), f32)
    for number, line in enumerate(
        planes(tire_row(*advance)) + [id_row, named[:, 0:128], named[:, 128:256], label_row]
    ):
        tail = jnp.where(place == number, line, tail)
    tail = tail.astype(bf16)
    mass_high = mass_tiles.astype(bf16)
    for peer in range(SOIL):
        for c, plane in enumerate(planes(mass_high)):
            payload[peer, FORCE_ROWS + NB * c : FORCE_ROWS + NB * c + NB] = plane
        payload[peer, FORCE_ROWS + 3 * NB :] = tail
    for_columns = jnp.concatenate(
        [
            jnp.broadcast_to(slot, (8, ENT)),
            jnp.broadcast_to(ids.astype(f32), (8, ENT)),
        ],
        axis=0,
    )
    columns = dot_rows(eye(ENT), for_columns.astype(bf16))
    slot_out[...] = jnp.broadcast_to(columns[:, 0:1], (ENT, 128))
    id_out[...] = jnp.broadcast_to(columns[:, 8:9], (ENT, 128))

    tile_part(3)
    sent = planes(forces[...].astype(bf16))
    for peer in range(SOIL):
        for c in range(3):
            payload[peer, ENT * c : ENT * c + ENT] = sent[c]


def slot_hits(me, slot_labels):
    column = iota((128, 128), 1)
    row = iota((128, 128), 0)
    mine = ones_where((row == me * CAP + (column >> 4)) & (column < CAP * NB))
    labels = dot(slot_labels.astype(bf16), mine)
    hits = ones_where(labels == ((iota((SOIL, 128), 1) & 15) + 1).astype(f32))
    peer = ones_where((iota((16 * SOIL, SOIL), 0) >> 4) == iota((16 * SOIL, SOIL), 1))
    return dot(peer, hits)


def mass_slots(rows):
    place = iota((16 * SOIL, 128), 0) & 15
    slot = iota((16 * SOIL, 128), 1) >> 4
    low = lanes_low((16 * SOIL, 128))
    shifted = slot - jnp.where(low, 0, CAP)
    first = jnp.where(shifted + jnp.where(low, 3, 3 + CAP) == place, both(rows, False), 0.0)
    second = jnp.where((slot + 3 + 2 * CAP == place) & low, rows, 0.0)
    return jnp.concatenate([first, second], axis=1).astype(bf16)


def owner_slots(rows, gather):
    place = iota((16 * SOIL, 128), 0) & 15
    slot = iota((16 * SOIL, 128), 1) >> 4
    fold = ones_where((iota((NB, 128), 1) & 15) == iota((NB, 128), 0))
    for c in range(3):
        chosen = jnp.where((slot + CAP * c == place) & (slot < CAP), rows, 0.0).astype(bf16)
        gather[NB * c : NB * c + NB] = dot_rows(fold, chosen).astype(bf16)


def match_shares(me, all_named, id_column, share, share_t, own):
    mine = iota((SOIL, BODIES), 0) == me
    named = jnp.sum(jnp.where(mine, all_named, 0.0), axis=0, keepdims=True)
    hits = ones_where(id_column == iota((ENT, BODIES), 1).astype(f32))
    hits_two = jnp.concatenate([hits, hits], axis=0)
    common = jnp.where(mine, 0.0, all_named * named)
    earlier = ones_where(iota((BODIES, BODIES), 0) < iota((BODIES, BODIES), 1))
    slots = jnp.where(common > 0, dot(common.astype(bf16), earlier) + 1.0, 0.0).astype(bf16)
    rank_t = dot_rows(hits, slots).astype(bf16)
    lane_start = iota((SOIL, ROWS), 0) * SHARED
    lanes = iota((SOIL, ROWS), 1)
    spread_lanes = ones_where((lanes >= lane_start) & (lanes < lane_start + SHARED))
    lane_rank = ((iota((ENT, ROWS), 1) & (SHARED - 1)) + 1).astype(f32)
    share_t[...] = ones_where(dot(rank_t, spread_lanes) == lane_rank)
    rank_two = dot_rows(slots, hits_two)
    order_row = (iota((SHARED, 128), 0) + 1).astype(f32)
    for peer in range(SOIL):
        line = jnp.broadcast_to(rank_two[peer : peer + 1], (SHARED, 128))
        share[SHARED * peer : SHARED * peer + SHARED] = ones_where(line == order_row)
    own[...] = dot_rows(hits, hits_two).astype(bf16)


def project_cone(normal, tangent_one, tangent_two, friction):
    tangent_size = jnp.sqrt(tangent_one * tangent_one + tangent_two * tangent_two)
    inside = tangent_size <= friction * normal
    polar_side = friction * tangent_size <= -normal
    middle = jnp.logical_not(jnp.logical_or(inside, polar_side))
    safe_size = jnp.where(middle, tangent_size, 1.0)
    new_normal = (friction * tangent_size + normal) / (1.0 + friction * friction)
    shrink = friction * new_normal / safe_size
    out_normal = jnp.where(inside, normal, jnp.where(polar_side, 0.0, new_normal))
    factor = jnp.where(inside, 1.0, jnp.where(polar_side, 0.0, shrink))
    return out_normal, tangent_one * factor, tangent_two * factor


def step_kernel(
    weight,
    is_first,
    is_last,
    arrived,
    pick,
    pick_t,
    tiles,
    flipped,
    current,
    advance,
    right_side,
    friction,
    *rest,
):
    copy = None
    if is_first:
        id_column, mass_in, matrix_far = rest[0:3]
        payload, new_current, new_advance, new_forces, mass_rows = rest[3:8]
        share, share_t, own, matrix, slot_labels = rest[8:13]
        picked, sem = rest[13:]
        copy = pltpu.make_async_copy(matrix_far, matrix, sem)
        copy.start()
        me = lax.axis_index("soil")
        mine = id_column[:, 0:1]
        tail = arrived[:, FORCE_ROWS + 3 * NB :, :].astype(f32)
        tail = tail.reshape(8 * SOIL, 128).astype(bf16)
        tail_lane = iota((7 * SOIL, 8 * SOIL), 1)
        tail_row = iota((7 * SOIL, 8 * SOIL), 0)
        tails = dot(
            ones_where(tail_lane == (tail_row & (SOIL - 1)) * 8 + (tail_row >> 4)), tail
        )
        tire_all = side_by_side(tails, SOIL)
        names = tails[3 * SOIL : 4 * SOIL]
        all_named = jnp.concatenate(
            [tails[4 * SOIL : 5 * SOIL], tails[5 * SOIL : 6 * SOIL]], axis=1
        )
        low_lanes = lanes_low((1, 128))
        own_name = jnp.where(mine >= 0, mine + 1.0, -1.0)
        match = jnp.concatenate(
            [
                ones_where(
                    own_name
                    == jnp.where(
                        low_lanes, names[2 * t : 2 * t + 1], names[2 * t + 1 : 2 * t + 2]
                    )
                )
                for t in range(SOIL // 2)
            ],
            axis=1,
        )
        name_pick = ones_where(mine == iota((ENT, BODIES), 1).astype(f32))
        found, sums = [], []
        for c in range(3):
            start = FORCE_ROWS + NB * c
            found.append(dot(name_pick, arrived[:, start : start + NB, :].reshape(BODIES, 128)))
            plane = arrived[:, ENT * c : ENT * c + ENT, :].reshape(SOIL * ENT, 128)
            sums.append(dot(match, plane))
        mass_high = jnp.concatenate(found, axis=1)
        mass_rows[...] = mass_high
        wanted = jnp.concatenate(sums, axis=1) * mass_high
        match_shares(me, all_named, mine, share, share_t, own)
        slot_labels[...] = tails[6 * SOIL : 7 * SOIL]
        tail_pick = mass_slots(slot_hits(me, tails[6 * SOIL : 7 * SOIL]))
        mass_low = (mass_in[...] - mass_in[...].astype(bf16).astype(f32)).astype(bf16)
        tail_rows = dot(
            tail_pick,
            jnp.concatenate(
                [plane for plane in planes(mass_low) for _ in range(CAP)]
                + [jnp.zeros((CAP * NB, 128), bf16)],
                axis=0,
            ),
        )
    else:
        forces_in, mass_in, share, share_t, own, matrix = rest[0:6]
        if is_last:
            outputs, picked = rest[6:-1], rest[-1]
        else:
            slot_column, outputs, picked = rest[6], rest[7:-1], rest[-1]
        size = 8 if is_last else 16
        tail = arrived[:, SHARE_ROWS:, :].astype(f32).reshape(size * SOIL, 128).astype(bf16)
        tail_lane = iota((3 * SOIL, size * SOIL), 1)
        tail_row = iota((3 * SOIL, size * SOIL), 0)
        tire_all = side_by_side(
            dot(
                ones_where(tail_lane == (tail_row & (SOIL - 1)) * size + (tail_row >> 4)), tail
            ),
            SOIL,
        )
        received = [
            arrived[:, SHARED * c : SHARED * c + SHARED, :].reshape(ROWS, 128) for c in range(3)
        ]
        sums = jnp.concatenate([dot(share_t[...], plane) for plane in received], axis=1)
        sums += dot(own[...], split_terms(forces_in[...], 2))
        mass_all = mass_in[...]
        if not is_last:
            lane = iota((ENT, 16 * SOIL), 1).astype(f32)
            first = slot_column[:, 0:1] + 3.0
            chosen = [ones_where(lane == first + float(CAP * c)) for c in range(3)]
            mass_all += side_by_side(dot(jnp.concatenate(chosen, axis=0), tail), ENT)
        wanted = sums * mass_all
    pieces = pull(wanted, pick_t[...], flipped)

    line = jnp.concatenate([tire_all[peer : peer + 1] for peer in range(SOIL)], axis=1)
    if copy is not None:
        copy.wait()
    tire = dot(line.astype(bf16), matrix[...])

    row = iota((CB, 128), 0)
    moved = []
    for piece in range(3):
        line = jnp.broadcast_to(tire[:, 128 * piece : 128 * piece + 128], (CB, 128))
        added = jnp.where(
            row == 0, both(line, False), jnp.where(row == 8, both(line, True), 0.0)
        )
        gradient = pieces[piece] + added + right_side[piece]
        moved.append(advance[piece] - step_size * gradient)
    updated = project_cone(*moved, friction[...])
    change = [updated[piece] - current[piece] for piece in range(3)]
    if is_last:
        impulses, doubles, squares = outputs
        low = lanes_low((8, 128))
        for piece in range(3):
            merged = jnp.where(low, updated[piece][0:8], updated[piece][8:16])
            for t in range(8):
                impulses[piece : piece + 1, 128 * t : 128 * t + 128] = merged[t : t + 1]
        doubles[...] = twice(*updated)
        total = change[0] * change[0] + change[1] * change[1] + change[2] * change[2]
        total = jnp.where(lanes_low((CB, 128)), total, 0.0)
        total = jnp.sum(jnp.sum(total, axis=1, keepdims=True), axis=0, keepdims=True)
        squares[...] = jnp.broadcast_to(total.reshape(1, 1, 1), squares.shape)
        return
    if not is_first:
        payload, new_current, new_advance, new_forces, mass_rows = outputs
        mass_rows[...] = mass_all
    ahead = [updated[piece] + weight * change[piece] for piece in range(3)]
    for piece in range(3):
        new_current[piece] = updated[piece]
        new_advance[piece] = ahead[piece]
    picked[...] = dot(pick[...], twice(*ahead)).astype(bf16)
    push(picked, tiles, new_forces)
    shares = dot(share[...], split_terms(new_forces[...], 2)).astype(bf16)
    for c, plane in enumerate(planes(shares)):
        payload[:, SHARED * c : SHARED * c + SHARED, :] = plane.reshape(SOIL, SHARED, 128)
    size = 16 if is_first else 8
    place = iota((size * SOIL, 128), 0) & (size - 1)
    tail_out = tail_rows if is_first else jnp.zeros((size * SOIL, 128), f32)
    for c, line in enumerate(planes(tire_row(*ahead))):
        tail_out = jnp.where(place == c, line, tail_out)
    payload[:, SHARE_ROWS:, :] = tail_out.reshape(SOIL, size, 128).astype(bf16)


def last_push_kernel(
    doubles, pick, slot_row, slot_labels, tiles_far, forces, owner_pick, gather, tiles, sems
):
    copies = [
        pltpu.make_async_copy(
            tiles_far.at[pl.ds(8 * g, 8)], tiles.at[pl.ds(8 * g, 8)], sems.at[g]
        )
        for g in range(8)
    ]
    for copy in copies:
        copy.start()
    picked = dot(pick[...], doubles[...]).astype(bf16)
    mask = entry_mask()
    for group in range(4):
        copies[2 * group].wait()
        copies[2 * group + 1].wait()
        part = slice(16 * group, 16 * group + 16)
        spread = jnp.concatenate([picked[part]] * 8, axis=1) * mask
        forces[part] = dot(spread, tiles[part].reshape(16 * TALL, WIDE))
        if group == 0:
            line = iota((16 * SOIL, ENT), 0).astype(f32)
            chosen = [ones_where(line == slot_row[0:1] + float(CAP * c)) for c in range(3)]
            owner_pick[...] = jnp.concatenate([part for part in chosen for _ in range(3)], axis=1)
        if group == 1:
            owner_slots(slot_hits(lax.axis_index("soil"), slot_labels[...]), gather)


def outgoing_kernel(forces, owner_pick, across, payload):
    terms = [split_terms(plane, 3) for plane in planes(forces[...])]
    rows = dot(owner_pick[...], jnp.concatenate(terms, axis=0))
    squares = jnp.sum(across[:, 0, :], axis=0, keepdims=True)[:, 0:1]
    place = iota((16 * SOIL, 128), 0) & 15
    payload[...] = jnp.where(place == 3 * CAP, squares, rows).reshape(SOIL, 16, 128)


def totals_kernel(scale, arrived, gather, mass, velocity, norm):
    rows = arrived[...].reshape(16 * SOIL, 128)
    is_square = (iota((16 * SOIL, 128), 0) & 15) == 3 * CAP
    squares = jnp.sum(jnp.where(is_square, rows, 0.0), axis=0, keepdims=True)
    norm[...] = jnp.sqrt(squares[:, 0:1] * scale + hold_eps) / step_size
    totals = dot(jnp.concatenate([gather[...]] * 3, axis=1), split_terms(rows, 3))
    totals = side_by_side(totals, NB) * mass[...]
    low = lanes_low((8, 128))
    for piece in range(3):
        tile = totals[:, 128 * piece : 128 * piece + 128]
        even, odd = tile[0:8], tile[8:16]
        for half, merged in enumerate(
            (
                jnp.where(low, even, pltpu.roll(odd, BLK, 1)),
                jnp.where(low, pltpu.roll(even, BLK, 1), odd),
            )
        ):
            component = 2 * piece + half
            for t in range(8):
                velocity[component : component + 1, 128 * t : 128 * t + 128] = merged[t : t + 1]


def step_scratch():
    return [pltpu.VMEM((ENT, WIDE), bf16)]


def on_device(
    warm_start,
    right_side,
    friction,
    inverse_mass,
    jacobian,
    compliance,
    entry_block,
    entry_owner,
    entry_body,
    block_count,
):
    regions = lax.axis_size("grp")
    contacts = warm_start.shape[1]
    elements = 3 * contacts * SOIL * regions
    state = shape_of((3, CB, 128), f32)

    def line(array):
        return far(array.reshape(1, -1))

    (
        payload,
        tiles,
        flipped,
        pick,
        pick_t,
        id_column,
        slot_column,
        slot_row,
        warm,
        right,
        rough,
        mass_tiles,
    ) = pl.pallas_call(
        first_kernel,
        out_shape=(
            shape_of((SOIL, SEND_FIRST, 128), bf16),
            resident((ENT, TALL, WIDE), bf16),
            resident((ENT // 2, WIDE, 2 * TALL), bf16),
            shape_of((ENT, CB), bf16),
            shape_of((CB, 3 * ENT), bf16),
            shape_of((ENT, 128), f32),
            shape_of((ENT, 128), f32),
            shape_of((8, ENT), f32),
            state,
            state,
            shape_of((CB, 128), f32),
            shape_of((NB, WIDE), f32),
        ),
        in_specs=[SCALAR] + [IN_HBM] * 8,
        out_specs=(VECTOR,) * 12,
        scratch_shapes=[
            pltpu.VMEM((1, ENT), i32),
            pltpu.VMEM((1, ENT), i32),
            pltpu.VMEM((1, ENT), i32),
            pltpu.VMEM((3, contacts), f32),
            pltpu.VMEM((3, contacts), f32),
            pltpu.VMEM((1, contacts), f32),
            pltpu.VMEM((6, contacts), f32),
            pltpu.VMEM((ENT, WIDE), f32),
            pltpu.VMEM((ENT, WIDE), f32),
            pltpu.SemaphoreType.DMA((7,)),
            pltpu.SemaphoreType.DMA((ENT // 8,)),
        ],
        compiler_params=params(8),
        name="first",
    )(
        block_count,
        line(entry_owner),
        line(entry_body),
        line(entry_block),
        far(warm_start),
        far(right_side),
        line(friction),
        far(inverse_mass),
        far(jacobian),
    )
    weights = momentum_weights(ITERS)
    current = warm
    advance = warm
    for iteration in range(ITERS):
        arrived = lax.all_to_all(payload, "soil", 0, 0, tiled=True)
        is_first, is_last = iteration == 0, iteration == ITERS - 1
        if is_last:
            outs = [
                shape_of((3, contacts), f32),
                shape_of((CB, WIDE), bf16),
                shape_of((regions, 1, 128), f32),
            ]
        else:
            outs = [
                shape_of((SOIL, SEND_SECOND if is_first else SEND_THIRD, 128), bf16),
                state,
                state,
                shape_of((ENT, WIDE), f32),
                shape_of((ENT, WIDE), f32),
            ]
        scratch = step_scratch()
        if is_first:
            outs += [
                shape_of((ROWS, 128), bf16),
                shape_of((ENT, ROWS), bf16),
                shape_of((ENT, 128), bf16),
                resident(compliance.shape, bf16),
                shape_of((SOIL, 128), f32),
            ]
            more = [id_column, mass_tiles, far(compliance)]
            more_specs = [VECTOR] * 2 + [IN_HBM]
            scratch.append(pltpu.SemaphoreType.DMA)
        else:
            more = [forces, mass_rows, *kept, keep(matrix)]
            if not is_last:
                more.append(slot_column)
            more_specs = [VECTOR] * len(more)
        results = pl.pallas_call(
            functools.partial(step_kernel, weights[iteration], is_first, is_last),
            out_shape=tuple(outs),
            in_specs=[VECTOR] * 9 + more_specs,
            out_specs=(VECTOR,) * len(outs),
            scratch_shapes=scratch,
            compiler_params=params(12),
            name=f"step{iteration}",
        )(
            arrived,
            pick,
            pick_t,
            keep(tiles),
            keep(flipped),
            current,
            advance,
            right,
            rough,
            *more,
        )
        if is_last:
            impulses, doubles, squares = results
            break
        payload, current, advance, forces, mass_rows = results[:5]
        if is_first:
            kept, matrix, slot_labels = results[5:8], results[8], results[9]

    across = lax.all_to_all(squares, "grp", 0, 0, tiled=True)
    forces, owner_pick, gather = pl.pallas_call(
        last_push_kernel,
        out_shape=(
            shape_of((ENT, WIDE), f32),
            shape_of((16 * SOIL, 9 * ENT), bf16),
            shape_of((3 * NB, 16 * SOIL), bf16),
        ),
        in_specs=[VECTOR] * 4 + [IN_HBM],
        out_specs=(VECTOR,) * 3,
        scratch_shapes=[
            pltpu.VMEM((ENT, TALL, WIDE), bf16),
            pltpu.SemaphoreType.DMA((8,)),
        ],
        compiler_params=params(14),
        cost_estimate=pl.CostEstimate(
            flops=10000000, bytes_accessed=10000000, transcendentals=0
        ),
        name="last_push",
    )(doubles, pick, slot_row, slot_labels, far(jacobian))
    outgoing = pl.pallas_call(
        outgoing_kernel,
        out_shape=shape_of((SOIL, 16, 128), f32),
        in_specs=[VECTOR] * 3,
        out_specs=VECTOR,
        compiler_params=params(6),
        name="outgoing",
    )(forces, owner_pick, across)
    arrived = lax.all_to_all(outgoing, "soil", 0, 0, tiled=True)
    velocity, norm = pl.pallas_call(
        functools.partial(totals_kernel, 1.0 / elements),
        out_shape=(shape_of((6, contacts), f32), shape_of((1, 1), f32)),
        in_specs=[VECTOR] * 3,
        out_specs=(VECTOR, VECTOR),
        compiler_params=params(4),
        name="totals",
    )(arrived, gather, mass_tiles)
    return (impulses, velocity, norm[0, 0])


def solution(mesh):
    placed = (
        P(None, ("grp", "soil")),
        P(None, ("grp", "soil")),
        P(("grp", "soil")),
        P(None, ("grp", "soil")),
        P(("grp", "soil"), None, None),
        P(None, "soil"),
        P(("grp", "soil")),
        P(("grp", "soil")),
        P(("grp", "soil")),
        P(("grp", "soil")),
    )
    return jax.shard_map(
        on_device,
        mesh=mesh,
        in_specs=placed,
        out_specs=(P(None, ("grp", "soil")), P(None, ("grp", "soil")), P()),
        check_vma=False,
    )
```

```python
import functools
import math

import jax
import jax.numpy as jnp
from jax import lax
from jax.experimental import pallas as pl
from jax.experimental.pallas import tpu as pltpu
from jax.sharding import PartitionSpec as P

BLK = 64
CB = 16
NB = 16
TC = 128
CAP = 4
ITERS = 3
ENT = 64
SOIL = 16
BODIES = SOIL * NB
WIDE = 6 * BLK
TALL = 3 * BLK
SHARED = 32
ROWS = SOIL * SHARED
FORCE_ROWS = 3 * ENT
SEND_FIRST = FORCE_ROWS + 3 * NB + 8
SHARE_ROWS = 3 * SHARED
SEND_SECOND = SHARE_ROWS + 16
SEND_THIRD = SHARE_ROWS + 8

step_size = 0.1
hold_eps = 1e-06

bf16, f32, i32 = jnp.bfloat16, jnp.float32, jnp.int32

IN_HBM = pl.BlockSpec(memory_space=pltpu.HBM)
VECTOR = pl.BlockSpec(memory_space=pltpu.VMEM)
SCALAR = pl.BlockSpec(memory_space=pltpu.SMEM)


def momentum_weights(number):
    nesterov = 1.0
    weights = []
    for iteration in range(number):
        following = 0.5 * (-nesterov * nesterov + nesterov * math.sqrt(nesterov * nesterov + 4.0))
        weights.append(nesterov * (1.0 - nesterov) / (nesterov * nesterov + following))
        nesterov = following
    return weights


def resident(shape, dtype):
    return pltpu.VMEM(shape, dtype)


def keep(array):
    return pltpu.with_memory_space_constraint(array, pltpu.VMEM)


def far(array):
    return pltpu.with_memory_space_constraint(array, pltpu.HBM)


def shape_of(shape, dtype):
    return jax.ShapeDtypeStruct(shape, dtype)


def params(megabytes):
    return pltpu.CompilerParams(vmem_limit_bytes=megabytes << 20)


def iota(shape, dim):
    return lax.broadcasted_iota(i32, shape, dim)


def ones_where(mask):
    return jnp.where(mask, 1.0, 0.0).astype(bf16)


def dot(left, right):
    return jnp.dot(left, right, preferred_element_type=f32)


def dot_rows(left, right):
    return lax.dot_general(left, right, (((1,), (1,)), ((), ())), preferred_element_type=f32)


def planes(values):
    return [values[:, 128 * c : 128 * c + 128] for c in range(3)]


def side_by_side(rows, size):
    return jnp.concatenate([rows[size * c : size * c + size] for c in range(3)], axis=1)


def split_terms(values, terms):
    parts = []
    for _ in range(terms):
        part = values.astype(bf16)
        parts.append(part)
        values = values - part.astype(f32)
    return jnp.concatenate(parts, axis=0)


def order(block):
    return ((block & 1) << 3) + (block >> 1)


def lanes_low(shape):
    return iota(shape, len(shape) - 1) < BLK


def both(values, upper):
    low = lanes_low(values.shape)
    turned = pltpu.roll(values, BLK, 1)
    return jnp.where(low, turned, values) if upper else jnp.where(low, values, turned)


def lane_tiles(ref, row):
    return jnp.concatenate([ref[row : row + 1, 128 * t : 128 * t + 128] for t in range(8)], axis=0)


def doubled(ref, row):
    tiles = lane_tiles(ref, row)
    return jnp.concatenate([both(tiles, False), both(tiles, True)], axis=0)


def twice(normal, first, second):
    low = lanes_low((CB, 2 * BLK))
    return jnp.concatenate(
        [
            jnp.where(low, normal, first),
            jnp.where(low, second, normal),
            jnp.where(low, first, second),
        ],
        axis=1,
    ).astype(bf16)


def entry_mask():
    column = iota((16, 16 * TALL), 1)
    first = iota((16, 16 * TALL), 0) * TALL
    return ones_where((column >= first) & (column < first + TALL))


def push(picked, tiles, forces):
    mask = entry_mask()

    def group(number):
        rows = picked[pl.ds(16 * number, 16)]
        spread = jnp.concatenate([rows] * 8, axis=1) * mask
        weights = tiles[pl.ds(16 * number, 16)].reshape(16 * TALL, WIDE)
        forces[pl.ds(16 * number, 16)] = dot(spread, weights)

    def step(number, carry):
        group(number)
        group(number + 2)
        return carry

    lax.fori_loop(0, 2, step, 0)


def pull(wanted, pick_t, flipped):
    row = iota((16, WIDE), 0)
    lower, upper = [], []
    for part in range(2):
        sides = []
        for half in range(2):
            start = 32 * half + 16 * part
            rows = wanted[start : start + 16]
            sides.append(
                jnp.concatenate(
                    [rows * ones_where(row == pair) for pair in range(16)], axis=1
                )
            )
        weights = flipped[16 * part : 16 * part + 16].reshape(16 * WIDE, WIDE)
        terms = dot(jnp.concatenate(sides, axis=0), weights)
        lower.append(terms[0:16])
        upper.append(terms[16:32])
    terms = jnp.concatenate(lower + upper, axis=0)
    wrong = (iota((ENT, WIDE), 0) < ENT // 2) == (iota((ENT, WIDE), 1) >= TALL)
    sums = dot(pick_t, split_terms(jnp.where(wrong, 0.0, terms), 3))
    left, middle, right = sums[:, 0:128], sums[:, 128:256], sums[:, 256:384]
    return (
        both(left, False) + both(middle, True),
        both(left, True) + both(right, False),
        both(middle, False) + both(right, True),
    )


def tire_row(normal, first, second):
    low = lanes_low((1, 128))
    return jnp.concatenate(
        [jnp.where(low, part[0:1], part[8:9]) for part in (normal, first, second)], axis=1
    )


def eye(size):
    return ones_where(iota((size, size), 0) == iota((size, size), 1))


def first_kernel(
    count,
    owner_far,
    body_far,
    block_far,
    warm_far,
    right_far,
    rough_far,
    mass_far,
    tiles_far,
    payload,
    tiles,
    flipped,
    pick_out,
    pick_t_out,
    id_out,
    slot_out,
    slot_row,
    warm_out,
    right_out,
    rough_out,
    mass_out,
    owner,
    body,
    block,
    warm,
    right,
    rough,
    mass,
    picked,
    forces,
    sems,
    tile_sems,
):
    small = [
        pltpu.make_async_copy(source, target, sems.at[n])
        for n, (source, target) in enumerate(
            [
                (block_far, block),
                (warm_far, warm),
                (owner_far, owner),
                (body_far, body),
                (mass_far, mass),
                (right_far, right),
                (rough_far, rough),
            ]
        )
    ]
    parts = ((0, 10), (10, 10), (20, 8), (28, 4))
    copies = []
    for part, (start, size) in enumerate(parts):
        for half in range(2):
            entries = pl.ds(32 * half + start, size)
            copies.append(
                pltpu.make_async_copy(
                    tiles_far.at[entries], tiles.at[entries], tile_sems.at[2 * part + half]
                )
            )
    for copy in small + copies[0 : 2 * 2]:
        copy.start()
    for copy in small[0:2]:
        copy.wait()
    live = iota((1, ENT), 1) < count[0]
    pick_t = ones_where((iota((CB, ENT), 0) == order(block[...])) & live)
    pick = dot_rows(eye(ENT), pick_t).astype(bf16)
    pick_out[...] = pick
    pick_t_out[...] = jnp.concatenate([pick_t] * 3, axis=1)
    advance = [doubled(warm, piece) for piece in range(3)]
    picked[...] = dot(pick, twice(*advance))

    def tile_part(part):
        copies[2 * part].wait()
        copies[2 * part + 1].wait()
        for copy in copies[2 * (part + 2) : 2 * (part + 2) + 2]:
            copy.start()
        for near in range(parts[part][0], parts[part][0] + parts[part][1]):
            away = near + 32
            above, below = tiles[near], tiles[away]
            flipped[near] = jnp.concatenate([above, below], axis=0).T
            for entry, tile in ((near, above), (away, below)):
                line = picked[entry : entry + 1, 0:TALL].astype(bf16)
                forces[entry : entry + 1] = dot(line, tile)

    for copy in small[2:]:
        copy.wait()
    tile_part(0)
    for piece in range(3):
        warm_out[piece] = advance[piece]
        right_out[piece] = doubled(right, piece)
    rough_out[...] = doubled(rough, 0)
    low = lanes_low((8, 128))
    lanes = []
    for piece in range(3):
        even, odd = lane_tiles(mass, 2 * piece), lane_tiles(mass, 2 * piece + 1)
        lanes.append(
            jnp.concatenate(
                [
                    jnp.where(low, even, pltpu.roll(odd, BLK, 1)),
                    jnp.where(low, pltpu.roll(even, BLK, 1), odd),
                ],
                axis=0,
            )
        )
    mass_tiles = jnp.concatenate(lanes, axis=1)
    mass_out[...] = mass_tiles
    ids = jnp.where(live, owner[...] * NB + order(body[...]), -1)
    hits_t = ones_where(iota((BODIES, ENT), 0) == ids)
    counts = dot_rows(jnp.ones((8, ENT), bf16), hits_t)
    named = jnp.where(counts > 0, 1.0, 0.0)

    owner_row = jnp.where(live, owner[...], -1)
    owner_hit = ones_where(iota((SOIL, ENT), 0) == owner_row)
    earlier = ones_where(iota((ENT, ENT), 0) < iota((ENT, ENT), 1))
    rank = jnp.sum(dot(owner_hit, earlier) * owner_hit.astype(f32), axis=0, keepdims=True)
    tile_part(1)
    slot = jnp.where(live, (owner_row * 16).astype(f32) + rank, -100.0)
    slot_row[...] = jnp.broadcast_to(slot, (8, ENT))
    slot_four = jnp.where(live, (owner_row * CAP).astype(f32) + rank, -100.0)
    chosen_four = ones_where(iota((ENT, ENT), 0).astype(f32) == slot_four)
    label = jnp.where(live, order(body[...]) + 1, 0).astype(bf16)
    label_row = dot_rows(jnp.broadcast_to(label, (8, ENT)), chosen_four)
    id_row = jnp.broadcast_to((ids + 1).astype(f32), (8, ENT))
    label_row = jnp.concatenate([label_row, label_row], axis=1)
    id_row = jnp.concatenate([id_row, id_row], axis=1)
    tile_part(2)
    place = iota((8, 128), 0)
    tail = jnp.zeros((8, 128), f32)
    for number, line in enumerate(
        planes(tire_row(*advance)) + [id_row, named[:, 0:128], named[:, 128:256], label_row]
    ):
        tail = jnp.where(place == number, line, tail)
    tail = tail.astype(bf16)
    mass_high = mass_tiles.astype(bf16)
    for peer in range(SOIL):
        for c, plane in enumerate(planes(mass_high)):
            payload[peer, FORCE_ROWS + NB * c : FORCE_ROWS + NB * c + NB] = plane
        payload[peer, FORCE_ROWS + 3 * NB :] = tail
    for_columns = jnp.concatenate(
        [
            jnp.broadcast_to(slot, (8, ENT)),
            jnp.broadcast_to(ids.astype(f32), (8, ENT)),
        ],
        axis=0,
    )
    columns = dot_rows(eye(ENT), for_columns.astype(bf16))
    slot_out[...] = jnp.broadcast_to(columns[:, 0:1], (ENT, 128))
    id_out[...] = jnp.broadcast_to(columns[:, 8:9], (ENT, 128))

    tile_part(3)
    sent = planes(forces[...].astype(bf16))
    for peer in range(SOIL):
        for c in range(3):
            payload[peer, ENT * c : ENT * c + ENT] = sent[c]


def slot_hits(me, slot_labels):
    column = iota((128, 128), 1)
    row = iota((128, 128), 0)
    mine = ones_where((row == me * CAP + (column >> 4)) & (column < CAP * NB))
    labels = dot(slot_labels.astype(bf16), mine)
    hits = ones_where(labels == ((iota((SOIL, 128), 1) & 15) + 1).astype(f32))
    peer = ones_where((iota((16 * SOIL, SOIL), 0) >> 4) == iota((16 * SOIL, SOIL), 1))
    return dot(peer, hits)


def mass_slots(rows):
    place = iota((16 * SOIL, 128), 0) & 15
    slot = iota((16 * SOIL, 128), 1) >> 4
    low = lanes_low((16 * SOIL, 128))
    shifted = slot - jnp.where(low, 0, CAP)
    first = jnp.where(shifted + jnp.where(low, 3, 3 + CAP) == place, both(rows, False), 0.0)
    second = jnp.where((slot + 3 + 2 * CAP == place) & low, rows, 0.0)
    return jnp.concatenate([first, second], axis=1).astype(bf16)


def owner_slots(rows, gather):
    place = iota((16 * SOIL, 128), 0) & 15
    slot = iota((16 * SOIL, 128), 1) >> 4
    fold = ones_where((iota((NB, 128), 1) & 15) == iota((NB, 128), 0))
    for c in range(3):
        chosen = jnp.where((slot + CAP * c == place) & (slot < CAP), rows, 0.0).astype(bf16)
        gather[NB * c : NB * c + NB] = dot_rows(fold, chosen).astype(bf16)


def match_shares(me, all_named, id_column, share, share_t, own):
    mine = iota((SOIL, BODIES), 0) == me
    named = jnp.sum(jnp.where(mine, all_named, 0.0), axis=0, keepdims=True)
    hits = ones_where(id_column == iota((ENT, BODIES), 1).astype(f32))
    hits_two = jnp.concatenate([hits, hits], axis=0)
    common = jnp.where(mine, 0.0, all_named * named)
    earlier = ones_where(iota((BODIES, BODIES), 0) < iota((BODIES, BODIES), 1))
    slots = jnp.where(common > 0, dot(common.astype(bf16), earlier) + 1.0, 0.0).astype(bf16)
    rank_t = dot_rows(hits, slots).astype(bf16)
    lane_start = iota((SOIL, ROWS), 0) * SHARED
    lanes = iota((SOIL, ROWS), 1)
    spread_lanes = ones_where((lanes >= lane_start) & (lanes < lane_start + SHARED))
    lane_rank = ((iota((ENT, ROWS), 1) & (SHARED - 1)) + 1).astype(f32)
    share_t[...] = ones_where(dot(rank_t, spread_lanes) == lane_rank)
    rank_two = dot_rows(slots, hits_two)
    order_row = (iota((SHARED, 128), 0) + 1).astype(f32)
    for peer in range(SOIL):
        line = jnp.broadcast_to(rank_two[peer : peer + 1], (SHARED, 128))
        share[SHARED * peer : SHARED * peer + SHARED] = ones_where(line == order_row)
    own[...] = dot_rows(hits, hits_two).astype(bf16)


def project_cone(normal, tangent_one, tangent_two, friction):
    tangent_size = jnp.sqrt(tangent_one * tangent_one + tangent_two * tangent_two)
    inside = tangent_size <= friction * normal
    polar_side = friction * tangent_size <= -normal
    middle = jnp.logical_not(jnp.logical_or(inside, polar_side))
    safe_size = jnp.where(middle, tangent_size, 1.0)
    new_normal = (friction * tangent_size + normal) / (1.0 + friction * friction)
    shrink = friction * new_normal / safe_size
    out_normal = jnp.where(inside, normal, jnp.where(polar_side, 0.0, new_normal))
    factor = jnp.where(inside, 1.0, jnp.where(polar_side, 0.0, shrink))
    return out_normal, tangent_one * factor, tangent_two * factor


def step_kernel(
    weight,
    is_first,
    is_last,
    arrived,
    pick,
    pick_t,
    tiles,
    flipped,
    current,
    advance,
    right_side,
    friction,
    *rest,
):
    copy = None
    if is_first:
        id_column, mass_in, matrix_far = rest[0:3]
        payload, new_current, new_advance, new_forces, mass_rows = rest[3:8]
        share, share_t, own, matrix, slot_labels = rest[8:13]
        spread, picked, sem = rest[13:]
        copy = pltpu.make_async_copy(matrix_far, matrix, sem)
        copy.start()
        me = lax.axis_index("soil")
        mine = id_column[:, 0:1]
        tail = arrived[:, FORCE_ROWS + 3 * NB :, :].astype(f32)
        tail = tail.reshape(8 * SOIL, 128).astype(bf16)
        tail_lane = iota((7 * SOIL, 8 * SOIL), 1)
        tail_row = iota((7 * SOIL, 8 * SOIL), 0)
        tails = dot(
            ones_where(tail_lane == (tail_row & (SOIL - 1)) * 8 + (tail_row >> 4)), tail
        )
        tire_all = side_by_side(tails, SOIL)
        names = tails[3 * SOIL : 4 * SOIL]
        all_named = jnp.concatenate(
            [tails[4 * SOIL : 5 * SOIL], tails[5 * SOIL : 6 * SOIL]], axis=1
        )
        low_lanes = lanes_low((1, 128))
        own_name = jnp.where(mine >= 0, mine + 1.0, -1.0)
        match = jnp.concatenate(
            [
                ones_where(
                    own_name
                    == jnp.where(
                        low_lanes, names[2 * t : 2 * t + 1], names[2 * t + 1 : 2 * t + 2]
                    )
                )
                for t in range(SOIL // 2)
            ],
            axis=1,
        )
        name_pick = ones_where(mine == iota((ENT, BODIES), 1).astype(f32))
        found, sums = [], []
        for c in range(3):
            start = FORCE_ROWS + NB * c
            found.append(dot(name_pick, arrived[:, start : start + NB, :].reshape(BODIES, 128)))
            plane = arrived[:, ENT * c : ENT * c + ENT, :].reshape(SOIL * ENT, 128)
            sums.append(dot(match, plane))
        mass_high = jnp.concatenate(found, axis=1)
        mass_rows[...] = mass_high
        wanted = jnp.concatenate(sums, axis=1) * mass_high
        match_shares(me, all_named, mine, share, share_t, own)
        slot_labels[...] = tails[6 * SOIL : 7 * SOIL]
        tail_pick = mass_slots(slot_hits(me, tails[6 * SOIL : 7 * SOIL]))
        mass_low = (mass_in[...] - mass_in[...].astype(bf16).astype(f32)).astype(bf16)
        tail_rows = dot(
            tail_pick,
            jnp.concatenate(
                [plane for plane in planes(mass_low) for _ in range(CAP)]
                + [jnp.zeros((CAP * NB, 128), bf16)],
                axis=0,
            ),
        )
    else:
        forces_in, mass_in, share, share_t, own, matrix = rest[0:6]
        if is_last:
            outputs, (spread, picked) = rest[6:-2], rest[-2:]
        else:
            slot_column, outputs, (spread, picked) = rest[6], rest[7:-2], rest[-2:]
        size = 8 if is_last else 16
        tail = arrived[:, SHARE_ROWS:, :].astype(f32).reshape(size * SOIL, 128).astype(bf16)
        tail_lane = iota((3 * SOIL, size * SOIL), 1)
        tail_row = iota((3 * SOIL, size * SOIL), 0)
        tire_all = side_by_side(
            dot(
                ones_where(tail_lane == (tail_row & (SOIL - 1)) * size + (tail_row >> 4)), tail
            ),
            SOIL,
        )
        received = [
            arrived[:, SHARED * c : SHARED * c + SHARED, :].reshape(ROWS, 128) for c in range(3)
        ]
        sums = jnp.concatenate([dot(share_t[...], plane) for plane in received], axis=1)
        sums += dot(own[...], split_terms(forces_in[...], 2))
        mass_all = mass_in[...]
        if not is_last:
            lane = iota((ENT, 16 * SOIL), 1).astype(f32)
            first = slot_column[:, 0:1] + 3.0
            chosen = [ones_where(lane == first + float(CAP * c)) for c in range(3)]
            mass_all += side_by_side(dot(jnp.concatenate(chosen, axis=0), tail), ENT)
        wanted = sums * mass_all
    pieces = pull(wanted.astype(bf16), pick_t[...], flipped)

    device = iota((SOIL, WIDE), 0)
    for peer in range(SOIL):
        spread[:, WIDE * peer : WIDE * peer + WIDE] = jnp.where(
            device == peer, tire_all, 0.0
        ).astype(bf16)
    if copy is not None:
        copy.wait()
    tire = jnp.sum(dot(spread[...], matrix[...]), axis=0, keepdims=True)

    row = iota((CB, 128), 0)
    moved = []
    for piece in range(3):
        line = jnp.broadcast_to(tire[:, 128 * piece : 128 * piece + 128], (CB, 128))
        added = jnp.where(
            row == 0, both(line, False), jnp.where(row == 8, both(line, True), 0.0)
        )
        gradient = pieces[piece] + added + right_side[piece]
        moved.append(advance[piece] - step_size * gradient)
    updated = project_cone(*moved, friction[...])
    change = [updated[piece] - current[piece] for piece in range(3)]
    if is_last:
        impulses, doubles, squares = outputs
        low = lanes_low((8, 128))
        for piece in range(3):
            merged = jnp.where(low, updated[piece][0:8], updated[piece][8:16])
            for t in range(8):
                impulses[piece : piece + 1, 128 * t : 128 * t + 128] = merged[t : t + 1]
        doubles[...] = twice(*updated)
        total = change[0] * change[0] + change[1] * change[1] + change[2] * change[2]
        total = jnp.where(lanes_low((CB, 128)), total, 0.0)
        total = jnp.sum(jnp.sum(total, axis=1, keepdims=True), axis=0, keepdims=True)
        squares[...] = jnp.broadcast_to(total.reshape(1, 1, 1), squares.shape)
        return
    if not is_first:
        payload, new_current, new_advance, new_forces, mass_rows = outputs
        mass_rows[...] = mass_all
    ahead = [updated[piece] + weight * change[piece] for piece in range(3)]
    for piece in range(3):
        new_current[piece] = updated[piece]
        new_advance[piece] = ahead[piece]
    picked[...] = dot(pick[...], twice(*ahead)).astype(bf16)
    push(picked, tiles, new_forces)
    shares = dot(share[...], split_terms(new_forces[...], 2)).astype(bf16)
    for c, plane in enumerate(planes(shares)):
        payload[:, SHARED * c : SHARED * c + SHARED, :] = plane.reshape(SOIL, SHARED, 128)
    size = 16 if is_first else 8
    place = iota((size * SOIL, 128), 0) & (size - 1)
    tail_out = tail_rows if is_first else jnp.zeros((size * SOIL, 128), f32)
    for c, line in enumerate(planes(tire_row(*ahead))):
        tail_out = jnp.where(place == c, line, tail_out)
    payload[:, SHARE_ROWS:, :] = tail_out.reshape(SOIL, size, 128).astype(bf16)


def last_push_kernel(
    doubles, pick, slot_row, slot_labels, tiles_far, forces, owner_pick, gather, tiles, sems
):
    copies = [
        pltpu.make_async_copy(
            tiles_far.at[pl.ds(16 * g, 16)], tiles.at[pl.ds(16 * g, 16)], sems.at[g]
        )
        for g in range(4)
    ]
    for copy in copies:
        copy.start()
    picked = dot(pick[...], doubles[...]).astype(bf16)
    mask = entry_mask()
    for group in range(4):
        copies[group].wait()
        part = slice(16 * group, 16 * group + 16)
        spread = jnp.concatenate([picked[part]] * 8, axis=1) * mask
        forces[part] = dot(spread, tiles[part].reshape(16 * TALL, WIDE))
        if group == 0:
            line = iota((16 * SOIL, ENT), 0).astype(f32)
            chosen = [ones_where(line == slot_row[0:1] + float(CAP * c)) for c in range(3)]
            owner_pick[...] = jnp.concatenate([part for part in chosen for _ in range(3)], axis=1)
        if group == 1:
            owner_slots(slot_hits(lax.axis_index("soil"), slot_labels[...]), gather)


def outgoing_kernel(forces, owner_pick, across, payload):
    terms = [split_terms(plane, 3) for plane in planes(forces[...])]
    rows = dot(owner_pick[...], jnp.concatenate(terms, axis=0))
    squares = jnp.sum(across[:, 0, :], axis=0, keepdims=True)[:, 0:1]
    place = iota((16 * SOIL, 128), 0) & 15
    payload[...] = jnp.where(place == 3 * CAP, squares, rows).reshape(SOIL, 16, 128)


def totals_kernel(scale, arrived, gather, mass, velocity, norm):
    rows = arrived[...].reshape(16 * SOIL, 128)
    is_square = (iota((16 * SOIL, 128), 0) & 15) == 3 * CAP
    squares = jnp.sum(jnp.where(is_square, rows, 0.0), axis=0, keepdims=True)
    norm[...] = jnp.sqrt(squares[:, 0:1] * scale + hold_eps) / step_size
    totals = dot(jnp.concatenate([gather[...]] * 3, axis=1), split_terms(rows, 3))
    totals = side_by_side(totals, NB) * mass[...]
    low = lanes_low((8, 128))
    for piece in range(3):
        tile = totals[:, 128 * piece : 128 * piece + 128]
        even, odd = tile[0:8], tile[8:16]
        for half, merged in enumerate(
            (
                jnp.where(low, even, pltpu.roll(odd, BLK, 1)),
                jnp.where(low, pltpu.roll(even, BLK, 1), odd),
            )
        ):
            component = 2 * piece + half
            for t in range(8):
                velocity[component : component + 1, 128 * t : 128 * t + 128] = merged[t : t + 1]


def step_scratch():
    return [pltpu.VMEM((SOIL, SOIL * 3 * TC), bf16), pltpu.VMEM((ENT, WIDE), bf16)]


def on_device(
    warm_start,
    right_side,
    friction,
    inverse_mass,
    jacobian,
    compliance,
    entry_block,
    entry_owner,
    entry_body,
    block_count,
):
    regions = lax.axis_size("grp")
    contacts = warm_start.shape[1]
    elements = 3 * contacts * SOIL * regions
    state = shape_of((3, CB, 128), f32)

    def line(array):
        return far(array.reshape(1, -1))

    (
        payload,
        tiles,
        flipped,
        pick,
        pick_t,
        id_column,
        slot_column,
        slot_row,
        warm,
        right,
        rough,
        mass_tiles,
    ) = pl.pallas_call(
        first_kernel,
        out_shape=(
            shape_of((SOIL, SEND_FIRST, 128), bf16),
            resident((ENT, TALL, WIDE), bf16),
            resident((ENT // 2, WIDE, 2 * TALL), bf16),
            shape_of((ENT, CB), bf16),
            shape_of((CB, 3 * ENT), bf16),
            shape_of((ENT, 128), f32),
            shape_of((ENT, 128), f32),
            shape_of((8, ENT), f32),
            state,
            state,
            shape_of((CB, 128), f32),
            shape_of((NB, WIDE), f32),
        ),
        in_specs=[SCALAR] + [IN_HBM] * 8,
        out_specs=(VECTOR,) * 12,
        scratch_shapes=[
            pltpu.VMEM((1, ENT), i32),
            pltpu.VMEM((1, ENT), i32),
            pltpu.VMEM((1, ENT), i32),
            pltpu.VMEM((3, contacts), f32),
            pltpu.VMEM((3, contacts), f32),
            pltpu.VMEM((1, contacts), f32),
            pltpu.VMEM((6, contacts), f32),
            pltpu.VMEM((ENT, WIDE), f32),
            pltpu.VMEM((ENT, WIDE), f32),
            pltpu.SemaphoreType.DMA((7,)),
            pltpu.SemaphoreType.DMA((ENT // 8,)),
        ],
        compiler_params=params(8),
        name="first",
    )(
        block_count,
        line(entry_owner),
        line(entry_body),
        line(entry_block),
        far(warm_start),
        far(right_side),
        line(friction),
        far(inverse_mass),
        far(jacobian),
    )
    weights = momentum_weights(ITERS)
    current = warm
    advance = warm
    for iteration in range(ITERS):
        arrived = lax.all_to_all(payload, "soil", 0, 0, tiled=True)
        is_first, is_last = iteration == 0, iteration == ITERS - 1
        if is_last:
            outs = [
                shape_of((3, contacts), f32),
                shape_of((CB, WIDE), bf16),
                shape_of((regions, 1, 128), f32),
            ]
        else:
            outs = [
                shape_of((SOIL, SEND_SECOND if is_first else SEND_THIRD, 128), bf16),
                state,
                state,
                shape_of((ENT, WIDE), f32),
                shape_of((ENT, WIDE), f32),
            ]
        scratch = step_scratch()
        if is_first:
            outs += [
                shape_of((ROWS, 128), bf16),
                shape_of((ENT, ROWS), bf16),
                shape_of((ENT, 128), bf16),
                resident(compliance.shape, bf16),
                shape_of((SOIL, 128), f32),
            ]
            more = [id_column, mass_tiles, far(compliance)]
            more_specs = [VECTOR] * 2 + [IN_HBM]
            scratch.append(pltpu.SemaphoreType.DMA)
        else:
            more = [forces, mass_rows, *kept, keep(matrix)]
            if not is_last:
                more.append(slot_column)
            more_specs = [VECTOR] * len(more)
        results = pl.pallas_call(
            functools.partial(step_kernel, weights[iteration], is_first, is_last),
            out_shape=tuple(outs),
            in_specs=[VECTOR] * 9 + more_specs,
            out_specs=(VECTOR,) * len(outs),
            scratch_shapes=scratch,
            compiler_params=params(12),
            name=f"step{iteration}",
        )(
            arrived,
            pick,
            pick_t,
            keep(tiles),
            keep(flipped),
            current,
            advance,
            right,
            rough,
            *more,
        )
        if is_last:
            impulses, doubles, squares = results
            break
        payload, current, advance, forces, mass_rows = results[:5]
        if is_first:
            kept, matrix, slot_labels = results[5:8], results[8], results[9]

    across = lax.all_to_all(squares, "grp", 0, 0, tiled=True)
    forces, owner_pick, gather = pl.pallas_call(
        last_push_kernel,
        out_shape=(
            shape_of((ENT, WIDE), f32),
            shape_of((16 * SOIL, 9 * ENT), bf16),
            shape_of((3 * NB, 16 * SOIL), bf16),
        ),
        in_specs=[VECTOR] * 4 + [IN_HBM],
        out_specs=(VECTOR,) * 3,
        scratch_shapes=[
            pltpu.VMEM((ENT, TALL, WIDE), bf16),
            pltpu.SemaphoreType.DMA((4,)),
        ],
        compiler_params=params(14),
        cost_estimate=pl.CostEstimate(
            flops=10000000, bytes_accessed=10000000, transcendentals=0
        ),
        name="last_push",
    )(doubles, pick, slot_row, slot_labels, far(jacobian))
    outgoing = pl.pallas_call(
        outgoing_kernel,
        out_shape=shape_of((SOIL, 16, 128), f32),
        in_specs=[VECTOR] * 3,
        out_specs=VECTOR,
        compiler_params=params(6),
        name="outgoing",
    )(forces, owner_pick, across)
    arrived = lax.all_to_all(outgoing, "soil", 0, 0, tiled=True)
    velocity, norm = pl.pallas_call(
        functools.partial(totals_kernel, 1.0 / elements),
        out_shape=(shape_of((6, contacts), f32), shape_of((1, 1), f32)),
        in_specs=[VECTOR] * 3,
        out_specs=(VECTOR, VECTOR),
        compiler_params=params(4),
        name="totals",
    )(arrived, gather, mass_tiles)
    return (impulses, velocity, norm[0, 0])


def solution(mesh):
    placed = (
        P(None, ("grp", "soil")),
        P(None, ("grp", "soil")),
        P(("grp", "soil")),
        P(None, ("grp", "soil")),
        P(("grp", "soil"), None, None),
        P(None, "soil"),
        P(("grp", "soil")),
        P(("grp", "soil")),
        P(("grp", "soil")),
        P(("grp", "soil")),
    )
    return jax.shard_map(
        on_device,
        mesh=mesh,
        in_specs=placed,
        out_specs=(P(None, ("grp", "soil")), P(None, ("grp", "soil")), P()),
        check_vma=False,
    )
```

```python
import functools
import math

import jax
import jax.numpy as jnp
from jax import lax
from jax.experimental import pallas as pl
from jax.experimental.pallas import tpu as pltpu
from jax.sharding import PartitionSpec as P

BLK = 64
CB = 16
NB = 16
TC = 128
CAP = 4
ITERS = 3
ENT = 64
SOIL = 16
BODIES = SOIL * NB
WIDE = 6 * BLK
TALL = 3 * BLK
SHARED = 32
ROWS = SOIL * SHARED
FORCE_ROWS = 3 * ENT
SEND_FIRST = FORCE_ROWS + 3 * NB + 8
SHARE_ROWS = 3 * SHARED
SEND_SECOND = SHARE_ROWS + 16
SEND_THIRD = SHARE_ROWS + 8

step_size = 0.1
hold_eps = 1e-06

bf16, f32, i32 = jnp.bfloat16, jnp.float32, jnp.int32

IN_HBM = pl.BlockSpec(memory_space=pltpu.HBM)
VECTOR = pl.BlockSpec(memory_space=pltpu.VMEM)
SCALAR = pl.BlockSpec(memory_space=pltpu.SMEM)


def momentum_weights(number):
    nesterov = 1.0
    weights = []
    for iteration in range(number):
        following = 0.5 * (-nesterov * nesterov + nesterov * math.sqrt(nesterov * nesterov + 4.0))
        weights.append(nesterov * (1.0 - nesterov) / (nesterov * nesterov + following))
        nesterov = following
    return weights


def resident(shape, dtype):
    return pltpu.VMEM(shape, dtype)


def keep(array):
    return pltpu.with_memory_space_constraint(array, pltpu.VMEM)


def far(array):
    return pltpu.with_memory_space_constraint(array, pltpu.HBM)


def shape_of(shape, dtype):
    return jax.ShapeDtypeStruct(shape, dtype)


def params(megabytes):
    return pltpu.CompilerParams(vmem_limit_bytes=megabytes << 20)


def iota(shape, dim):
    return lax.broadcasted_iota(i32, shape, dim)


def ones_where(mask):
    return jnp.where(mask, 1.0, 0.0).astype(bf16)


def dot(left, right):
    return jnp.dot(left, right, preferred_element_type=f32)


def dot_rows(left, right):
    return lax.dot_general(left, right, (((1,), (1,)), ((), ())), preferred_element_type=f32)


def planes(values):
    return [values[:, 128 * c : 128 * c + 128] for c in range(3)]


def side_by_side(rows, size):
    return jnp.concatenate([rows[size * c : size * c + size] for c in range(3)], axis=1)


def split_terms(values, terms):
    parts = []
    for _ in range(terms):
        part = values.astype(bf16)
        parts.append(part)
        values = values - part.astype(f32)
    return jnp.concatenate(parts, axis=0)


def order(block):
    return ((block & 1) << 3) + (block >> 1)


def lanes_low(shape):
    return iota(shape, len(shape) - 1) < BLK


def both(values, upper):
    low = lanes_low(values.shape)
    turned = pltpu.roll(values, BLK, 1)
    return jnp.where(low, turned, values) if upper else jnp.where(low, values, turned)


def lane_tiles(ref, row):
    return jnp.concatenate([ref[row : row + 1, 128 * t : 128 * t + 128] for t in range(8)], axis=0)


def doubled(ref, row):
    tiles = lane_tiles(ref, row)
    return jnp.concatenate([both(tiles, False), both(tiles, True)], axis=0)


def twice(normal, first, second):
    low = lanes_low((CB, 2 * BLK))
    return jnp.concatenate(
        [
            jnp.where(low, normal, first),
            jnp.where(low, second, normal),
            jnp.where(low, first, second),
        ],
        axis=1,
    ).astype(bf16)


def entry_mask():
    column = iota((16, 16 * TALL), 1)
    first = iota((16, 16 * TALL), 0) * TALL
    return ones_where((column >= first) & (column < first + TALL))


def push(picked, tiles, forces):
    mask = entry_mask()

    def group(number):
        rows = picked[pl.ds(16 * number, 16)]
        spread = jnp.concatenate([rows] * 8, axis=1) * mask
        weights = tiles[pl.ds(16 * number, 16)].reshape(16 * TALL, WIDE)
        forces[pl.ds(16 * number, 16)] = dot(spread, weights)

    def step(number, carry):
        group(number)
        group(number + 2)
        return carry

    lax.fori_loop(0, 2, step, 0)


def pull(wanted, pick_t, flipped):
    row = iota((16, WIDE), 0)
    lower, upper = [], []
    for part in range(2):
        sides = []
        for half in range(2):
            start = 32 * half + 16 * part
            rows = wanted[start : start + 16]
            sides.append(
                jnp.concatenate(
                    [rows * ones_where(row == pair) for pair in range(16)], axis=1
                )
            )
        weights = flipped[16 * part : 16 * part + 16].reshape(16 * WIDE, WIDE)
        terms = dot(jnp.concatenate(sides, axis=0), weights)
        lower.append(terms[0:16])
        upper.append(terms[16:32])
    terms = jnp.concatenate(lower + upper, axis=0)
    wrong = (iota((ENT, WIDE), 0) < ENT // 2) == (iota((ENT, WIDE), 1) >= TALL)
    sums = dot(pick_t, split_terms(jnp.where(wrong, 0.0, terms), 3))
    left, middle, right = sums[:, 0:128], sums[:, 128:256], sums[:, 256:384]
    return (
        both(left, False) + both(middle, True),
        both(left, True) + both(right, False),
        both(middle, False) + both(right, True),
    )


def tire_row(normal, first, second):
    low = lanes_low((1, 128))
    return jnp.concatenate(
        [jnp.where(low, part[0:1], part[8:9]) for part in (normal, first, second)], axis=1
    )


def eye(size):
    return ones_where(iota((size, size), 0) == iota((size, size), 1))


def first_kernel(
    count,
    owner_far,
    body_far,
    block_far,
    warm_far,
    right_far,
    rough_far,
    mass_far,
    tiles_far,
    payload,
    tiles,
    flipped,
    pick_out,
    pick_t_out,
    id_out,
    slot_out,
    slot_row,
    warm_out,
    right_out,
    rough_out,
    mass_out,
    owner,
    body,
    block,
    warm,
    right,
    rough,
    mass,
    picked,
    forces,
    sems,
    tile_sems,
):
    small = [
        pltpu.make_async_copy(source, target, sems.at[n])
        for n, (source, target) in enumerate(
            [
                (block_far, block),
                (warm_far, warm),
                (owner_far, owner),
                (body_far, body),
                (mass_far, mass),
                (right_far, right),
                (rough_far, rough),
            ]
        )
    ]
    copies = []
    for start in (0, 32, 8, 40, 16, 48, 24, 56):
        part = pl.ds(start, 8)
        copies.append(
            pltpu.make_async_copy(tiles_far.at[part], tiles.at[part], tile_sems.at[start // 8])
        )
    for copy in small + copies[0 : 2 * 2]:
        copy.start()
    for copy in small[0:2]:
        copy.wait()
    live = iota((1, ENT), 1) < count[0]
    pick_t = ones_where((iota((CB, ENT), 0) == order(block[...])) & live)
    pick = dot_rows(eye(ENT), pick_t).astype(bf16)
    pick_out[...] = pick
    pick_t_out[...] = jnp.concatenate([pick_t] * 3, axis=1)
    advance = [doubled(warm, piece) for piece in range(3)]
    picked[...] = dot(pick, twice(*advance))

    def tile_part(part):
        copies[2 * part].wait()
        copies[2 * part + 1].wait()
        for copy in copies[2 * (part + 2) : 2 * (part + 2) + 2]:
            copy.start()
        for number in range(8):
            near, away = 8 * part + number, 32 + 8 * part + number
            above, below = tiles[near], tiles[away]
            flipped[near] = jnp.concatenate([above, below], axis=0).T
            for entry, tile in ((near, above), (away, below)):
                line = picked[entry : entry + 1, 0:TALL].astype(bf16)
                forces[entry : entry + 1] = dot(line, tile)

    for copy in small[2:]:
        copy.wait()
    tile_part(0)
    for piece in range(3):
        warm_out[piece] = advance[piece]
        right_out[piece] = doubled(right, piece)
    rough_out[...] = doubled(rough, 0)
    low = lanes_low((8, 128))
    lanes = []
    for piece in range(3):
        even, odd = lane_tiles(mass, 2 * piece), lane_tiles(mass, 2 * piece + 1)
        lanes.append(
            jnp.concatenate(
                [
                    jnp.where(low, even, pltpu.roll(odd, BLK, 1)),
                    jnp.where(low, pltpu.roll(even, BLK, 1), odd),
                ],
                axis=0,
            )
        )
    mass_tiles = jnp.concatenate(lanes, axis=1)
    mass_out[...] = mass_tiles
    ids = jnp.where(live, owner[...] * NB + order(body[...]), -1)
    hits_t = ones_where(iota((BODIES, ENT), 0) == ids)
    counts = dot_rows(jnp.ones((8, ENT), bf16), hits_t)
    named = jnp.where(counts > 0, 1.0, 0.0)

    owner_row = jnp.where(live, owner[...], -1)
    owner_hit = ones_where(iota((SOIL, ENT), 0) == owner_row)
    earlier = ones_where(iota((ENT, ENT), 0) < iota((ENT, ENT), 1))
    rank = jnp.sum(dot(owner_hit, earlier) * owner_hit.astype(f32), axis=0, keepdims=True)
    tile_part(1)
    slot = jnp.where(live, (owner_row * 16).astype(f32) + rank, -100.0)
    slot_row[...] = jnp.broadcast_to(slot, (8, ENT))
    slot_four = jnp.where(live, (owner_row * CAP).astype(f32) + rank, -100.0)
    chosen_four = ones_where(iota((ENT, ENT), 0).astype(f32) == slot_four)
    label = jnp.where(live, order(body[...]) + 1, 0).astype(bf16)
    label_row = dot_rows(jnp.broadcast_to(label, (8, ENT)), chosen_four)
    id_row = jnp.broadcast_to((ids + 1).astype(f32), (8, ENT))
    label_row = jnp.concatenate([label_row, label_row], axis=1)
    id_row = jnp.concatenate([id_row, id_row], axis=1)
    tile_part(2)
    place = iota((8, 128), 0)
    tail = jnp.zeros((8, 128), f32)
    for number, line in enumerate(
        planes(tire_row(*advance)) + [id_row, named[:, 0:128], named[:, 128:256], label_row]
    ):
        tail = jnp.where(place == number, line, tail)
    tail = tail.astype(bf16)
    mass_high = mass_tiles.astype(bf16)
    for peer in range(SOIL):
        for c, plane in enumerate(planes(mass_high)):
            payload[peer, FORCE_ROWS + NB * c : FORCE_ROWS + NB * c + NB] = plane
        payload[peer, FORCE_ROWS + 3 * NB :] = tail
    for_columns = jnp.concatenate(
        [
            jnp.broadcast_to(slot, (8, ENT)),
            jnp.broadcast_to(ids.astype(f32), (8, ENT)),
        ],
        axis=0,
    )
    columns = dot_rows(eye(ENT), for_columns.astype(bf16))
    slot_out[...] = jnp.broadcast_to(columns[:, 0:1], (ENT, 128))
    id_out[...] = jnp.broadcast_to(columns[:, 8:9], (ENT, 128))

    tile_part(3)
    sent = planes(forces[...].astype(bf16))
    for peer in range(SOIL):
        for c in range(3):
            payload[peer, ENT * c : ENT * c + ENT] = sent[c]


def slot_hits(me, slot_labels):
    column = iota((128, 128), 1)
    row = iota((128, 128), 0)
    mine = ones_where((row == me * CAP + (column >> 4)) & (column < CAP * NB))
    labels = dot(slot_labels.astype(bf16), mine)
    hits = ones_where(labels == ((iota((SOIL, 128), 1) & 15) + 1).astype(f32))
    peer = ones_where((iota((16 * SOIL, SOIL), 0) >> 4) == iota((16 * SOIL, SOIL), 1))
    return dot(peer, hits)


def mass_slots(rows):
    place = iota((16 * SOIL, 128), 0) & 15
    slot = iota((16 * SOIL, 128), 1) >> 4
    low = lanes_low((16 * SOIL, 128))
    shifted = slot - jnp.where(low, 0, CAP)
    first = jnp.where(shifted + jnp.where(low, 3, 3 + CAP) == place, both(rows, False), 0.0)
    second = jnp.where((slot + 3 + 2 * CAP == place) & low, rows, 0.0)
    return jnp.concatenate([first, second], axis=1).astype(bf16)


def owner_slots(rows, gather):
    place = iota((16 * SOIL, 128), 0) & 15
    slot = iota((16 * SOIL, 128), 1) >> 4
    fold = ones_where((iota((NB, 128), 1) & 15) == iota((NB, 128), 0))
    for c in range(3):
        chosen = jnp.where((slot + CAP * c == place) & (slot < CAP), rows, 0.0).astype(bf16)
        gather[NB * c : NB * c + NB] = dot_rows(fold, chosen).astype(bf16)


def match_shares(me, all_named, id_column, share, share_t, own):
    mine = iota((SOIL, BODIES), 0) == me
    named = jnp.sum(jnp.where(mine, all_named, 0.0), axis=0, keepdims=True)
    hits = ones_where(id_column == iota((ENT, BODIES), 1).astype(f32))
    hits_two = jnp.concatenate([hits, hits], axis=0)
    common = jnp.where(mine, 0.0, all_named * named)
    earlier = ones_where(iota((BODIES, BODIES), 0) < iota((BODIES, BODIES), 1))
    slots = jnp.where(common > 0, dot(common.astype(bf16), earlier) + 1.0, 0.0).astype(bf16)
    rank_t = dot_rows(hits, slots).astype(bf16)
    lane_start = iota((SOIL, ROWS), 0) * SHARED
    lanes = iota((SOIL, ROWS), 1)
    spread_lanes = ones_where((lanes >= lane_start) & (lanes < lane_start + SHARED))
    lane_rank = ((iota((ENT, ROWS), 1) & (SHARED - 1)) + 1).astype(f32)
    share_t[...] = ones_where(dot(rank_t, spread_lanes) == lane_rank)
    rank_two = dot_rows(slots, hits_two)
    order_row = (iota((SHARED, 128), 0) + 1).astype(f32)
    for peer in range(SOIL):
        line = jnp.broadcast_to(rank_two[peer : peer + 1], (SHARED, 128))
        share[SHARED * peer : SHARED * peer + SHARED] = ones_where(line == order_row)
    own[...] = dot_rows(hits, hits_two).astype(bf16)


def project_cone(normal, tangent_one, tangent_two, friction):
    tangent_size = jnp.sqrt(tangent_one * tangent_one + tangent_two * tangent_two)
    inside = tangent_size <= friction * normal
    polar_side = friction * tangent_size <= -normal
    middle = jnp.logical_not(jnp.logical_or(inside, polar_side))
    safe_size = jnp.where(middle, tangent_size, 1.0)
    new_normal = (friction * tangent_size + normal) / (1.0 + friction * friction)
    shrink = friction * new_normal / safe_size
    out_normal = jnp.where(inside, normal, jnp.where(polar_side, 0.0, new_normal))
    factor = jnp.where(inside, 1.0, jnp.where(polar_side, 0.0, shrink))
    return out_normal, tangent_one * factor, tangent_two * factor


def step_kernel(
    weight,
    is_first,
    is_last,
    arrived,
    pick,
    pick_t,
    tiles,
    flipped,
    current,
    advance,
    right_side,
    friction,
    *rest,
):
    copy = None
    if is_first:
        id_column, mass_in, matrix_far = rest[0:3]
        payload, new_current, new_advance, new_forces, mass_rows = rest[3:8]
        share, share_t, own, matrix, slot_labels = rest[8:13]
        spread, picked, sem = rest[13:]
        copy = pltpu.make_async_copy(matrix_far, matrix, sem)
        copy.start()
        me = lax.axis_index("soil")
        mine = id_column[:, 0:1]
        tail = arrived[:, FORCE_ROWS + 3 * NB :, :].astype(f32)
        tail = tail.reshape(8 * SOIL, 128).astype(bf16)
        tail_lane = iota((7 * SOIL, 8 * SOIL), 1)
        tail_row = iota((7 * SOIL, 8 * SOIL), 0)
        tails = dot(
            ones_where(tail_lane == (tail_row & (SOIL - 1)) * 8 + (tail_row >> 4)), tail
        )
        tire_all = side_by_side(tails, SOIL)
        names = tails[3 * SOIL : 4 * SOIL]
        all_named = jnp.concatenate(
            [tails[4 * SOIL : 5 * SOIL], tails[5 * SOIL : 6 * SOIL]], axis=1
        )
        low_lanes = lanes_low((1, 128))
        own_name = jnp.where(mine >= 0, mine + 1.0, -1.0)
        match = jnp.concatenate(
            [
                ones_where(
                    own_name
                    == jnp.where(
                        low_lanes, names[2 * t : 2 * t + 1], names[2 * t + 1 : 2 * t + 2]
                    )
                )
                for t in range(SOIL // 2)
            ],
            axis=1,
        )
        name_pick = ones_where(mine == iota((ENT, BODIES), 1).astype(f32))
        found, sums = [], []
        for c in range(3):
            start = FORCE_ROWS + NB * c
            found.append(arrived[:, start : start + NB, :].reshape(BODIES, 128))
            sums.append(arrived[:, ENT * c : ENT * c + ENT, :].reshape(SOIL * ENT, 128))
        mass_high = dot(name_pick, jnp.concatenate(found, axis=1))
        mass_rows[...] = mass_high
        wanted = dot(match, jnp.concatenate(sums, axis=1)) * mass_high
        match_shares(me, all_named, mine, share, share_t, own)
        slot_labels[...] = tails[6 * SOIL : 7 * SOIL]
        tail_pick = mass_slots(slot_hits(me, tails[6 * SOIL : 7 * SOIL]))
        mass_low = (mass_in[...] - mass_in[...].astype(bf16).astype(f32)).astype(bf16)
        tail_rows = dot(
            tail_pick,
            jnp.concatenate(
                [plane for plane in planes(mass_low) for _ in range(CAP)]
                + [jnp.zeros((CAP * NB, 128), bf16)],
                axis=0,
            ),
        )
    else:
        forces_in, mass_in, share, share_t, own, matrix = rest[0:6]
        if is_last:
            outputs, (spread, picked) = rest[6:-2], rest[-2:]
        else:
            slot_column, outputs, (spread, picked) = rest[6], rest[7:-2], rest[-2:]
        size = 8 if is_last else 16
        tail = arrived[:, SHARE_ROWS:, :].astype(f32).reshape(size * SOIL, 128).astype(bf16)
        tail_lane = iota((3 * SOIL, size * SOIL), 1)
        tail_row = iota((3 * SOIL, size * SOIL), 0)
        tire_all = side_by_side(
            dot(
                ones_where(tail_lane == (tail_row & (SOIL - 1)) * size + (tail_row >> 4)), tail
            ),
            SOIL,
        )
        received = [
            arrived[:, SHARED * c : SHARED * c + SHARED, :].reshape(ROWS, 128) for c in range(3)
        ]
        sums = dot(share_t[...], jnp.concatenate(received, axis=1))
        sums += dot(own[...], split_terms(forces_in[...], 2))
        mass_all = mass_in[...]
        if not is_last:
            lane = iota((ENT, 16 * SOIL), 1).astype(f32)
            first = slot_column[:, 0:1] + 3.0
            chosen = [ones_where(lane == first + float(CAP * c)) for c in range(3)]
            mass_all += side_by_side(dot(jnp.concatenate(chosen, axis=0), tail), ENT)
        wanted = sums * mass_all
    pieces = pull(wanted.astype(bf16), pick_t[...], flipped)

    device = iota((SOIL, WIDE), 0)
    for peer in range(SOIL):
        spread[:, WIDE * peer : WIDE * peer + WIDE] = jnp.where(
            device == peer, tire_all, 0.0
        ).astype(bf16)
    if copy is not None:
        copy.wait()
    tire = jnp.sum(dot(spread[...], matrix[...]), axis=0, keepdims=True)

    row = iota((CB, 128), 0)
    moved = []
    for piece in range(3):
        line = jnp.broadcast_to(tire[:, 128 * piece : 128 * piece + 128], (CB, 128))
        added = jnp.where(
            row == 0, both(line, False), jnp.where(row == 8, both(line, True), 0.0)
        )
        gradient = pieces[piece] + added + right_side[piece]
        moved.append(advance[piece] - step_size * gradient)
    updated = project_cone(*moved, friction[...])
    change = [updated[piece] - current[piece] for piece in range(3)]
    if is_last:
        impulses, doubles, squares = outputs
        low = lanes_low((8, 128))
        for piece in range(3):
            merged = jnp.where(low, updated[piece][0:8], updated[piece][8:16])
            for t in range(8):
                impulses[piece : piece + 1, 128 * t : 128 * t + 128] = merged[t : t + 1]
        doubles[...] = twice(*updated)
        total = change[0] * change[0] + change[1] * change[1] + change[2] * change[2]
        total = jnp.where(lanes_low((CB, 128)), total, 0.0)
        total = jnp.sum(jnp.sum(total, axis=1, keepdims=True), axis=0, keepdims=True)
        squares[...] = jnp.broadcast_to(total.reshape(1, 1, 1), squares.shape)
        return
    if not is_first:
        payload, new_current, new_advance, new_forces, mass_rows = outputs
        mass_rows[...] = mass_all
    ahead = [updated[piece] + weight * change[piece] for piece in range(3)]
    for piece in range(3):
        new_current[piece] = updated[piece]
        new_advance[piece] = ahead[piece]
    picked[...] = dot(pick[...], twice(*ahead)).astype(bf16)
    push(picked, tiles, new_forces)
    shares = dot(share[...], split_terms(new_forces[...], 2)).astype(bf16)
    for c, plane in enumerate(planes(shares)):
        payload[:, SHARED * c : SHARED * c + SHARED, :] = plane.reshape(SOIL, SHARED, 128)
    size = 16 if is_first else 8
    place = iota((size * SOIL, 128), 0) & (size - 1)
    tail_out = tail_rows if is_first else jnp.zeros((size * SOIL, 128), f32)
    for c, line in enumerate(planes(tire_row(*ahead))):
        tail_out = jnp.where(place == c, line, tail_out)
    payload[:, SHARE_ROWS:, :] = tail_out.reshape(SOIL, size, 128).astype(bf16)


def last_push_kernel(
    doubles, pick, slot_row, slot_labels, tiles_far, forces, owner_pick, gather, tiles, sems
):
    copies = [
        pltpu.make_async_copy(
            tiles_far.at[pl.ds(16 * g, 16)], tiles.at[pl.ds(16 * g, 16)], sems.at[g]
        )
        for g in range(4)
    ]
    for copy in copies:
        copy.start()
    picked = dot(pick[...], doubles[...]).astype(bf16)
    mask = entry_mask()
    for group in range(4):
        copies[group].wait()
        part = slice(16 * group, 16 * group + 16)
        spread = jnp.concatenate([picked[part]] * 8, axis=1) * mask
        forces[part] = dot(spread, tiles[part].reshape(16 * TALL, WIDE))
        if group == 0:
            line = iota((16 * SOIL, ENT), 0).astype(f32)
            chosen = [ones_where(line == slot_row[0:1] + float(CAP * c)) for c in range(3)]
            owner_pick[...] = jnp.concatenate([part for part in chosen for _ in range(3)], axis=1)
        if group == 1:
            owner_slots(slot_hits(lax.axis_index("soil"), slot_labels[...]), gather)


def outgoing_kernel(forces, owner_pick, across, payload):
    terms = [split_terms(plane, 3) for plane in planes(forces[...])]
    rows = dot(owner_pick[...], jnp.concatenate(terms, axis=0))
    squares = jnp.sum(across[:, 0, :], axis=0, keepdims=True)[:, 0:1]
    place = iota((16 * SOIL, 128), 0) & 15
    payload[...] = jnp.where(place == 3 * CAP, squares, rows).reshape(SOIL, 16, 128)


def totals_kernel(scale, arrived, gather, mass, velocity, norm):
    rows = arrived[...].reshape(16 * SOIL, 128)
    is_square = (iota((16 * SOIL, 128), 0) & 15) == 3 * CAP
    squares = jnp.sum(jnp.where(is_square, rows, 0.0), axis=0, keepdims=True)
    norm[...] = jnp.sqrt(squares[:, 0:1] * scale + hold_eps) / step_size
    totals = dot(jnp.concatenate([gather[...]] * 3, axis=1), split_terms(rows, 3))
    totals = side_by_side(totals, NB) * mass[...]
    low = lanes_low((8, 128))
    for piece in range(3):
        tile = totals[:, 128 * piece : 128 * piece + 128]
        even, odd = tile[0:8], tile[8:16]
        for half, merged in enumerate(
            (
                jnp.where(low, even, pltpu.roll(odd, BLK, 1)),
                jnp.where(low, pltpu.roll(even, BLK, 1), odd),
            )
        ):
            component = 2 * piece + half
            for t in range(8):
                velocity[component : component + 1, 128 * t : 128 * t + 128] = merged[t : t + 1]


def step_scratch():
    return [pltpu.VMEM((SOIL, SOIL * 3 * TC), bf16), pltpu.VMEM((ENT, WIDE), bf16)]


def on_device(
    warm_start,
    right_side,
    friction,
    inverse_mass,
    jacobian,
    compliance,
    entry_block,
    entry_owner,
    entry_body,
    block_count,
):
    regions = lax.axis_size("grp")
    contacts = warm_start.shape[1]
    elements = 3 * contacts * SOIL * regions
    state = shape_of((3, CB, 128), f32)

    def line(array):
        return far(array.reshape(1, -1))

    (
        payload,
        tiles,
        flipped,
        pick,
        pick_t,
        id_column,
        slot_column,
        slot_row,
        warm,
        right,
        rough,
        mass_tiles,
    ) = pl.pallas_call(
        first_kernel,
        out_shape=(
            shape_of((SOIL, SEND_FIRST, 128), bf16),
            resident((ENT, TALL, WIDE), bf16),
            resident((ENT // 2, WIDE, 2 * TALL), bf16),
            shape_of((ENT, CB), bf16),
            shape_of((CB, 3 * ENT), bf16),
            shape_of((ENT, 128), f32),
            shape_of((ENT, 128), f32),
            shape_of((8, ENT), f32),
            state,
            state,
            shape_of((CB, 128), f32),
            shape_of((NB, WIDE), f32),
        ),
        in_specs=[SCALAR] + [IN_HBM] * 8,
        out_specs=(VECTOR,) * 12,
        scratch_shapes=[
            pltpu.VMEM((1, ENT), i32),
            pltpu.VMEM((1, ENT), i32),
            pltpu.VMEM((1, ENT), i32),
            pltpu.VMEM((3, contacts), f32),
            pltpu.VMEM((3, contacts), f32),
            pltpu.VMEM((1, contacts), f32),
            pltpu.VMEM((6, contacts), f32),
            pltpu.VMEM((ENT, WIDE), f32),
            pltpu.VMEM((ENT, WIDE), f32),
            pltpu.SemaphoreType.DMA((7,)),
            pltpu.SemaphoreType.DMA((ENT // 8,)),
        ],
        compiler_params=params(8),
        name="first",
    )(
        block_count,
        line(entry_owner),
        line(entry_body),
        line(entry_block),
        far(warm_start),
        far(right_side),
        line(friction),
        far(inverse_mass),
        far(jacobian),
    )
    weights = momentum_weights(ITERS)
    current = warm
    advance = warm
    for iteration in range(ITERS):
        arrived = lax.all_to_all(payload, "soil", 0, 0, tiled=True)
        is_first, is_last = iteration == 0, iteration == ITERS - 1
        if is_last:
            outs = [
                shape_of((3, contacts), f32),
                shape_of((CB, WIDE), bf16),
                shape_of((regions, 1, 128), f32),
            ]
        else:
            outs = [
                shape_of((SOIL, SEND_SECOND if is_first else SEND_THIRD, 128), bf16),
                state,
                state,
                shape_of((ENT, WIDE), f32),
                shape_of((ENT, WIDE), f32),
            ]
        scratch = step_scratch()
        if is_first:
            outs += [
                shape_of((ROWS, 128), bf16),
                shape_of((ENT, ROWS), bf16),
                shape_of((ENT, 128), bf16),
                resident(compliance.shape, bf16),
                shape_of((SOIL, 128), f32),
            ]
            more = [id_column, mass_tiles, far(compliance)]
            more_specs = [VECTOR] * 2 + [IN_HBM]
            scratch.append(pltpu.SemaphoreType.DMA)
        else:
            more = [forces, mass_rows, *kept, keep(matrix)]
            if not is_last:
                more.append(slot_column)
            more_specs = [VECTOR] * len(more)
        results = pl.pallas_call(
            functools.partial(step_kernel, weights[iteration], is_first, is_last),
            out_shape=tuple(outs),
            in_specs=[VECTOR] * 9 + more_specs,
            out_specs=(VECTOR,) * len(outs),
            scratch_shapes=scratch,
            compiler_params=params(12),
            name=f"step{iteration}",
        )(
            arrived,
            pick,
            pick_t,
            keep(tiles),
            keep(flipped),
            current,
            advance,
            right,
            rough,
            *more,
        )
        if is_last:
            impulses, doubles, squares = results
            break
        payload, current, advance, forces, mass_rows = results[:5]
        if is_first:
            kept, matrix, slot_labels = results[5:8], results[8], results[9]

    across = lax.all_to_all(squares, "grp", 0, 0, tiled=True)
    forces, owner_pick, gather = pl.pallas_call(
        last_push_kernel,
        out_shape=(
            shape_of((ENT, WIDE), f32),
            shape_of((16 * SOIL, 9 * ENT), bf16),
            shape_of((3 * NB, 16 * SOIL), bf16),
        ),
        in_specs=[VECTOR] * 4 + [IN_HBM],
        out_specs=(VECTOR,) * 3,
        scratch_shapes=[
            pltpu.VMEM((ENT, TALL, WIDE), bf16),
            pltpu.SemaphoreType.DMA((4,)),
        ],
        compiler_params=params(14),
        cost_estimate=pl.CostEstimate(
            flops=10000000, bytes_accessed=10000000, transcendentals=0
        ),
        name="last_push",
    )(doubles, pick, slot_row, slot_labels, far(jacobian))
    outgoing = pl.pallas_call(
        outgoing_kernel,
        out_shape=shape_of((SOIL, 16, 128), f32),
        in_specs=[VECTOR] * 3,
        out_specs=VECTOR,
        compiler_params=params(6),
        name="outgoing",
    )(forces, owner_pick, across)
    arrived = lax.all_to_all(outgoing, "soil", 0, 0, tiled=True)
    velocity, norm = pl.pallas_call(
        functools.partial(totals_kernel, 1.0 / elements),
        out_shape=(shape_of((6, contacts), f32), shape_of((1, 1), f32)),
        in_specs=[VECTOR] * 3,
        out_specs=(VECTOR, VECTOR),
        compiler_params=params(4),
        name="totals",
    )(arrived, gather, mass_tiles)
    return (impulses, velocity, norm[0, 0])


def solution(mesh):
    placed = (
        P(None, ("grp", "soil")),
        P(None, ("grp", "soil")),
        P(("grp", "soil")),
        P(None, ("grp", "soil")),
        P(("grp", "soil"), None, None),
        P(None, "soil"),
        P(("grp", "soil")),
        P(("grp", "soil")),
        P(("grp", "soil")),
        P(("grp", "soil")),
    )
    return jax.shard_map(
        on_device,
        mesh=mesh,
        in_specs=placed,
        out_specs=(P(None, ("grp", "soil")), P(None, ("grp", "soil")), P()),
        check_vma=False,
    )
```
